32 devices in a mesh: sect: 4 (over z), tx: 4 (over y, x), ty: 2 (over core).
Axes of the slice: x: 2, y: 2, z: 4, core: 2. Of those that a mesh axis runs over, the one named last changes fastest.
Arguments:
- solute_amounts: float32 [19, 16, 8, 1024], P(None, None, 'sect', ('tx', 'ty')), may hold values from 0.2 to 2
- submerged_layer_tally: int32 [8, 1024], P('sect', ('tx', 'ty')), may hold values from 0 to 16
- zonal_boundary_transport: float32 [16, 8, 1024], P('sect', None, ('tx', 'ty')), may hold values from -0.25 to 0.25
- meridional_boundary_transport: float32 [16, 8, 1024], P('sect', None, ('tx', 'ty')), may hold values from -0.25 to 0.25
- diffusion_factor: float32 [16, 8, 1024], P('sect', None, ('tx', 'ty')), may hold values from 0.05 to 5
- thermal_state: float32 [16, 8, 1024], P('sect', None, ('tx', 'ty')), may hold values from -2 to 30
- saltiness_field: float32 [16, 8, 1024], P('sect', None, ('tx', 'ty')), may hold values from 32 to 38
- chemistry_matrix: float32 [19, 19], replicated, may hold values from -1.25 to 1.25
Outputs:
- advanced_solutes: float32 [19, 16, 8, 1024], P(None, None, 'sect', ('tx', 'ty'))
- heating: float32 [16, 8, 1024], P('sect', None, ('tx', 'ty'))
The draws below stay inside these ranges and needn't reach their ends.
All inputs are finite; a program needn't handle non-finite values.
Results may differ from the reference program's by a relative error of at most 0.0003.
Values sent between devices are 32-bit elements; how exact they have to be, the bound alone decides.
A program may use at most 64 MiB of HBM per device.

```python
import math
import jax
import jax.numpy as jnp
from jax import lax

NTR = 19
STRATA_TOTAL = 16
ZONAL_SIZE = 8
MERIDIONAL_SIZE = 1024


def set_ends(values, own_key, least, high):
    place = [jax.random.randint(jax.random.fold_in(own_key, axis), (), 0, length) for axis, length in enumerate(values.shape)]
    widest = values.shape.index(max(values.shape))
    beside = place[:widest] + [(place[widest] + 1) % values.shape[widest]] + place[widest + 1:]
    return values.at[tuple(place)].set(least).at[tuple(beside)].set(high)


def levels(own_key, dims, shards, low, top_value):
    def one(dim, blocks):
        draws = jax.random.uniform(jax.random.fold_in(jax.random.fold_in(own_key, 6), dim), (blocks,), jnp.float32, low / len(shards), top_value / len(shards))
        return jnp.repeat(jnp.exp(draws), dims[dim] // blocks).reshape((-1,) + (1,) * (len(dims) - dim - 1))

    level = one(*shards[0])
    for cut in shards[1:]:
        level = level * one(*cut)
    return level


def noise(stream_key, extent, width, most, kind=jnp.bfloat16):
    entries = jax.random.normal(stream_key, extent, jnp.float32) * width
    return jnp.minimum(jnp.maximum(entries, -most), most).astype(kind)


def setup_inputs(seed: int = 0) -> dict:
    keys = jax.random.split(jax.random.key(seed), 9)
    solute_amounts = jnp.clip(jnp.exp(math.log(2.0) - 2.3025851 * jax.random.uniform(keys[0], (NTR, STRATA_TOTAL, ZONAL_SIZE, MERIDIONAL_SIZE), jnp.float32) ** levels(keys[0], (NTR, STRATA_TOTAL, ZONAL_SIZE, MERIDIONAL_SIZE), ((2, 4), (3, 8)), -0.2, 0.2)), 0.2, 2.0)
    submerged_layer_tally = set_ends(jax.random.randint(keys[1], (ZONAL_SIZE, MERIDIONAL_SIZE), 0, STRATA_TOTAL + 1), jax.random.fold_in(keys[1], 1), 0, STRATA_TOTAL).astype(jnp.int32)
    zonal_boundary_transport = jnp.clip(jax.random.uniform(keys[2], (STRATA_TOTAL, ZONAL_SIZE, MERIDIONAL_SIZE), jnp.float32, -0.25, 0.25) * levels(keys[2], (STRATA_TOTAL, ZONAL_SIZE, MERIDIONAL_SIZE), ((0, 4), (2, 8)), -0.4, 0.0), -0.25, 0.25)
    meridional_boundary_transport = jnp.clip(jax.random.uniform(keys[3], (STRATA_TOTAL, ZONAL_SIZE, MERIDIONAL_SIZE), jnp.float32, -0.25, 0.25) * levels(keys[3], (STRATA_TOTAL, ZONAL_SIZE, MERIDIONAL_SIZE), ((0, 4), (2, 8)), -0.4, 0.0), -0.25, 0.25)
    diffusion_factor = jnp.clip(jnp.exp(math.log(5.0) - 4.6051702 * jax.random.uniform(keys[4], (STRATA_TOTAL, ZONAL_SIZE, MERIDIONAL_SIZE), jnp.float32) ** levels(keys[4], (STRATA_TOTAL, ZONAL_SIZE, MERIDIONAL_SIZE), ((0, 4), (2, 8)), -0.2, 0.2)), 0.05, 5.0)
    thermal_state = jnp.clip(-2.0 + 32.0 * jax.random.uniform(keys[5], (STRATA_TOTAL, ZONAL_SIZE, MERIDIONAL_SIZE), jnp.float32) ** levels(keys[5], (STRATA_TOTAL, ZONAL_SIZE, MERIDIONAL_SIZE), ((0, 4), (2, 8)), -0.2, 0.2), -2.0, 30.0)
    saltiness_field = jnp.clip(32.0 + 6.0 * jax.random.uniform(keys[6], (STRATA_TOTAL, ZONAL_SIZE, MERIDIONAL_SIZE), jnp.float32) ** levels(keys[6], (STRATA_TOTAL, ZONAL_SIZE, MERIDIONAL_SIZE), ((0, 4), (2, 8)), -0.2, 0.2), 32.0, 38.0)
    chemistry_matrix = noise(keys[7], (NTR, NTR), NTR ** -0.5, 1.25, jnp.float32)
    return dict(solute_amounts=solute_amounts, submerged_layer_tally=submerged_layer_tally, zonal_boundary_transport=zonal_boundary_transport, meridional_boundary_transport=meridional_boundary_transport, diffusion_factor=diffusion_factor, thermal_state=thermal_state, saltiness_field=saltiness_field, chemistry_matrix=chemistry_matrix)


def window(array, start, length, along):
    return lax.slice_in_dim(array, start, start + length, axis=along)


def minmod(first, second):
    return jnp.where(first * second > 0, jnp.sign(first) * jnp.minimum(jnp.abs(first), jnp.abs(second)), 0.0)


def sweep(values, courant, along, length):
    far_low = window(values, 0, length + 1, along)
    near_low = window(values, 1, length + 1, along)
    near_high = window(values, 2, length + 1, along)
    far_high = window(values, 3, length + 1, along)
    upwind_east = near_low + 0.5 * (1.0 - courant) * minmod(near_low - far_low, near_high - near_low)
    upwind_west = near_high - 0.5 * (1.0 + courant) * minmod(near_high - near_low, far_high - near_high)
    face_flux = courant * jnp.where(courant >= 0, upwind_east, upwind_west)
    return window(face_flux, 0, length, along) - window(face_flux, 1, length, along)


def advect(conc_pad, wet_pad, east_faces, north_faces):
    cells_x = conc_pad.shape[2] - 4
    cells_y = conc_pad.shape[3] - 4
    inner_y = conc_pad[:, :, :, 2:cells_y + 2]
    mask_y = wet_pad[:, :, 2:cells_y + 2]
    open_x = mask_y[:, 1:cells_x + 2] * mask_y[:, 2:cells_x + 3]
    tend_x = sweep(inner_y, east_faces * open_x, 2, cells_x)
    inner_x = conc_pad[:, :, 2:cells_x + 2, :]
    mask_x = wet_pad[:, 2:cells_x + 2, :]
    open_y = mask_x[:, :, 1:cells_y + 2] * mask_x[:, :, 2:cells_y + 3]
    tend_y = sweep(inner_x, north_faces * open_y, 3, cells_y)
    return conc_pad[:, :, 2:cells_x + 2, 2:cells_y + 2] + tend_x + tend_y


def diffuse(moved, diffusion_factor, ocean_indicator):
    lower_mask = jnp.concatenate([ocean_indicator[1:], jnp.zeros_like(ocean_indicator[:1])], 0)
    coupling = diffusion_factor * ocean_indicator * lower_mask
    upper_link = jnp.concatenate([jnp.zeros_like(coupling[:1]), coupling[:-1]], 0)
    diagonal = 1.0 + upper_link + coupling
    source_all = jnp.moveaxis(moved, 1, 0)

    def forward(carry, inputs):
        sweep_ratio, sweep_rhs = carry
        diag_now, upper_now, coupling_now, source = inputs
        divisor = diag_now + upper_now * sweep_ratio
        new_ratio = -coupling_now / divisor
        new_rhs = (source + upper_now[None] * sweep_rhs) / divisor[None]
        return (new_ratio, new_rhs), (new_ratio, new_rhs)

    start = (jnp.zeros(diagonal.shape[1:], jnp.float32), jnp.zeros(source_all.shape[1:], jnp.float32))
    unused, (ratios, rhs_all) = lax.scan(forward, start, (diagonal, upper_link, coupling, source_all))

    def backward(following, inputs):
        sweep_ratio, sweep_rhs = inputs
        solved = sweep_rhs - sweep_ratio[None] * following
        return solved, solved

    unused, solved_all = lax.scan(backward, jnp.zeros(source_all.shape[1:], jnp.float32), (ratios, rhs_all), reverse=True)
    return jnp.moveaxis(solved_all, 0, 1)


def perform_chemistry(blended_solutes, thermal_state, saltiness_field, chemistry_matrix, ocean_indicator):
    expansion_speed = jnp.exp(0.0633 * (thermal_state - 15.0)) * (1.0 + 0.25 * (saltiness_field - 35.0))
    reacted = jnp.einsum("ij,jkxy->ikxy", chemistry_matrix, blended_solutes, precision=lax.Precision.HIGHEST)
    return ocean_indicator[None] * (blended_solutes + 0.2 * expansion_speed[None] * reacted)


def reference(solute_amounts, submerged_layer_tally, zonal_boundary_transport, meridional_boundary_transport, diffusion_factor, thermal_state, saltiness_field, chemistry_matrix):
    depth_index = lax.broadcasted_iota(jnp.int32, zonal_boundary_transport.shape, 0)
    ocean_indicator = (depth_index < submerged_layer_tally[None]).astype(jnp.float32)
    grid_x = zonal_boundary_transport.shape[1]
    grid_y = zonal_boundary_transport.shape[2]
    spread = ((0, 0), (2, 2), (2, 2))
    wet_pad = jnp.pad(ocean_indicator, spread)
    east_faces = jnp.pad(zonal_boundary_transport, spread)[:, 1:grid_x + 2, 2:grid_y + 2]
    north_faces = jnp.pad(meridional_boundary_transport, spread)[:, 2:grid_x + 2, 1:grid_y + 2]

    def advect_tracer(tracer):
        conc_pad = jnp.pad(tracer * ocean_indicator, spread)[None]
        return advect(conc_pad, wet_pad, east_faces, north_faces)[0]

    moved = lax.map(advect_tracer, solute_amounts)
    blended_solutes = diffuse(moved, diffusion_factor, ocean_indicator)
    advanced_solutes = perform_chemistry(blended_solutes, thermal_state, saltiness_field, chemistry_matrix, ocean_indicator)
    absorption = ocean_indicator * (0.02 + 0.04 * jnp.maximum(advanced_solutes[0], 0.0))
    optical_depth = jnp.cumsum(absorption, 0) - absorption
    heating = 16.0 * jnp.exp(-optical_depth) * (1.0 - jnp.exp(-absorption))
    return advanced_solutes, heating
```

```python
import functools

import jax
import jax.numpy as jnp
from jax import lax
from jax.experimental import pallas as pl
from jax.experimental.pallas import tpu as pltpu
from jax.sharding import PartitionSpec as P

MESH = pl.DeviceIdType.MESH
SUB = 8
HALO = 2
F32 = jnp.float32


def round_up(value, unit):
    return -(-value // unit) * unit


def limited(first, second):
    return jnp.maximum(jnp.minimum(first, second), 0.0) + jnp.minimum(
        jnp.maximum(first, second), 0.0
    )


def face_flux(c, weight, near_low, near_high, low, mid, high):
    up = c >= 0
    base = jnp.where(up, near_low, near_high)
    return c * base + weight * limited(mid, jnp.where(up, low, high))


def limiter_weight(c):
    size = jnp.abs(c)
    return 0.5 * size * (1.0 - size)


def kernel(
    sizes,
    sol_hbm,
    tally_ref,
    east_ref,
    north_ref,
    kappa_ref,
    temp_ref,
    salt_ref,
    chem_ref,
    adv_hbm,
    heat_ref,
    own,
    lo,
    hi,
    outp,
    xs,
    mv,
    fsend,
    frecv,
    ysend,
    yleft,
    yright,
    csend,
    cleft,
    fld,
    elow,
    coef,
    clow,
    flp,
    hsend,
    hrecv,
    chem,
    f_ssem,
    f_rsem,
    z_ssem,
    z_rsem,
    y_ssem,
    y_rsem,
    c_ssem,
    c_rsem,
    h_ssem,
    h_rsem,
    own_sem,
    out_sem,
):
    T, K, R, C, n, ntx, nty = sizes
    L = K // n
    LR = L * R
    KR = K * R
    TP = round_up(T, SUB)
    groups = TP // SUB
    me = lax.axis_index("sect")
    tx = lax.axis_index("tx")
    ty = lax.axis_index("ty")
    flat = tx * nty + ty
    has_lo = me > 0
    has_hi = me < n - 1
    has_left = flat > 0
    has_right = flat < ntx * nty - 1
    left = {"tx": (flat + ntx * nty - 1) % (ntx * nty) // nty, "ty": (flat + ntx * nty - 1) % nty}
    right = {"tx": (flat + 1) % (ntx * nty) // nty, "ty": (flat + 1) % nty}

    own_copy = pltpu.make_async_copy(sol_hbm, own.at[pl.ds(0, T * KR)], own_sem)
    own_copy.start()

    barrier = pltpu.get_barrier_semaphore()
    for off in range(1, n):
        pl.semaphore_signal(
            barrier, inc=1, device_id={"sect": (me + off) % n}, device_id_type=MESH
        )

    @pl.when(has_left)
    def _():
        pl.semaphore_signal(barrier, inc=1, device_id=left, device_id_type=MESH)

    @pl.when(has_right)
    def _():
        pl.semaphore_signal(barrier, inc=1, device_id=right, device_id_type=MESH)

    growth = jnp.exp(0.0633 * (temp_ref[...] - 15.0)) * (1.0 + 0.25 * (salt_ref[...] - 35.0))
    tally = tally_ref[...].astype(F32)
    used = 4 * LR + L + R
    block_rows = fsend.shape[1]
    fsend[...] = jnp.zeros(fsend.shape, F32)
    for d in range(n):
        for l in range(L):
            at = l * R
            rows = slice(d * R, (d + 1) * R)
            fsend[d, at : at + R] = east_ref[l, rows]
            fsend[d, LR + at : LR + at + R] = north_ref[l, rows]
            fsend[d, 2 * LR + at : 2 * LR + at + R] = kappa_ref[l, rows]
            fsend[d, 3 * LR + at : 3 * LR + at + R] = growth[l, d * R : (d + 1) * R]
            if d > 0:
                fsend[d, 4 * LR + l : 4 * LR + l + 1] = east_ref[l, d * R - 1 : d * R]
        fsend[d, used - R : used] = tally

    for buf in (own, lo, hi):
        if TP > T:
            buf[T * KR :] = jnp.zeros(((TP - T) * KR, C), F32)

    pl.semaphore_wait(
        barrier, n - 1 + has_left.astype(jnp.int32) + has_right.astype(jnp.int32)
    )

    def field_copy(off):
        to = (me + off) % n
        return pltpu.make_async_remote_copy(
            src_ref=fsend.at[to],
            dst_ref=frecv.at[me],
            send_sem=f_ssem.at[off],
            recv_sem=f_rsem.at[off],
            device_id={"sect": to},
            device_id_type=MESH,
        )

    for off in range(1, n):
        field_copy(off).start()

    def tile_copy(up, g):
        rows = pl.ds(g * SUB * KR, (min((g + 1) * SUB, T) - g * SUB) * KR)
        return pltpu.make_async_remote_copy(
            src_ref=sol_hbm.at[rows],
            dst_ref=(lo if up else hi).at[rows],
            send_sem=z_ssem.at[int(up), g],
            recv_sem=z_rsem.at[int(up), g],
            device_id={"sect": (me + 1) % n if up else (me + n - 1) % n},
            device_id_type=MESH,
        )

    for g in range(groups):

        @pl.when(has_hi)
        def _():
            tile_copy(True, g).start()

        @pl.when(has_lo)
        def _():
            tile_copy(False, g).start()

    frecv[pl.ds(me, 1)] = fsend[pl.ds(me, 1)]

    lane_t = lax.broadcasted_iota(jnp.int32, (TP, C), 1)
    tal_row = [tally[r : r + 1] for r in range(R)]
    own_copy.wait()

    def pack(k, packed):
        for r in range(R):
            kr = k * R + r
            wet = lax.convert_element_type(k, F32) < tal_row[r]
            cells = jnp.where(wet, own[pl.ds(kr, TP, stride=KR), :], 0.0)
            xs[kr] = cells
            moved_edge = pltpu.roll(cells, HALO + 4 * kr, 1)
            packed = jnp.where(jnp.right_shift(lane_t, 2) == kr, moved_edge, packed)
        return packed

    packed_own = lax.fori_loop(0, K, pack, jnp.zeros((TP, C), F32), unroll=True)
    ysend[0:TP] = packed_own
    ysend[TP:] = jnp.zeros((SUB, C), F32)
    ysend[TP : TP + R] = tally

    def edge_copy(to_right):
        return pltpu.make_async_remote_copy(
            src_ref=ysend,
            dst_ref=yleft if to_right else yright,
            send_sem=y_ssem.at[int(to_right)],
            recv_sem=y_rsem.at[int(to_right)],
            device_id=right if to_right else left,
            device_id_type=MESH,
        )

    def north_copy():
        return pltpu.make_async_remote_copy(
            src_ref=csend,
            dst_ref=cleft,
            send_sem=c_ssem,
            recv_sem=c_rsem,
            device_id=right,
            device_id_type=MESH,
        )

    @pl.when(has_right)
    def _():
        edge_copy(True).start()

    @pl.when(has_left)
    def _():
        edge_copy(False).start()

    for off in range(1, n):
        field_copy(off).wait_recv()
    for s in range(n):
        for f in range(4):
            fld[f, s * LR : (s + 1) * LR] = frecv[s, f * LR : (f + 1) * LR]
        elow[s * L : (s + 1) * L] = frecv[s, 4 * LR : 4 * LR + L]

    row = lax.broadcasted_iota(jnp.int32, (KR, C), 0)
    lane = lax.broadcasted_iota(jnp.int32, (KR, C), 1)
    level = jnp.right_shift(row, 1).astype(F32)
    odd = jnp.bitwise_and(row, 1) == 1
    north = fld[1]
    edge_c = jnp.where(jnp.right_shift(lane, 2) == row, north[:, C - 1 : C], 0.0)
    csend[...] = jnp.broadcast_to(jnp.sum(edge_c, axis=0, keepdims=True), (SUB, C))

    @pl.when(has_right)
    def _():
        north_copy().start()

    below = frecv[lax.rem(me + n - 1, n), used - R : used]
    above = frecv[lax.rem(me + 1, n), used - R : used]
    below = jnp.where(has_lo, below, 0.0)
    above = jnp.where(has_hi, above, 0.0)
    tal = jnp.where(odd, tal_row[1], tal_row[0])
    tal_next = jnp.where(odd, above[0:1], tal_row[1])
    CX, WX, CY, WY, INV, UINV, RATIO, COUP, WET, WG, ABS, OPT = range(12)
    c_x = jnp.where(level < jnp.minimum(tal, tal_next), fld[0], 0.0)
    coef[CX] = c_x
    coef[WX] = limiter_weight(c_x)
    level_k = lax.broadcasted_iota(jnp.int32, (K, C), 0).astype(F32)
    c_low = jnp.where(level_k < jnp.minimum(below[R - 1 : R], tal_row[0]), elow[0:K], 0.0)
    clow[0] = c_low
    clow[1] = limiter_weight(c_low)
    wet_all = (level < tal).astype(F32)
    coef[WET] = wet_all
    coef[WG] = wet_all * (0.2 * fld[3])
    coef[COUP] = jnp.where(level + 1.0 < tal, fld[2], 0.0)

    def eliminate(k, carry):
        out = []
        for r in range(R):
            ratio, above_link = carry[r]
            at = pl.ds(k * R + r, 1)
            link = coef[COUP, at]
            inverse = 1.0 / (1.0 + above_link + link + above_link * ratio)
            ratio = -link * inverse
            coef[INV, at] = inverse
            coef[UINV, at] = above_link * inverse
            coef[RATIO, at] = ratio
            out.append((ratio, link))
        return tuple(out)

    none = jnp.zeros((1, C), F32)
    lax.fori_loop(0, K, eliminate, tuple((none, none) for _ in range(R)), unroll=True)

    @pl.when(has_left)
    def _():
        edge_copy(True).wait_recv()

    @pl.when(has_right)
    def _():
        edge_copy(False).wait_recv()

    left_cols = jnp.where(has_left, yleft[0:TP], 0.0)
    right_cols = jnp.where(has_right, yright[0:TP], 0.0)
    tal_left = jnp.where(has_left, yleft[TP : TP + R], 0.0)
    tal_right = jnp.where(has_right, yright[TP : TP + R], 0.0)
    tal_far = jnp.where(odd, tal_right[1:2], tal_right[0:1])
    tal_east = pltpu.roll(jnp.where(lane == 0, tal_far, tal), C - 1, 1)
    c_y = jnp.where(level < jnp.minimum(tal, tal_east), north, 0.0)
    coef[CY] = c_y
    coef[WY] = limiter_weight(c_y)

    part = jnp.bitwise_and(lane_t, 3)
    packed_own = ysend[0:TP]
    edges = jnp.where(part < HALO, left_cols, right_cols)
    around = jnp.where(part < HALO, left_cols, packed_own)

    @pl.when(has_left)
    def _():
        north_copy().wait_recv()

    wide = (SUB, C)
    lane_8 = lax.broadcasted_iota(jnp.int32, wide, 1)
    shut = []
    for r in range(R):
        before = pltpu.roll(jnp.broadcast_to(tal_left[r : r + 1], wide), 1, 1)
        both = jnp.minimum(before, jnp.broadcast_to(tal_row[r], wide))
        shut.append(jnp.broadcast_to(both[:, 0:1], wide))
    tal_edge = jnp.where(jnp.bitwise_and(jnp.right_shift(lane_8, 2), 1) == 1, shut[1], shut[0])
    level_8 = jnp.right_shift(lane_8, 3).astype(F32)
    c_edge = jnp.where(level_8 < tal_edge, cleft[...], 0.0)[0:1]
    nxt = pltpu.roll(around, C - 1, 1)
    nxt2 = pltpu.roll(around, C - 2, 1)
    prv = pltpu.roll(around, 1, 1)
    flp[...] = face_flux(
        c_edge, limiter_weight(c_edge), around, nxt, around - prv, nxt - around, nxt2 - nxt
    )

    def along_y(k, carry):
        for r in range(R):
            kr = k * R + r
            at = pl.ds(kr, 1)
            cells = xs[kr]
            side = pltpu.roll(edges, C - HALO - 4 * kr, 1)
            prv = pltpu.roll(jnp.where(lane_t == C - 1, side, cells), 1, 1)
            nxt = pltpu.roll(jnp.where(lane_t == 0, side, cells), C - 1, 1)
            nxt2 = pltpu.roll(jnp.where(lane_t < HALO, side, cells), C - HALO, 1)
            flux = face_flux(
                coef[CY, at], coef[WY, at], cells, nxt, cells - prv, nxt - cells, nxt2 - nxt
            )
            first = pltpu.roll(flp[...], C - 1 - 4 * kr, 1)
            lower = jnp.where(lane_t == 0, first, pltpu.roll(flux, 1, 1))
            mv[kr] = cells + (lower - flux)
        return carry

    lax.fori_loop(0, K, along_y, 0, unroll=4)

    for g in range(groups):

        @pl.when(has_lo)
        def _():
            tile_copy(True, g).wait_recv()

        @pl.when(has_hi)
        def _():
            tile_copy(False, g).wait_recv()

        tracers = pl.ds(g * SUB, SUB)

        def along_x(k, carry):
            base = g * SUB * KR + k * R
            depth = lax.convert_element_type(k, F32)
            cells = []
            for r in range(R):
                value = lo[pl.ds(base + r, SUB, stride=KR), :]
                cells.append(jnp.where(depth < below[r : r + 1], value, 0.0))
            for r in range(R):
                cells.append(xs[k * R + r, tracers])
            for r in range(R):
                value = hi[pl.ds(base + r, SUB, stride=KR), :]
                cells.append(jnp.where(depth < above[r : r + 1], value, 0.0))
            diff = [b - a for a, b in zip(cells, cells[1:])]
            flux = []
            for face in range(R + 1):
                if face == 0:
                    c, weight = clow[0, pl.ds(k, 1)], clow[1, pl.ds(k, 1)]
                else:
                    at = pl.ds(k * R + face - 1, 1)
                    c, weight = coef[CX, at], coef[WX, at]
                flux.append(face_flux(c, weight, cells[face + 1], cells[face + 2], *diff[face : face + 3]))
            out = []
            for r in range(R):
                kr = k * R + r
                at = pl.ds(kr, 1)
                moved = mv[kr, tracers] + (flux[r] - flux[r + 1])
                rhs = moved * coef[INV, at] + coef[UINV, at] * carry[r]
                mv[kr, tracers] = rhs
                out.append(rhs)
            return tuple(out)

        zero = jnp.zeros((SUB, C), F32)
        lax.fori_loop(0, K, along_x, (zero,) * R, unroll=4)

        def upward(i, carry):
            k = K - 1 - i
            out = []
            for r in range(R):
                kr = k * R + r
                solved = mv[kr, tracers] - coef[RATIO, pl.ds(kr, 1)] * carry[r]
                mv[kr, tracers] = solved
                out.append(solved)
            return tuple(out)

        lax.fori_loop(0, K, upward, (zero,) * R, unroll=True)

    chem[...] = jnp.zeros(chem.shape, F32)
    chem[0:T, 0:T] = chem_ref[...]
    rates = chem[...]

    def react(k, carry):
        mixed = [mv[k * R + r] for r in range(R)]
        reacted = jnp.dot(
            rates,
            jnp.concatenate(mixed, axis=1),
            precision=lax.Precision.HIGHEST,
            preferred_element_type=F32,
        )
        out = []
        for r in range(R):
            kr = k * R + r
            at = pl.ds(kr, 1)
            wet = coef[WET, at]
            value = wet * mixed[r] + coef[WG, at] * reacted[:, r * C : (r + 1) * C]
            outp[pl.ds(kr, TP, stride=KR), :] = value
            absorbed = wet * (0.02 + 0.04 * jnp.maximum(value[0:1], 0.0))
            coef[ABS, at] = absorbed
            coef[OPT, at] = carry[r]
            out.append(carry[r] + absorbed)
        return tuple(out)

    lax.fori_loop(0, K, react, (none,) * R, unroll=4)
    out_copy = pltpu.make_async_copy(outp.at[pl.ds(0, T * KR)], adv_hbm, out_sem)
    out_copy.start()

    heat = 16.0 * jnp.exp(-coef[OPT]) * (1.0 - jnp.exp(-coef[ABS]))
    if hsend.shape[1] > LR:
        hsend[...] = jnp.zeros(hsend.shape, F32)
    for d in range(n):
        hsend[d, 0:LR] = heat[d * LR : (d + 1) * LR]

    def heat_copy(off):
        to = (me + off) % n
        return pltpu.make_async_remote_copy(
            src_ref=hsend.at[to],
            dst_ref=hrecv.at[me],
            send_sem=h_ssem.at[off],
            recv_sem=h_rsem.at[off],
            device_id={"sect": to},
            device_id_type=MESH,
        )

    for off in range(1, n):
        heat_copy(off).start()
    hrecv[pl.ds(me, 1)] = hsend[pl.ds(me, 1)]

    for off in range(1, n):
        field_copy(off).wait_send()
    for g in range(groups):

        @pl.when(has_hi)
        def _():
            tile_copy(True, g).wait_send()

        @pl.when(has_lo)
        def _():
            tile_copy(False, g).wait_send()

    @pl.when(has_right)
    def _():
        edge_copy(True).wait_send()
        north_copy().wait_send()

    @pl.when(has_left)
    def _():
        edge_copy(False).wait_send()

    for off in range(1, n):
        heat_copy(off).wait_recv()
    for s in range(n):
        for l in range(L):
            heat_ref[l, s * R : (s + 1) * R] = hrecv[s, l * R : (l + 1) * R]
    for off in range(1, n):
        heat_copy(off).wait_send()
    out_copy.wait()


def body(sizes, solutes, tally, east, north, kappa, temp, salt, chemistry):
    T, K, R, C, n, ntx, nty = sizes
    KR, LR = K * R, K // n * R
    TP = round_up(T, SUB)
    groups = TP // SUB
    block = round_up(4 * LR + K // n + R, SUB)
    dma = pltpu.SemaphoreType.DMA
    vmem = pl.BlockSpec(memory_space=pltpu.VMEM)
    hbm = pl.BlockSpec(memory_space=pl.ANY)
    tile = pltpu.VMEM((TP * KR, C), F32)
    stack = pltpu.VMEM((KR, TP, C), F32)
    advanced, heating = pl.pallas_call(
        functools.partial(kernel, sizes),
        out_shape=(
            jax.ShapeDtypeStruct((T * KR, C), F32),
            jax.ShapeDtypeStruct(east.shape, F32),
        ),
        in_specs=[hbm] + [vmem] * 7,
        out_specs=(hbm, vmem),
        scratch_shapes=[
            tile,
            tile,
            tile,
            tile,
            stack,
            stack,
            pltpu.VMEM((n, block, C), F32),
            pltpu.VMEM((n, block, C), F32),
            pltpu.VMEM((TP + SUB, C), F32),
            pltpu.VMEM((TP + SUB, C), F32),
            pltpu.VMEM((TP + SUB, C), F32),
            pltpu.VMEM((SUB, C), F32),
            pltpu.VMEM((SUB, C), F32),
            pltpu.VMEM((4, KR, C), F32),
            pltpu.VMEM((round_up(K, SUB), C), F32),
            pltpu.VMEM((12, KR, C), F32),
            pltpu.VMEM((2, round_up(K, SUB), C), F32),
            pltpu.VMEM((TP, C), F32),
            pltpu.VMEM((n, round_up(LR, SUB), C), F32),
            pltpu.VMEM((n, round_up(LR, SUB), C), F32),
            pltpu.VMEM((TP, TP), F32),
            dma((n,)),
            dma((n,)),
            dma((2, groups)),
            dma((2, groups)),
            dma((2,)),
            dma((2,)),
            dma,
            dma,
            dma((n,)),
            dma((n,)),
            dma,
            dma,
        ],
        compiler_params=pltpu.CompilerParams(
            collective_id=0, has_side_effects=True, vmem_limit_bytes=24 * 1024 * 1024
        ),
        name="ocean_step",
    )(solutes.reshape(T * KR, C), tally, east, north, kappa, temp, salt, chemistry)
    return advanced.reshape(T, K, R, C), heating


def solution(mesh):
    n, ntx, nty = (mesh.shape[axis] for axis in ("sect", "tx", "ty"))
    columns = P("sect", None, ("tx", "ty"))
    in_specs = (
        P(None, None, "sect", ("tx", "ty")),
        P("sect", ("tx", "ty")),
        columns,
        columns,
        columns,
        columns,
        columns,
        P(),
    )
    out_specs = (P(None, None, "sect", ("tx", "ty")), columns)

    def step(solutes, *rest):
        T, K, X, Y = solutes.shape
        R, C = X // n, Y // (ntx * nty)
        assert R == HALO and K % n == 0 and 4 * K * R == C
        sizes = (T, K, R, C, n, ntx, nty)
        return jax.shard_map(
            functools.partial(body, sizes),
            mesh=mesh,
            in_specs=in_specs,
            out_specs=out_specs,
            check_vma=False,
        )(solutes, *rest)

    return step
```

```python
import functools

import jax
import jax.numpy as jnp
from jax import lax
from jax.experimental import pallas as pl
from jax.experimental.pallas import tpu as pltpu
from jax.sharding import PartitionSpec as P

MESH = pl.DeviceIdType.MESH
SUB = 8
HALO = 2
F32 = jnp.float32
VMEM_LIMIT = 60 * 1024 * 1024


def round_up(value, unit):
    return -(-value // unit) * unit


def limited(first, second):
    return jnp.maximum(jnp.minimum(first, second), 0.0) + jnp.minimum(
        jnp.maximum(first, second), 0.0
    )


def face_flux(c, weight, near_low, near_high, low, mid, high):
    up = c >= 0
    base = jnp.where(up, near_low, near_high)
    return c * base + weight * limited(mid, jnp.where(up, low, high))


def limiter_weight(c):
    size = jnp.abs(c)
    return 0.5 * size * (1.0 - size)


def kernel(
    sizes,
    sol_hbm,
    tally_hbm,
    east_hbm,
    north_hbm,
    kappa_hbm,
    temp_hbm,
    salt_hbm,
    chem_hbm,
    adv_hbm,
    heat_hbm,
    heat_ref,
    outp,
    tally_ref,
    east_ref,
    north_ref,
    kappa_ref,
    temp_ref,
    salt_ref,
    chem_ref,
    own,
    lo,
    hi,
    xs,
    mv,
    fsend,
    frecv,
    ysend,
    yleft,
    yright,
    csend,
    cleft,
    fld,
    elow,
    coef,
    clow,
    flp,
    hsend,
    hrecv,
    chem,
    f_ssem,
    f_rsem,
    z_ssem,
    z_rsem,
    y_ssem,
    y_rsem,
    c_ssem,
    c_rsem,
    h_ssem,
    h_rsem,
    own_sem,
    in_sem,
    out_sem,
):
    T, K, R, C, n, ntx, nty = sizes
    L = K // n
    LR = L * R
    KR = K * R
    TP = round_up(T, SUB)
    groups = TP // SUB
    me = lax.axis_index("sect")
    tx = lax.axis_index("tx")
    ty = lax.axis_index("ty")
    flat = tx * nty + ty
    has_lo = me > 0
    has_hi = me < n - 1
    has_left = flat > 0
    has_right = flat < ntx * nty - 1
    left = {"tx": (flat + ntx * nty - 1) % (ntx * nty) // nty, "ty": (flat + ntx * nty - 1) % nty}
    right = {"tx": (flat + 1) % (ntx * nty) // nty, "ty": (flat + 1) % nty}

    pairs = (
        (tally_hbm, tally_ref),
        (east_hbm, east_ref),
        (north_hbm, north_ref),
        (kappa_hbm, kappa_ref),
        (temp_hbm, temp_ref),
        (salt_hbm, salt_ref),
        (chem_hbm, chem_ref),
    )
    fetches = [pltpu.make_async_copy(a, b, in_sem.at[i]) for i, (a, b) in enumerate(pairs)]
    for fetch in fetches:
        fetch.start()
    own_copy = pltpu.make_async_copy(sol_hbm, own.at[pl.ds(0, T * KR)], own_sem)
    own_copy.start()

    barrier = pltpu.get_barrier_semaphore()
    for off in range(1, n):
        pl.semaphore_signal(
            barrier, inc=1, device_id={"sect": (me + off) % n}, device_id_type=MESH
        )

    @pl.when(has_left)
    def _():
        pl.semaphore_signal(barrier, inc=1, device_id=left, device_id_type=MESH)

    @pl.when(has_right)
    def _():
        pl.semaphore_signal(barrier, inc=1, device_id=right, device_id_type=MESH)

    for fetch in fetches:
        fetch.wait()

    growth = jnp.exp(0.0633 * (temp_ref[...] - 15.0)) * (1.0 + 0.25 * (salt_ref[...] - 35.0))
    tally = tally_ref[...].astype(F32)
    used = 4 * LR + L + R
    block_rows = fsend.shape[1]
    fsend[...] = jnp.zeros(fsend.shape, F32)
    for d in range(n):
        for l in range(L):
            at = l * R
            rows = slice(d * R, (d + 1) * R)
            fsend[d, at : at + R] = east_ref[l, rows]
            fsend[d, LR + at : LR + at + R] = north_ref[l, rows]
            fsend[d, 2 * LR + at : 2 * LR + at + R] = kappa_ref[l, rows]
            fsend[d, 3 * LR + at : 3 * LR + at + R] = growth[l, d * R : (d + 1) * R]
            if d > 0:
                fsend[d, 4 * LR + l : 4 * LR + l + 1] = east_ref[l, d * R - 1 : d * R]
        fsend[d, used - R : used] = tally

    for buf in (own, lo, hi):
        if TP > T:
            buf[T * KR :] = jnp.zeros(((TP - T) * KR, C), F32)

    pl.semaphore_wait(
        barrier, n - 1 + has_left.astype(jnp.int32) + has_right.astype(jnp.int32)
    )

    def field_copy(off):
        to = (me + off) % n
        return pltpu.make_async_remote_copy(
            src_ref=fsend.at[to],
            dst_ref=frecv.at[me],
            send_sem=f_ssem.at[off],
            recv_sem=f_rsem.at[off],
            device_id={"sect": to},
            device_id_type=MESH,
        )

    for off in range(1, n):
        field_copy(off).start()

    def tile_copy(up, g):
        rows = pl.ds(g * SUB * KR, (min((g + 1) * SUB, T) - g * SUB) * KR)
        return pltpu.make_async_remote_copy(
            src_ref=sol_hbm.at[rows],
            dst_ref=(lo if up else hi).at[rows],
            send_sem=z_ssem.at[int(up), g],
            recv_sem=z_rsem.at[int(up), g],
            device_id={"sect": (me + 1) % n if up else (me + n - 1) % n},
            device_id_type=MESH,
        )

    for g in range(groups):

        @pl.when(has_hi)
        def _():
            tile_copy(True, g).start()

        @pl.when(has_lo)
        def _():
            tile_copy(False, g).start()

    frecv[pl.ds(me, 1)] = fsend[pl.ds(me, 1)]

    lane_t = lax.broadcasted_iota(jnp.int32, (TP, C), 1)
    tal_row = [tally[r : r + 1] for r in range(R)]
    own_copy.wait()

    def pack(k, packed):
        for r in range(R):
            kr = k * R + r
            wet = lax.convert_element_type(k, F32) < tal_row[r]
            cells = jnp.where(wet, own[pl.ds(kr, TP, stride=KR), :], 0.0)
            xs[kr] = cells
            moved_edge = pltpu.roll(cells, HALO + 4 * kr, 1)
            packed = jnp.where(jnp.right_shift(lane_t, 2) == kr, moved_edge, packed)
        return packed

    packed_own = lax.fori_loop(0, K, pack, jnp.zeros((TP, C), F32), unroll=True)
    ysend[0:TP] = packed_own
    ysend[TP:] = jnp.zeros((SUB, C), F32)
    ysend[TP : TP + R] = tally

    def edge_copy(to_right):
        return pltpu.make_async_remote_copy(
            src_ref=ysend,
            dst_ref=yleft if to_right else yright,
            send_sem=y_ssem.at[int(to_right)],
            recv_sem=y_rsem.at[int(to_right)],
            device_id=right if to_right else left,
            device_id_type=MESH,
        )

    def north_copy():
        return pltpu.make_async_remote_copy(
            src_ref=csend,
            dst_ref=cleft,
            send_sem=c_ssem,
            recv_sem=c_rsem,
            device_id=right,
            device_id_type=MESH,
        )

    @pl.when(has_right)
    def _():
        edge_copy(True).start()

    @pl.when(has_left)
    def _():
        edge_copy(False).start()

    for off in range(1, n):
        field_copy(off).wait_recv()
    for s in range(n):
        for f in range(4):
            fld[f, s * LR : (s + 1) * LR] = frecv[s, f * LR : (f + 1) * LR]
        elow[s * L : (s + 1) * L] = frecv[s, 4 * LR : 4 * LR + L]

    row = lax.broadcasted_iota(jnp.int32, (KR, C), 0)
    lane = lax.broadcasted_iota(jnp.int32, (KR, C), 1)
    level = jnp.right_shift(row, 1).astype(F32)
    odd = jnp.bitwise_and(row, 1) == 1
    north = fld[1]
    edge_c = jnp.where(jnp.right_shift(lane, 2) == row, north[:, C - 1 : C], 0.0)
    csend[...] = jnp.broadcast_to(jnp.sum(edge_c, axis=0, keepdims=True), (SUB, C))

    @pl.when(has_right)
    def _():
        north_copy().start()

    below = frecv[lax.rem(me + n - 1, n), used - R : used]
    above = frecv[lax.rem(me + 1, n), used - R : used]
    below = jnp.where(has_lo, below, 0.0)
    above = jnp.where(has_hi, above, 0.0)
    tal = jnp.where(odd, tal_row[1], tal_row[0])
    tal_next = jnp.where(odd, above[0:1], tal_row[1])
    CX, WX, CY, WY, INV, UINV, RATIO, COUP, WET, WG, ABS, OPT = range(12)
    c_x = jnp.where(level < jnp.minimum(tal, tal_next), fld[0], 0.0)
    coef[CX] = c_x
    coef[WX] = limiter_weight(c_x)
    level_k = lax.broadcasted_iota(jnp.int32, (K, C), 0).astype(F32)
    c_low = jnp.where(level_k < jnp.minimum(below[R - 1 : R], tal_row[0]), elow[0:K], 0.0)
    clow[0] = c_low
    clow[1] = limiter_weight(c_low)
    wet_all = (level < tal).astype(F32)
    coef[WET] = wet_all
    coef[WG] = wet_all * (0.2 * fld[3])
    coef[COUP] = jnp.where(level + 1.0 < tal, fld[2], 0.0)

    def eliminate(k, carry):
        out = []
        for r in range(R):
            ratio, above_link = carry[r]
            at = pl.ds(k * R + r, 1)
            link = coef[COUP, at]
            inverse = 1.0 / (1.0 + above_link + link + above_link * ratio)
            ratio = -link * inverse
            coef[INV, at] = inverse
            coef[UINV, at] = above_link * inverse
            coef[RATIO, at] = ratio
            out.append((ratio, link))
        return tuple(out)

    none = jnp.zeros((1, C), F32)
    lax.fori_loop(0, K, eliminate, tuple((none, none) for _ in range(R)), unroll=True)

    @pl.when(has_left)
    def _():
        edge_copy(True).wait_recv()

    @pl.when(has_right)
    def _():
        edge_copy(False).wait_recv()

    left_cols = jnp.where(has_left, yleft[0:TP], 0.0)
    right_cols = jnp.where(has_right, yright[0:TP], 0.0)
    tal_left = jnp.where(has_left, yleft[TP : TP + R], 0.0)
    tal_right = jnp.where(has_right, yright[TP : TP + R], 0.0)
    tal_far = jnp.where(odd, tal_right[1:2], tal_right[0:1])
    tal_east = pltpu.roll(jnp.where(lane == 0, tal_far, tal), C - 1, 1)
    c_y = jnp.where(level < jnp.minimum(tal, tal_east), north, 0.0)
    coef[CY] = c_y
    coef[WY] = limiter_weight(c_y)

    part = jnp.bitwise_and(lane_t, 3)
    packed_own = ysend[0:TP]
    edges = jnp.where(part < HALO, left_cols, right_cols)
    around = jnp.where(part < HALO, left_cols, packed_own)

    @pl.when(has_left)
    def _():
        north_copy().wait_recv()

    wide = (SUB, C)
    lane_8 = lax.broadcasted_iota(jnp.int32, wide, 1)
    shut = []
    for r in range(R):
        before = pltpu.roll(jnp.broadcast_to(tal_left[r : r + 1], wide), 1, 1)
        both = jnp.minimum(before, jnp.broadcast_to(tal_row[r], wide))
        shut.append(jnp.broadcast_to(both[:, 0:1], wide))
    tal_edge = jnp.where(jnp.bitwise_and(jnp.right_shift(lane_8, 2), 1) == 1, shut[1], shut[0])
    level_8 = jnp.right_shift(lane_8, 3).astype(F32)
    c_edge = jnp.where(level_8 < tal_edge, cleft[...], 0.0)[0:1]
    nxt = pltpu.roll(around, C - 1, 1)
    nxt2 = pltpu.roll(around, C - 2, 1)
    prv = pltpu.roll(around, 1, 1)
    flp[...] = face_flux(
        c_edge, limiter_weight(c_edge), around, nxt, around - prv, nxt - around, nxt2 - nxt
    )

    def along_y(k, carry):
        for r in range(R):
            kr = k * R + r
            at = pl.ds(kr, 1)
            cells = xs[kr]
            side = pltpu.roll(edges, C - HALO - 4 * kr, 1)
            prv = pltpu.roll(jnp.where(lane_t == C - 1, side, cells), 1, 1)
            nxt = pltpu.roll(jnp.where(lane_t == 0, side, cells), C - 1, 1)
            nxt2 = pltpu.roll(jnp.where(lane_t < HALO, side, cells), C - HALO, 1)
            flux = face_flux(
                coef[CY, at], coef[WY, at], cells, nxt, cells - prv, nxt - cells, nxt2 - nxt
            )
            first = pltpu.roll(flp[...], C - 1 - 4 * kr, 1)
            lower = jnp.where(lane_t == 0, first, pltpu.roll(flux, 1, 1))
            mv[kr] = cells + (lower - flux)
        return carry

    lax.fori_loop(0, K, along_y, 0, unroll=4)

    for g in range(groups):

        @pl.when(has_lo)
        def _():
            tile_copy(True, g).wait_recv()

        @pl.when(has_hi)
        def _():
            tile_copy(False, g).wait_recv()

        tracers = pl.ds(g * SUB, SUB)

        def along_x(k, carry):
            base = g * SUB * KR + k * R
            depth = lax.convert_element_type(k, F32)
            cells = []
            for r in range(R):
                value = lo[pl.ds(base + r, SUB, stride=KR), :]
                cells.append(jnp.where(depth < below[r : r + 1], value, 0.0))
            for r in range(R):
                cells.append(xs[k * R + r, tracers])
            for r in range(R):
                value = hi[pl.ds(base + r, SUB, stride=KR), :]
                cells.append(jnp.where(depth < above[r : r + 1], value, 0.0))
            diff = [b - a for a, b in zip(cells, cells[1:])]
            flux = []
            for face in range(R + 1):
                if face == 0:
                    c, weight = clow[0, pl.ds(k, 1)], clow[1, pl.ds(k, 1)]
                else:
                    at = pl.ds(k * R + face - 1, 1)
                    c, weight = coef[CX, at], coef[WX, at]
                flux.append(face_flux(c, weight, cells[face + 1], cells[face + 2], *diff[face : face + 3]))
            out = []
            for r in range(R):
                kr = k * R + r
                at = pl.ds(kr, 1)
                moved = mv[kr, tracers] + (flux[r] - flux[r + 1])
                rhs = moved * coef[INV, at] + coef[UINV, at] * carry[r]
                mv[kr, tracers] = rhs
                out.append(rhs)
            return tuple(out)

        zero = jnp.zeros((SUB, C), F32)
        lax.fori_loop(0, K, along_x, (zero,) * R, unroll=4)

        def upward(i, carry):
            k = K - 1 - i
            out = []
            for r in range(R):
                kr = k * R + r
                solved = mv[kr, tracers] - coef[RATIO, pl.ds(kr, 1)] * carry[r]
                mv[kr, tracers] = solved
                out.append(solved)
            return tuple(out)

        lax.fori_loop(0, K, upward, (zero,) * R, unroll=True)

    chem[...] = jnp.zeros(chem.shape, F32)
    chem[0:T, 0:T] = chem_ref[...]
    rates = chem[...]

    def react(k, carry):
        mixed = [mv[k * R + r] for r in range(R)]
        reacted = jnp.dot(
            rates,
            jnp.concatenate(mixed, axis=1),
            precision=lax.Precision.HIGHEST,
            preferred_element_type=F32,
        )
        out = []
        for r in range(R):
            kr = k * R + r
            at = pl.ds(kr, 1)
            wet = coef[WET, at]
            value = wet * mixed[r] + coef[WG, at] * reacted[:, r * C : (r + 1) * C]
            outp[pl.ds(kr, TP, stride=KR), :] = value
            absorbed = wet * (0.02 + 0.04 * jnp.maximum(value[0:1], 0.0))
            coef[ABS, at] = absorbed
            coef[OPT, at] = carry[r]
            out.append(carry[r] + absorbed)
        return tuple(out)

    lax.fori_loop(0, K, react, (none,) * R, unroll=4)

    heat = 16.0 * jnp.exp(-coef[OPT]) * (1.0 - jnp.exp(-coef[ABS]))
    if hsend.shape[1] > LR:
        hsend[...] = jnp.zeros(hsend.shape, F32)
    for d in range(n):
        hsend[d, 0:LR] = heat[d * LR : (d + 1) * LR]

    def heat_copy(off):
        to = (me + off) % n
        return pltpu.make_async_remote_copy(
            src_ref=hsend.at[to],
            dst_ref=hrecv.at[me],
            send_sem=h_ssem.at[off],
            recv_sem=h_rsem.at[off],
            device_id={"sect": to},
            device_id_type=MESH,
        )

    for off in range(1, n):
        heat_copy(off).start()
    adv_copy = pltpu.make_async_copy(outp.at[pl.ds(0, T * KR)], adv_hbm, out_sem.at[0])
    adv_copy.start()
    hrecv[pl.ds(me, 1)] = hsend[pl.ds(me, 1)]

    for off in range(1, n):
        field_copy(off).wait_send()
    for g in range(groups):

        @pl.when(has_hi)
        def _():
            tile_copy(True, g).wait_send()

        @pl.when(has_lo)
        def _():
            tile_copy(False, g).wait_send()

    @pl.when(has_right)
    def _():
        edge_copy(True).wait_send()
        north_copy().wait_send()

    @pl.when(has_left)
    def _():
        edge_copy(False).wait_send()

    for off in range(1, n):
        heat_copy(off).wait_recv()
    for s in range(n):
        for l in range(L):
            heat_ref[l, s * R : (s + 1) * R] = hrecv[s, l * R : (l + 1) * R]
    heating_copy = pltpu.make_async_copy(heat_ref, heat_hbm, out_sem.at[1])
    heating_copy.start()
    for off in range(1, n):
        heat_copy(off).wait_send()
    adv_copy.wait()
    heating_copy.wait()


def store(adv, heat, adv_hbm, heat_hbm, sem):
    copies = (
        pltpu.make_async_copy(adv, adv_hbm, sem.at[0]),
        pltpu.make_async_copy(heat, heat_hbm, sem.at[1]),
    )
    for copy in copies:
        copy.start()
    for copy in copies:
        copy.wait()


def body(sizes, solutes, tally, east, north, kappa, temp, salt, chemistry):
    T, K, R, C, n, ntx, nty = sizes
    KR, LR = K * R, K // n * R
    TP = round_up(T, SUB)
    groups = TP // SUB
    block = round_up(4 * LR + K // n + R, SUB)
    dma = pltpu.SemaphoreType.DMA
    hbm = pl.BlockSpec(memory_space=pltpu.HBM)
    tile = pltpu.VMEM((TP * KR, C), F32)
    stack = pltpu.VMEM((KR, TP, C), F32)
    advanced, heating = pl.pallas_call(
        functools.partial(kernel, sizes),
        out_shape=(
            jax.ShapeDtypeStruct((T * KR, C), F32),
            jax.ShapeDtypeStruct(east.shape, F32),
        ),
        in_specs=[hbm] * 8,
        out_specs=(hbm, hbm),
        scratch_shapes=[
            pltpu.VMEM(east.shape, F32),
            tile,
            pltpu.VMEM(tally.shape, tally.dtype),
            *[pltpu.VMEM(east.shape, F32)] * 5,
            pltpu.VMEM(chemistry.shape, F32),
            tile,
            tile,
            tile,
            stack,
            stack,
            pltpu.VMEM((n, block, C), F32),
            pltpu.VMEM((n, block, C), F32),
            pltpu.VMEM((TP + SUB, C), F32),
            pltpu.VMEM((TP + SUB, C), F32),
            pltpu.VMEM((TP + SUB, C), F32),
            pltpu.VMEM((SUB, C), F32),
            pltpu.VMEM((SUB, C), F32),
            pltpu.VMEM((4, KR, C), F32),
            pltpu.VMEM((round_up(K, SUB), C), F32),
            pltpu.VMEM((12, KR, C), F32),
            pltpu.VMEM((2, round_up(K, SUB), C), F32),
            pltpu.VMEM((TP, C), F32),
            pltpu.VMEM((n, round_up(LR, SUB), C), F32),
            pltpu.VMEM((n, round_up(LR, SUB), C), F32),
            pltpu.VMEM((TP, TP), F32),
            dma((n,)),
            dma((n,)),
            dma((2, groups)),
            dma((2, groups)),
            dma((2,)),
            dma((2,)),
            dma,
            dma,
            dma((n,)),
            dma((n,)),
            dma,
            dma((7,)),
            dma((2,)),
        ],
        compiler_params=pltpu.CompilerParams(
            collective_id=0, has_side_effects=True, vmem_limit_bytes=VMEM_LIMIT
        ),
        name="ocean_step",
    )(solutes.reshape(T * KR, C), tally, east, north, kappa, temp, salt, chemistry)
    advanced, heating = pl.pallas_call(
        store,
        out_shape=(
            jax.ShapeDtypeStruct((T * KR, C), F32),
            jax.ShapeDtypeStruct(east.shape, F32),
        ),
        in_specs=[hbm, hbm],
        out_specs=(hbm, hbm),
        scratch_shapes=[dma((2,))],
        compiler_params=pltpu.CompilerParams(vmem_limit_bytes=VMEM_LIMIT),
        name="store_outputs",
    )(advanced, heating)
    return advanced.reshape(T, K, R, C), heating


def solution(mesh):
    n, ntx, nty = (mesh.shape[axis] for axis in ("sect", "tx", "ty"))
    columns = P("sect", None, ("tx", "ty"))
    in_specs = (
        P(None, None, "sect", ("tx", "ty")),
        P("sect", ("tx", "ty")),
        columns,
        columns,
        columns,
        columns,
        columns,
        P(),
    )
    out_specs = (P(None, None, "sect", ("tx", "ty")), columns)

    def step(solutes, *rest):
        T, K, X, Y = solutes.shape
        R, C = X // n, Y // (ntx * nty)
        assert R == HALO and K % n == 0 and 4 * K * R == C
        sizes = (T, K, R, C, n, ntx, nty)
        return jax.shard_map(
            functools.partial(body, sizes),
            mesh=mesh,
            in_specs=in_specs,
            out_specs=out_specs,
            check_vma=False,
        )(solutes, *rest)

    return step
```

```python
import functools

import jax
import jax.numpy as jnp
from jax import lax
from jax.experimental import pallas as pl
from jax.experimental.pallas import tpu as pltpu
from jax.sharding import PartitionSpec as P

MESH = pl.DeviceIdType.MESH
SUB = 8
HALO = 2
F32 = jnp.float32
VMEM_LIMIT = 60 * 1024 * 1024


def round_up(value, unit):
    return -(-value // unit) * unit


def limited(first, second):
    return jnp.maximum(jnp.minimum(first, second), 0.0) + jnp.minimum(
        jnp.maximum(first, second), 0.0
    )


def face_flux(c, weight, near_low, near_high, low, mid, high):
    up = c >= 0
    base = jnp.where(up, near_low, near_high)
    return c * base + weight * limited(mid, jnp.where(up, low, high))


def limiter_weight(c):
    size = jnp.abs(c)
    return 0.5 * size * (1.0 - size)


def kernel(
    sizes,
    sol_hbm,
    tally_hbm,
    east_hbm,
    north_hbm,
    kappa_hbm,
    temp_hbm,
    salt_hbm,
    chem_hbm,
    outp,
    heat_ref,
    tally_ref,
    east_ref,
    north_ref,
    kappa_ref,
    temp_ref,
    salt_ref,
    chem_ref,
    own,
    lo,
    hi,
    xs,
    mv,
    fsend,
    frecv,
    ysend,
    yleft,
    yright,
    csend,
    cleft,
    fld,
    elow,
    coef,
    clow,
    flp,
    hsend,
    hrecv,
    chem,
    early,
    f_ssem,
    f_rsem,
    z_ssem,
    z_rsem,
    y_ssem,
    y_rsem,
    c_ssem,
    c_rsem,
    h_ssem,
    h_rsem,
    own_sem,
    in_sem,
):
    T, K, R, C, n, ntx, nty = sizes
    L = K // n
    LR = L * R
    KR = K * R
    TP = round_up(T, SUB)
    groups = TP // SUB
    me = lax.axis_index("sect")
    tx = lax.axis_index("tx")
    ty = lax.axis_index("ty")
    flat = tx * nty + ty
    has_lo = me > 0
    has_hi = me < n - 1
    has_left = flat > 0
    has_right = flat < ntx * nty - 1
    left = {"tx": (flat + ntx * nty - 1) % (ntx * nty) // nty, "ty": (flat + ntx * nty - 1) % nty}
    right = {"tx": (flat + 1) % (ntx * nty) // nty, "ty": (flat + 1) % nty}

    pairs = (
        (tally_hbm, tally_ref),
        (east_hbm, east_ref),
        (north_hbm, north_ref),
        (kappa_hbm, kappa_ref),
        (temp_hbm, temp_ref),
        (salt_hbm, salt_ref),
        (chem_hbm, chem_ref),
    )
    fetches = [pltpu.make_async_copy(a, b, in_sem.at[i]) for i, (a, b) in enumerate(pairs)]
    for fetch in fetches:
        fetch.start()
    own_copy = pltpu.make_async_copy(sol_hbm, own.at[pl.ds(0, T * KR)], own_sem)
    own_copy.start()

    barrier = pltpu.get_barrier_semaphore()
    for off in range(1, n):
        pl.semaphore_signal(
            barrier, inc=1, device_id={"sect": (me + off) % n}, device_id_type=MESH
        )

    @pl.when(has_left)
    def _():
        pl.semaphore_signal(barrier, inc=1, device_id=left, device_id_type=MESH)

    @pl.when(has_right)
    def _():
        pl.semaphore_signal(barrier, inc=1, device_id=right, device_id_type=MESH)

    for fetch in fetches:
        fetch.wait()

    growth = jnp.exp(0.0633 * (temp_ref[...] - 15.0)) * (1.0 + 0.25 * (salt_ref[...] - 35.0))
    tally = tally_ref[...].astype(F32)
    used = 4 * LR + L + R
    block_rows = fsend.shape[1]
    fsend[...] = jnp.zeros(fsend.shape, F32)
    for d in range(n):
        for l in range(L):
            at = l * R
            rows = slice(d * R, (d + 1) * R)
            fsend[d, at : at + R] = east_ref[l, rows]
            fsend[d, LR + at : LR + at + R] = north_ref[l, rows]
            fsend[d, 2 * LR + at : 2 * LR + at + R] = kappa_ref[l, rows]
            fsend[d, 3 * LR + at : 3 * LR + at + R] = growth[l, d * R : (d + 1) * R]
            if d > 0:
                fsend[d, 4 * LR + l : 4 * LR + l + 1] = east_ref[l, d * R - 1 : d * R]
        fsend[d, used - R : used] = tally

    for buf in (own, lo, hi):
        if TP > T:
            buf[T * KR :] = jnp.zeros(((TP - T) * KR, C), F32)

    pl.semaphore_wait(
        barrier, n - 1 + has_left.astype(jnp.int32) + has_right.astype(jnp.int32)
    )

    def field_copy(off):
        to = (me + off) % n
        return pltpu.make_async_remote_copy(
            src_ref=fsend.at[to],
            dst_ref=frecv.at[me],
            send_sem=f_ssem.at[off],
            recv_sem=f_rsem.at[off],
            device_id={"sect": to},
            device_id_type=MESH,
        )

    for off in range(1, n):
        field_copy(off).start()

    def tile_copy(up, g):
        rows = pl.ds(g * SUB * KR, (min((g + 1) * SUB, T) - g * SUB) * KR)
        return pltpu.make_async_remote_copy(
            src_ref=sol_hbm.at[rows],
            dst_ref=(lo if up else hi).at[rows],
            send_sem=z_ssem.at[int(up), g],
            recv_sem=z_rsem.at[int(up), g],
            device_id={"sect": (me + 1) % n if up else (me + n - 1) % n},
            device_id_type=MESH,
        )

    for g in range(groups):

        @pl.when(has_hi)
        def _():
            tile_copy(True, g).start()

        @pl.when(has_lo)
        def _():
            tile_copy(False, g).start()

    frecv[pl.ds(me, 1)] = fsend[pl.ds(me, 1)]

    lane_t = lax.broadcasted_iota(jnp.int32, (TP, C), 1)
    tal_row = [tally[r : r + 1] for r in range(R)]
    own_copy.wait()

    def pack(k, packed):
        for r in range(R):
            kr = k * R + r
            wet = lax.convert_element_type(k, F32) < tal_row[r]
            cells = jnp.where(wet, own[pl.ds(kr, TP, stride=KR), :], 0.0)
            xs[kr] = cells
            moved_edge = pltpu.roll(cells, HALO + 4 * kr, 1)
            packed = jnp.where(jnp.right_shift(lane_t, 2) == kr, moved_edge, packed)
        return packed

    packed_own = lax.fori_loop(0, K, pack, jnp.zeros((TP, C), F32), unroll=True)
    ysend[0:TP] = packed_own
    ysend[TP:] = jnp.zeros((SUB, C), F32)
    ysend[TP : TP + R] = tally

    def edge_copy(to_right):
        return pltpu.make_async_remote_copy(
            src_ref=ysend,
            dst_ref=yleft if to_right else yright,
            send_sem=y_ssem.at[int(to_right)],
            recv_sem=y_rsem.at[int(to_right)],
            device_id=right if to_right else left,
            device_id_type=MESH,
        )

    def north_copy():
        return pltpu.make_async_remote_copy(
            src_ref=csend,
            dst_ref=cleft,
            send_sem=c_ssem,
            recv_sem=c_rsem,
            device_id=right,
            device_id_type=MESH,
        )

    @pl.when(has_right)
    def _():
        edge_copy(True).start()

    @pl.when(has_left)
    def _():
        edge_copy(False).start()

    for off in range(1, n):
        field_copy(off).wait_recv()
    for s in range(n):
        for f in range(4):
            fld[f, s * LR : (s + 1) * LR] = frecv[s, f * LR : (f + 1) * LR]
        elow[s * L : (s + 1) * L] = frecv[s, 4 * LR : 4 * LR + L]

    row = lax.broadcasted_iota(jnp.int32, (KR, C), 0)
    lane = lax.broadcasted_iota(jnp.int32, (KR, C), 1)
    level = jnp.right_shift(row, 1).astype(F32)
    odd = jnp.bitwise_and(row, 1) == 1
    north = fld[1]
    edge_c = jnp.where(jnp.right_shift(lane, 2) == row, north[:, C - 1 : C], 0.0)
    csend[...] = jnp.broadcast_to(jnp.sum(edge_c, axis=0, keepdims=True), (SUB, C))

    @pl.when(has_right)
    def _():
        north_copy().start()

    below = frecv[lax.rem(me + n - 1, n), used - R : used]
    above = frecv[lax.rem(me + 1, n), used - R : used]
    below = jnp.where(has_lo, below, 0.0)
    above = jnp.where(has_hi, above, 0.0)
    tal = jnp.where(odd, tal_row[1], tal_row[0])
    tal_next = jnp.where(odd, above[0:1], tal_row[1])
    CX, WX, CY, WY, INV, UINV, RATIO, COUP, WET, WG, ABS, OPT, ROW0 = range(13)
    c_x = jnp.where(level < jnp.minimum(tal, tal_next), fld[0], 0.0)
    coef[CX] = c_x
    coef[WX] = limiter_weight(c_x)
    level_k = lax.broadcasted_iota(jnp.int32, (K, C), 0).astype(F32)
    c_low = jnp.where(level_k < jnp.minimum(below[R - 1 : R], tal_row[0]), elow[0:K], 0.0)
    clow[0] = c_low
    clow[1] = limiter_weight(c_low)
    wet_all = (level < tal).astype(F32)
    coef[WET] = wet_all
    coef[WG] = wet_all * (0.2 * fld[3])
    coef[COUP] = jnp.where(level + 1.0 < tal, fld[2], 0.0)

    def eliminate(k, carry):
        out = []
        for r in range(R):
            ratio, above_link = carry[r]
            at = pl.ds(k * R + r, 1)
            link = coef[COUP, at]
            inverse = 1.0 / (1.0 + above_link + link + above_link * ratio)
            ratio = -link * inverse
            coef[INV, at] = inverse
            coef[UINV, at] = above_link * inverse
            coef[RATIO, at] = ratio
            out.append((ratio, link))
        return tuple(out)

    none = jnp.zeros((1, C), F32)
    lax.fori_loop(0, K, eliminate, tuple((none, none) for _ in range(R)), unroll=True)

    @pl.when(has_left)
    def _():
        edge_copy(True).wait_recv()

    @pl.when(has_right)
    def _():
        edge_copy(False).wait_recv()

    left_cols = jnp.where(has_left, yleft[0:TP], 0.0)
    right_cols = jnp.where(has_right, yright[0:TP], 0.0)
    tal_left = jnp.where(has_left, yleft[TP : TP + R], 0.0)
    tal_right = jnp.where(has_right, yright[TP : TP + R], 0.0)
    tal_far = jnp.where(odd, tal_right[1:2], tal_right[0:1])
    tal_east = pltpu.roll(jnp.where(lane == 0, tal_far, tal), C - 1, 1)
    c_y = jnp.where(level < jnp.minimum(tal, tal_east), north, 0.0)
    coef[CY] = c_y
    coef[WY] = limiter_weight(c_y)

    part = jnp.bitwise_and(lane_t, 3)
    packed_own = ysend[0:TP]
    edges = jnp.where(part < HALO, left_cols, right_cols)
    around = jnp.where(part < HALO, left_cols, packed_own)

    @pl.when(has_left)
    def _():
        north_copy().wait_recv()

    wide = (SUB, C)
    lane_8 = lax.broadcasted_iota(jnp.int32, wide, 1)
    shut = []
    for r in range(R):
        before = pltpu.roll(jnp.broadcast_to(tal_left[r : r + 1], wide), 1, 1)
        both = jnp.minimum(before, jnp.broadcast_to(tal_row[r], wide))
        shut.append(jnp.broadcast_to(both[:, 0:1], wide))
    tal_edge = jnp.where(jnp.bitwise_and(jnp.right_shift(lane_8, 2), 1) == 1, shut[1], shut[0])
    level_8 = jnp.right_shift(lane_8, 3).astype(F32)
    c_edge = jnp.where(level_8 < tal_edge, cleft[...], 0.0)[0:1]
    nxt = pltpu.roll(around, C - 1, 1)
    nxt2 = pltpu.roll(around, C - 2, 1)
    prv = pltpu.roll(around, 1, 1)
    flp[...] = face_flux(
        c_edge, limiter_weight(c_edge), around, nxt, around - prv, nxt - around, nxt2 - nxt
    )

    def along_y(k, carry):
        for r in range(R):
            kr = k * R + r
            at = pl.ds(kr, 1)
            cells = xs[kr]
            side = pltpu.roll(edges, C - HALO - 4 * kr, 1)
            prv = pltpu.roll(jnp.where(lane_t == C - 1, side, cells), 1, 1)
            nxt = pltpu.roll(jnp.where(lane_t == 0, side, cells), C - 1, 1)
            nxt2 = pltpu.roll(jnp.where(lane_t < HALO, side, cells), C - HALO, 1)
            flux = face_flux(
                coef[CY, at], coef[WY, at], cells, nxt, cells - prv, nxt - cells, nxt2 - nxt
            )
            first = pltpu.roll(flp[...], C - 1 - 4 * kr, 1)
            lower = jnp.where(lane_t == 0, first, pltpu.roll(flux, 1, 1))
            mv[kr] = cells + (lower - flux)
        return carry

    lax.fori_loop(0, K, along_y, 0, unroll=4)

    chem[...] = jnp.zeros(chem.shape, F32)
    chem[0:T, 0:T] = chem_ref[...]
    square = (TP, TP)
    across = lax.broadcasted_iota(jnp.int32, square, 1)
    down = lax.broadcasted_iota(jnp.int32, square, 0)
    first_row = jnp.where(across == down, jnp.broadcast_to(chem[0:1], square), 0.0)
    first_rates = jnp.broadcast_to(jnp.sum(first_row, axis=1, keepdims=True), (TP, C))

    def products(k, first, last):
        return jnp.dot(
            chem[:, first:last],
            jnp.concatenate([mv[k * R + r, first:last] for r in range(R)], axis=1),
            precision=lax.Precision.HIGHEST,
            preferred_element_type=F32,
        )

    for g in range(groups):

        @pl.when(has_lo)
        def _():
            tile_copy(True, g).wait_recv()

        @pl.when(has_hi)
        def _():
            tile_copy(False, g).wait_recv()

        tracers = pl.ds(g * SUB, SUB)

        def along_x(k, carry):
            base = g * SUB * KR + k * R
            depth = lax.convert_element_type(k, F32)
            cells = []
            for r in range(R):
                value = lo[pl.ds(base + r, SUB, stride=KR), :]
                cells.append(jnp.where(depth < below[r : r + 1], value, 0.0))
            for r in range(R):
                cells.append(xs[k * R + r, tracers])
            for r in range(R):
                value = hi[pl.ds(base + r, SUB, stride=KR), :]
                cells.append(jnp.where(depth < above[r : r + 1], value, 0.0))
            diff = [b - a for a, b in zip(cells, cells[1:])]
            flux = []
            for face in range(R + 1):
                if face == 0:
                    c, weight = clow[0, pl.ds(k, 1)], clow[1, pl.ds(k, 1)]
                else:
                    at = pl.ds(k * R + face - 1, 1)
                    c, weight = coef[CX, at], coef[WX, at]
                flux.append(face_flux(c, weight, cells[face + 1], cells[face + 2], *diff[face : face + 3]))
            out = []
            for r in range(R):
                kr = k * R + r
                at = pl.ds(kr, 1)
                moved = mv[kr, tracers] + (flux[r] - flux[r + 1])
                rhs = moved * coef[INV, at] + coef[UINV, at] * carry[r]
                mv[kr, tracers] = rhs
                out.append(rhs)
            return tuple(out)

        zero = jnp.zeros((SUB, C), F32)
        lax.fori_loop(0, K, along_x, (zero,) * R, unroll=4)

        def upward(i, carry):
            k = K - 1 - i
            out = []
            for r in range(R):
                kr = k * R + r
                at = pl.ds(kr, 1)
                solved = mv[kr, tracers] - coef[RATIO, at] * carry[r]
                mv[kr, tracers] = solved
                part = jnp.sum(solved * first_rates[g * SUB : (g + 1) * SUB], axis=0, keepdims=True)
                if g > 0:
                    part = coef[ROW0, at] + part
                if g < groups - 1:
                    coef[ROW0, at] = part
                else:
                    wet = coef[WET, at]
                    value = wet * mv[kr, 0:1] + coef[WG, at] * part
                    coef[ABS, at] = wet * (0.02 + 0.04 * jnp.maximum(value, 0.0))
                out.append(solved)
            return tuple(out)

        lax.fori_loop(0, K, upward, (zero,) * R, unroll=True)

        if g == 0:

            def begin(k, carry):
                early[k] = products(k, 0, SUB)
                return carry

            lax.fori_loop(0, K, begin, 0, unroll=4)

    def shade(k, carry):
        out = []
        for r in range(R):
            at = pl.ds(k * R + r, 1)
            coef[OPT, at] = carry[r]
            out.append(carry[r] + coef[ABS, at])
        return tuple(out)

    lax.fori_loop(0, K, shade, (none,) * R, unroll=True)
    heat = 16.0 * jnp.exp(-coef[OPT]) * (1.0 - jnp.exp(-coef[ABS]))
    if hsend.shape[1] > LR:
        hsend[...] = jnp.zeros(hsend.shape, F32)
    for d in range(n):
        hsend[d, 0:LR] = heat[d * LR : (d + 1) * LR]

    def heat_copy(off):
        to = (me + off) % n
        return pltpu.make_async_remote_copy(
            src_ref=hsend.at[to],
            dst_ref=hrecv.at[me],
            send_sem=h_ssem.at[off],
            recv_sem=h_rsem.at[off],
            device_id={"sect": to},
            device_id_type=MESH,
        )

    for off in range(1, n):
        heat_copy(off).start()
    hrecv[pl.ds(me, 1)] = hsend[pl.ds(me, 1)]

    def react(k, carry):
        reacted = early[k] + products(k, SUB, TP)
        for r in range(R):
            kr = k * R + r
            at = pl.ds(kr, 1)
            outp[pl.ds(kr, TP, stride=KR), :] = (
                coef[WET, at] * mv[kr] + coef[WG, at] * reacted[:, r * C : (r + 1) * C]
            )
        return carry

    lax.fori_loop(0, K, react, 0, unroll=4)

    for off in range(1, n):
        field_copy(off).wait_send()
    for g in range(groups):

        @pl.when(has_hi)
        def _():
            tile_copy(True, g).wait_send()

        @pl.when(has_lo)
        def _():
            tile_copy(False, g).wait_send()

    @pl.when(has_right)
    def _():
        edge_copy(True).wait_send()
        north_copy().wait_send()

    @pl.when(has_left)
    def _():
        edge_copy(False).wait_send()

    for off in range(1, n):
        heat_copy(off).wait_recv()
    for s in range(n):
        for l in range(L):
            heat_ref[l, s * R : (s + 1) * R] = hrecv[s, l * R : (l + 1) * R]
    for off in range(1, n):
        heat_copy(off).wait_send()


def store(adv, heat, adv_hbm, heat_hbm, sem):
    copies = (
        pltpu.make_async_copy(adv.at[pl.ds(0, adv_hbm.shape[0])], adv_hbm, sem.at[0]),
        pltpu.make_async_copy(heat, heat_hbm, sem.at[1]),
    )
    for copy in copies:
        copy.start()
    for copy in copies:
        copy.wait()


def body(sizes, solutes, tally, east, north, kappa, temp, salt, chemistry):
    T, K, R, C, n, ntx, nty = sizes
    KR, LR = K * R, K // n * R
    TP = round_up(T, SUB)
    groups = TP // SUB
    block = round_up(4 * LR + K // n + R, SUB)
    dma = pltpu.SemaphoreType.DMA
    vmem = pl.BlockSpec(memory_space=pltpu.VMEM)
    hbm = pl.BlockSpec(memory_space=pltpu.HBM)
    tile = pltpu.VMEM((TP * KR, C), F32)
    stack = pltpu.VMEM((KR, TP, C), F32)
    advanced, heating = pl.pallas_call(
        functools.partial(kernel, sizes),
        out_shape=(
            pltpu.VMEM((TP * KR, C), F32),
            pltpu.VMEM(east.shape, F32),
        ),
        in_specs=[hbm] * 8,
        out_specs=(vmem, vmem),
        scratch_shapes=[
            pltpu.VMEM(tally.shape, tally.dtype),
            *[pltpu.VMEM(east.shape, F32)] * 5,
            pltpu.VMEM(chemistry.shape, F32),
            tile,
            tile,
            tile,
            stack,
            stack,
            pltpu.VMEM((n, block, C), F32),
            pltpu.VMEM((n, block, C), F32),
            pltpu.VMEM((TP + SUB, C), F32),
            pltpu.VMEM((TP + SUB, C), F32),
            pltpu.VMEM((TP + SUB, C), F32),
            pltpu.VMEM((SUB, C), F32),
            pltpu.VMEM((SUB, C), F32),
            pltpu.VMEM((4, KR, C), F32),
            pltpu.VMEM((round_up(K, SUB), C), F32),
            pltpu.VMEM((13, KR, C), F32),
            pltpu.VMEM((2, round_up(K, SUB), C), F32),
            pltpu.VMEM((TP, C), F32),
            pltpu.VMEM((n, round_up(LR, SUB), C), F32),
            pltpu.VMEM((n, round_up(LR, SUB), C), F32),
            pltpu.VMEM((TP, TP), F32),
            pltpu.VMEM((K, TP, R * C), F32),
            dma((n,)),
            dma((n,)),
            dma((2, groups)),
            dma((2, groups)),
            dma((2,)),
            dma((2,)),
            dma,
            dma,
            dma((n,)),
            dma((n,)),
            dma,
            dma((7,)),
        ],
        compiler_params=pltpu.CompilerParams(
            collective_id=0, has_side_effects=True, vmem_limit_bytes=VMEM_LIMIT
        ),
        name="ocean_step",
    )(solutes.reshape(T * KR, C), tally, east, north, kappa, temp, salt, chemistry)
    advanced, heating = pl.pallas_call(
        store,
        out_shape=(
            jax.ShapeDtypeStruct((T * KR, C), F32),
            jax.ShapeDtypeStruct(east.shape, F32),
        ),
        in_specs=[vmem, vmem],
        out_specs=(hbm, hbm),
        scratch_shapes=[dma((2,))],
        name="store_outputs",
    )(advanced, heating)
    return advanced.reshape(T, K, R, C), heating


def solution(mesh):
    n, ntx, nty = (mesh.shape[axis] for axis in ("sect", "tx", "ty"))
    columns = P("sect", None, ("tx", "ty"))
    in_specs = (
        P(None, None, "sect", ("tx", "ty")),
        P("sect", ("tx", "ty")),
        columns,
        columns,
        columns,
        columns,
        columns,
        P(),
    )
    out_specs = (P(None, None, "sect", ("tx", "ty")), columns)

    def step(solutes, *rest):
        T, K, X, Y = solutes.shape
        R, C = X // n, Y // (ntx * nty)
        assert R == HALO and K % n == 0 and 4 * K * R == C
        sizes = (T, K, R, C, n, ntx, nty)
        return jax.shard_map(
            functools.partial(body, sizes),
            mesh=mesh,
            in_specs=in_specs,
            out_specs=out_specs,
            check_vma=False,
        )(solutes, *rest)

    return step
```

```python
import functools

import jax
import jax.numpy as jnp
from jax import lax
from jax.experimental import pallas as pl
from jax.experimental.pallas import tpu as pltpu
from jax.sharding import PartitionSpec as P

MESH = pl.DeviceIdType.MESH
SUB = 8
HALO = 2
F32 = jnp.float32
VMEM_LIMIT = 60 * 1024 * 1024


def round_up(value, unit):
    return -(-value // unit) * unit


def limited(first, second):
    return jnp.maximum(jnp.minimum(first, second), 0.0) + jnp.minimum(
        jnp.maximum(first, second), 0.0
    )


def face_flux(c, weight, near_low, near_high, low, mid, high):
    up = c >= 0
    base = jnp.where(up, near_low, near_high)
    return c * base + weight * limited(mid, jnp.where(up, low, high))


def limiter_weight(c):
    size = jnp.abs(c)
    return 0.5 * size * (1.0 - size)


def kernel(
    sizes,
    sol_hbm,
    tally_hbm,
    east_hbm,
    north_hbm,
    kappa_hbm,
    temp_hbm,
    salt_hbm,
    chem_hbm,
    outp,
    heat_ref,
    tally_ref,
    east_ref,
    north_ref,
    kappa_ref,
    temp_ref,
    salt_ref,
    chem_ref,
    own,
    lo,
    hi,
    xs,
    mv,
    fsend,
    frecv,
    ysend,
    yleft,
    yright,
    csend,
    cleft,
    fld,
    elow,
    coef,
    clow,
    flp,
    hsend,
    hrecv,
    chem,
    early,
    f_ssem,
    f_rsem,
    z_ssem,
    z_rsem,
    y_ssem,
    y_rsem,
    c_ssem,
    c_rsem,
    h_ssem,
    h_rsem,
    own_sem,
    in_sem,
):
    T, K, R, C, n, ntx, nty = sizes
    L = K // n
    LR = L * R
    KR = K * R
    TP = round_up(T, SUB)
    groups = TP // SUB
    me = lax.axis_index("sect")
    tx = lax.axis_index("tx")
    ty = lax.axis_index("ty")
    flat = tx * nty + ty
    has_lo = me > 0
    has_hi = me < n - 1
    has_left = flat > 0
    has_right = flat < ntx * nty - 1
    left = {"tx": (flat + ntx * nty - 1) % (ntx * nty) // nty, "ty": (flat + ntx * nty - 1) % nty}
    right = {"tx": (flat + 1) % (ntx * nty) // nty, "ty": (flat + 1) % nty}

    pairs = (
        (tally_hbm, tally_ref),
        (east_hbm, east_ref),
        (north_hbm, north_ref),
        (kappa_hbm, kappa_ref),
        (temp_hbm, temp_ref),
        (salt_hbm, salt_ref),
        (chem_hbm, chem_ref),
    )
    fetches = [pltpu.make_async_copy(a, b, in_sem.at[i]) for i, (a, b) in enumerate(pairs)]
    for fetch in fetches:
        fetch.start()
    own_copy = pltpu.make_async_copy(sol_hbm, own.at[pl.ds(0, T * KR)], own_sem)
    own_copy.start()

    barrier = pltpu.get_barrier_semaphore()
    for off in range(1, n):
        pl.semaphore_signal(
            barrier, inc=1, device_id={"sect": (me + off) % n}, device_id_type=MESH
        )

    @pl.when(has_left)
    def _():
        pl.semaphore_signal(barrier, inc=1, device_id=left, device_id_type=MESH)

    @pl.when(has_right)
    def _():
        pl.semaphore_signal(barrier, inc=1, device_id=right, device_id_type=MESH)

    pl.semaphore_wait(
        barrier, n - 1 + has_left.astype(jnp.int32) + has_right.astype(jnp.int32)
    )

    def tile_copy(up, g):
        rows = pl.ds(g * SUB * KR, (min((g + 1) * SUB, T) - g * SUB) * KR)
        return pltpu.make_async_remote_copy(
            src_ref=sol_hbm.at[rows],
            dst_ref=(lo if up else hi).at[rows],
            send_sem=z_ssem.at[int(up), g],
            recv_sem=z_rsem.at[int(up), g],
            device_id={"sect": (me + 1) % n if up else (me + n - 1) % n},
            device_id_type=MESH,
        )

    def send_tiles(g):
        @pl.when(has_hi)
        def _():
            tile_copy(True, g).start()

        @pl.when(has_lo)
        def _():
            tile_copy(False, g).start()

    send_tiles(0)

    for fetch in fetches:
        fetch.wait()

    growth = jnp.exp(0.0633 * (temp_ref[...] - 15.0)) * (1.0 + 0.25 * (salt_ref[...] - 35.0))
    tally = tally_ref[...].astype(F32)
    used = 4 * LR + L + R
    block_rows = fsend.shape[1]
    fsend[...] = jnp.zeros(fsend.shape, F32)
    for d in range(n):
        for l in range(L):
            at = l * R
            rows = slice(d * R, (d + 1) * R)
            fsend[d, at : at + R] = east_ref[l, rows]
            fsend[d, LR + at : LR + at + R] = north_ref[l, rows]
            fsend[d, 2 * LR + at : 2 * LR + at + R] = kappa_ref[l, rows]
            fsend[d, 3 * LR + at : 3 * LR + at + R] = growth[l, d * R : (d + 1) * R]
            if d > 0:
                fsend[d, 4 * LR + l : 4 * LR + l + 1] = east_ref[l, d * R - 1 : d * R]
        fsend[d, used - R : used] = tally

    def field_copy(off):
        to = (me + off) % n
        return pltpu.make_async_remote_copy(
            src_ref=fsend.at[to],
            dst_ref=frecv.at[me],
            send_sem=f_ssem.at[off],
            recv_sem=f_rsem.at[off],
            device_id={"sect": to},
            device_id_type=MESH,
        )

    for off in range(1, n):
        field_copy(off).start()

    for g in range(1, groups):
        send_tiles(g)

    frecv[pl.ds(me, 1)] = fsend[pl.ds(me, 1)]

    for buf in (own, lo, hi):
        if TP > T:
            buf[T * KR :] = jnp.zeros(((TP - T) * KR, C), F32)

    lane_t = lax.broadcasted_iota(jnp.int32, (TP, C), 1)
    tal_row = [tally[r : r + 1] for r in range(R)]
    own_copy.wait()

    def pack(k, packed):
        for r in range(R):
            kr = k * R + r
            wet = lax.convert_element_type(k, F32) < tal_row[r]
            cells = jnp.where(wet, own[pl.ds(kr, TP, stride=KR), :], 0.0)
            xs[kr] = cells
            moved_edge = pltpu.roll(cells, HALO + 4 * kr, 1)
            packed = jnp.where(jnp.right_shift(lane_t, 2) == kr, moved_edge, packed)
        return packed

    packed_own = lax.fori_loop(0, K, pack, jnp.zeros((TP, C), F32), unroll=True)
    ysend[0:TP] = packed_own
    ysend[TP:] = jnp.zeros((SUB, C), F32)
    ysend[TP : TP + R] = tally

    def edge_copy(to_right):
        return pltpu.make_async_remote_copy(
            src_ref=ysend,
            dst_ref=yleft if to_right else yright,
            send_sem=y_ssem.at[int(to_right)],
            recv_sem=y_rsem.at[int(to_right)],
            device_id=right if to_right else left,
            device_id_type=MESH,
        )

    def north_copy():
        return pltpu.make_async_remote_copy(
            src_ref=csend,
            dst_ref=cleft,
            send_sem=c_ssem,
            recv_sem=c_rsem,
            device_id=right,
            device_id_type=MESH,
        )

    @pl.when(has_right)
    def _():
        edge_copy(True).start()

    @pl.when(has_left)
    def _():
        edge_copy(False).start()

    for off in range(1, n):
        field_copy(off).wait_recv()
    for s in range(n):
        for f in range(4):
            fld[f, s * LR : (s + 1) * LR] = frecv[s, f * LR : (f + 1) * LR]
        elow[s * L : (s + 1) * L] = frecv[s, 4 * LR : 4 * LR + L]

    row = lax.broadcasted_iota(jnp.int32, (KR, C), 0)
    lane = lax.broadcasted_iota(jnp.int32, (KR, C), 1)
    level = jnp.right_shift(row, 1).astype(F32)
    odd = jnp.bitwise_and(row, 1) == 1
    north = fld[1]
    edge_c = jnp.where(jnp.right_shift(lane, 2) == row, north[:, C - 1 : C], 0.0)
    csend[...] = jnp.broadcast_to(jnp.sum(edge_c, axis=0, keepdims=True), (SUB, C))

    @pl.when(has_right)
    def _():
        north_copy().start()

    below = frecv[lax.rem(me + n - 1, n), used - R : used]
    above = frecv[lax.rem(me + 1, n), used - R : used]
    below = jnp.where(has_lo, below, 0.0)
    above = jnp.where(has_hi, above, 0.0)
    tal = jnp.where(odd, tal_row[1], tal_row[0])
    tal_next = jnp.where(odd, above[0:1], tal_row[1])
    CX, WX, CY, WY, INV, UINV, RATIO, COUP, WET, WG, ABS, OPT, ROW0 = range(13)
    c_x = jnp.where(level < jnp.minimum(tal, tal_next), fld[0], 0.0)
    coef[CX] = c_x
    coef[WX] = limiter_weight(c_x)
    level_k = lax.broadcasted_iota(jnp.int32, (K, C), 0).astype(F32)
    c_low = jnp.where(level_k < jnp.minimum(below[R - 1 : R], tal_row[0]), elow[0:K], 0.0)
    clow[0] = c_low
    clow[1] = limiter_weight(c_low)
    wet_all = (level < tal).astype(F32)
    coef[WET] = wet_all
    coef[WG] = wet_all * (0.2 * fld[3])
    coef[COUP] = jnp.where(level + 1.0 < tal, fld[2], 0.0)

    def eliminate(k, carry):
        out = []
        for r in range(R):
            ratio, above_link = carry[r]
            at = pl.ds(k * R + r, 1)
            link = coef[COUP, at]
            inverse = 1.0 / (1.0 + above_link + link + above_link * ratio)
            ratio = -link * inverse
            coef[INV, at] = inverse
            coef[UINV, at] = above_link * inverse
            coef[RATIO, at] = ratio
            out.append((ratio, link))
        return tuple(out)

    none = jnp.zeros((1, C), F32)
    lax.fori_loop(0, K, eliminate, tuple((none, none) for _ in range(R)), unroll=True)

    @pl.when(has_left)
    def _():
        edge_copy(True).wait_recv()

    @pl.when(has_right)
    def _():
        edge_copy(False).wait_recv()

    left_cols = jnp.where(has_left, yleft[0:TP], 0.0)
    right_cols = jnp.where(has_right, yright[0:TP], 0.0)
    tal_left = jnp.where(has_left, yleft[TP : TP + R], 0.0)
    tal_right = jnp.where(has_right, yright[TP : TP + R], 0.0)
    tal_far = jnp.where(odd, tal_right[1:2], tal_right[0:1])
    tal_east = pltpu.roll(jnp.where(lane == 0, tal_far, tal), C - 1, 1)
    c_y = jnp.where(level < jnp.minimum(tal, tal_east), north, 0.0)
    coef[CY] = c_y
    coef[WY] = limiter_weight(c_y)

    part = jnp.bitwise_and(lane_t, 3)
    packed_own = ysend[0:TP]
    edges = jnp.where(part < HALO, left_cols, right_cols)
    around = jnp.where(part < HALO, left_cols, packed_own)

    @pl.when(has_left)
    def _():
        north_copy().wait_recv()

    wide = (SUB, C)
    lane_8 = lax.broadcasted_iota(jnp.int32, wide, 1)
    shut = []
    for r in range(R):
        before = pltpu.roll(jnp.broadcast_to(tal_left[r : r + 1], wide), 1, 1)
        both = jnp.minimum(before, jnp.broadcast_to(tal_row[r], wide))
        shut.append(jnp.broadcast_to(both[:, 0:1], wide))
    tal_edge = jnp.where(jnp.bitwise_and(jnp.right_shift(lane_8, 2), 1) == 1, shut[1], shut[0])
    level_8 = jnp.right_shift(lane_8, 3).astype(F32)
    c_edge = jnp.where(level_8 < tal_edge, cleft[...], 0.0)[0:1]
    nxt = pltpu.roll(around, C - 1, 1)
    nxt2 = pltpu.roll(around, C - 2, 1)
    prv = pltpu.roll(around, 1, 1)
    flp[...] = face_flux(
        c_edge, limiter_weight(c_edge), around, nxt, around - prv, nxt - around, nxt2 - nxt
    )

    def along_y(k, carry):
        for r in range(R):
            kr = k * R + r
            at = pl.ds(kr, 1)
            cells = xs[kr]
            side = pltpu.roll(edges, C - HALO - 4 * kr, 1)
            prv = pltpu.roll(jnp.where(lane_t == C - 1, side, cells), 1, 1)
            nxt = pltpu.roll(jnp.where(lane_t == 0, side, cells), C - 1, 1)
            nxt2 = pltpu.roll(jnp.where(lane_t < HALO, side, cells), C - HALO, 1)
            flux = face_flux(
                coef[CY, at], coef[WY, at], cells, nxt, cells - prv, nxt - cells, nxt2 - nxt
            )
            first = pltpu.roll(flp[...], C - 1 - 4 * kr, 1)
            lower = jnp.where(lane_t == 0, first, pltpu.roll(flux, 1, 1))
            mv[kr] = cells + (lower - flux)
        return carry

    lax.fori_loop(0, K, along_y, 0, unroll=4)

    chem[...] = jnp.zeros(chem.shape, F32)
    chem[0:T, 0:T] = chem_ref[...]
    square = (TP, TP)
    across = lax.broadcasted_iota(jnp.int32, square, 1)
    down = lax.broadcasted_iota(jnp.int32, square, 0)
    first_row = jnp.where(across == down, jnp.broadcast_to(chem[0:1], square), 0.0)
    first_rates = jnp.broadcast_to(jnp.sum(first_row, axis=1, keepdims=True), (TP, C))

    def products(k, first, last):
        return jnp.dot(
            chem[:, first:last],
            jnp.concatenate([mv[k * R + r, first:last] for r in range(R)], axis=1),
            precision=lax.Precision.HIGHEST,
            preferred_element_type=F32,
        )

    for g in range(groups):

        @pl.when(has_lo)
        def _():
            tile_copy(True, g).wait_recv()

        @pl.when(has_hi)
        def _():
            tile_copy(False, g).wait_recv()

        tracers = pl.ds(g * SUB, SUB)

        def along_x(k, carry):
            base = g * SUB * KR + k * R
            depth = lax.convert_element_type(k, F32)
            cells = []
            for r in range(R):
                value = lo[pl.ds(base + r, SUB, stride=KR), :]
                cells.append(jnp.where(depth < below[r : r + 1], value, 0.0))
            for r in range(R):
                cells.append(xs[k * R + r, tracers])
            for r in range(R):
                value = hi[pl.ds(base + r, SUB, stride=KR), :]
                cells.append(jnp.where(depth < above[r : r + 1], value, 0.0))
            diff = [b - a for a, b in zip(cells, cells[1:])]
            flux = []
            for face in range(R + 1):
                if face == 0:
                    c, weight = clow[0, pl.ds(k, 1)], clow[1, pl.ds(k, 1)]
                else:
                    at = pl.ds(k * R + face - 1, 1)
                    c, weight = coef[CX, at], coef[WX, at]
                flux.append(face_flux(c, weight, cells[face + 1], cells[face + 2], *diff[face : face + 3]))
            out = []
            for r in range(R):
                kr = k * R + r
                at = pl.ds(kr, 1)
                moved = mv[kr, tracers] + (flux[r] - flux[r + 1])
                rhs = moved * coef[INV, at] + coef[UINV, at] * carry[r]
                mv[kr, tracers] = rhs
                out.append(rhs)
            return tuple(out)

        zero = jnp.zeros((SUB, C), F32)
        lax.fori_loop(0, K, along_x, (zero,) * R, unroll=4)

        def upward(i, carry):
            k = K - 1 - i
            out = []
            for r in range(R):
                kr = k * R + r
                at = pl.ds(kr, 1)
                solved = mv[kr, tracers] - coef[RATIO, at] * carry[r]
                mv[kr, tracers] = solved
                part = jnp.sum(solved * first_rates[g * SUB : (g + 1) * SUB], axis=0, keepdims=True)
                if g > 0:
                    part = coef[ROW0, at] + part
                if g < groups - 1:
                    coef[ROW0, at] = part
                else:
                    wet = coef[WET, at]
                    value = wet * mv[kr, 0:1] + coef[WG, at] * part
                    coef[ABS, at] = wet * (0.02 + 0.04 * jnp.maximum(value, 0.0))
                out.append(solved)
            return tuple(out)

        lax.fori_loop(0, K, upward, (zero,) * R, unroll=True)

        if g == 0:

            def begin(k, carry):
                early[k] = products(k, 0, SUB)
                return carry

            lax.fori_loop(0, K, begin, 0, unroll=4)

    def shade(k, carry):
        out = []
        for r in range(R):
            at = pl.ds(k * R + r, 1)
            coef[OPT, at] = carry[r]
            out.append(carry[r] + coef[ABS, at])
        return tuple(out)

    lax.fori_loop(0, K, shade, (none,) * R, unroll=True)
    heat = 16.0 * jnp.exp(-coef[OPT]) * (1.0 - jnp.exp(-coef[ABS]))
    if hsend.shape[1] > LR:
        hsend[...] = jnp.zeros(hsend.shape, F32)
    for d in range(n):
        hsend[d, 0:LR] = heat[d * LR : (d + 1) * LR]

    def heat_copy(off):
        to = (me + off) % n
        return pltpu.make_async_remote_copy(
            src_ref=hsend.at[to],
            dst_ref=hrecv.at[me],
            send_sem=h_ssem.at[off],
            recv_sem=h_rsem.at[off],
            device_id={"sect": to},
            device_id_type=MESH,
        )

    for off in range(1, n):
        heat_copy(off).start()
    hrecv[pl.ds(me, 1)] = hsend[pl.ds(me, 1)]

    def react(k, carry):
        reacted = early[k] + products(k, SUB, TP)
        for r in range(R):
            kr = k * R + r
            at = pl.ds(kr, 1)
            outp[pl.ds(kr, TP, stride=KR), :] = (
                coef[WET, at] * mv[kr] + coef[WG, at] * reacted[:, r * C : (r + 1) * C]
            )
        return carry

    lax.fori_loop(0, K, react, 0, unroll=4)

    for off in range(1, n):
        field_copy(off).wait_send()
    for g in range(groups):

        @pl.when(has_hi)
        def _():
            tile_copy(True, g).wait_send()

        @pl.when(has_lo)
        def _():
            tile_copy(False, g).wait_send()

    @pl.when(has_right)
    def _():
        edge_copy(True).wait_send()
        north_copy().wait_send()

    @pl.when(has_left)
    def _():
        edge_copy(False).wait_send()

    for off in range(1, n):
        heat_copy(off).wait_recv()
    for s in range(n):
        for l in range(L):
            heat_ref[l, s * R : (s + 1) * R] = hrecv[s, l * R : (l + 1) * R]
    for off in range(1, n):
        heat_copy(off).wait_send()


def store(adv, heat, adv_hbm, heat_hbm, sem):
    copies = (
        pltpu.make_async_copy(adv.at[pl.ds(0, adv_hbm.shape[0])], adv_hbm, sem.at[0]),
        pltpu.make_async_copy(heat, heat_hbm, sem.at[1]),
    )
    for copy in copies:
        copy.start()
    for copy in copies:
        copy.wait()


def body(sizes, solutes, tally, east, north, kappa, temp, salt, chemistry):
    T, K, R, C, n, ntx, nty = sizes
    KR, LR = K * R, K // n * R
    TP = round_up(T, SUB)
    groups = TP // SUB
    block = round_up(4 * LR + K // n + R, SUB)
    dma = pltpu.SemaphoreType.DMA
    vmem = pl.BlockSpec(memory_space=pltpu.VMEM)
    hbm = pl.BlockSpec(memory_space=pltpu.HBM)
    tile = pltpu.VMEM((TP * KR, C), F32)
    stack = pltpu.VMEM((KR, TP, C), F32)
    advanced, heating = pl.pallas_call(
        functools.partial(kernel, sizes),
        out_shape=(
            pltpu.VMEM((TP * KR, C), F32),
            pltpu.VMEM(east.shape, F32),
        ),
        in_specs=[hbm] * 8,
        out_specs=(vmem, vmem),
        scratch_shapes=[
            pltpu.VMEM(tally.shape, tally.dtype),
            *[pltpu.VMEM(east.shape, F32)] * 5,
            pltpu.VMEM(chemistry.shape, F32),
            tile,
            tile,
            tile,
            stack,
            stack,
            pltpu.VMEM((n, block, C), F32),
            pltpu.VMEM((n, block, C), F32),
            pltpu.VMEM((TP + SUB, C), F32),
            pltpu.VMEM((TP + SUB, C), F32),
            pltpu.VMEM((TP + SUB, C), F32),
            pltpu.VMEM((SUB, C), F32),
            pltpu.VMEM((SUB, C), F32),
            pltpu.VMEM((4, KR, C), F32),
            pltpu.VMEM((round_up(K, SUB), C), F32),
            pltpu.VMEM((13, KR, C), F32),
            pltpu.VMEM((2, round_up(K, SUB), C), F32),
            pltpu.VMEM((TP, C), F32),
            pltpu.VMEM((n, round_up(LR, SUB), C), F32),
            pltpu.VMEM((n, round_up(LR, SUB), C), F32),
            pltpu.VMEM((TP, TP), F32),
            pltpu.VMEM((K, TP, R * C), F32),
            dma((n,)),
            dma((n,)),
            dma((2, groups)),
            dma((2, groups)),
            dma((2,)),
            dma((2,)),
            dma,
            dma,
            dma((n,)),
            dma((n,)),
            dma,
            dma((7,)),
        ],
        compiler_params=pltpu.CompilerParams(
            collective_id=0, has_side_effects=True, vmem_limit_bytes=VMEM_LIMIT
        ),
        name="ocean_step",
    )(solutes.reshape(T * KR, C), tally, east, north, kappa, temp, salt, chemistry)
    advanced, heating = pl.pallas_call(
        store,
        out_shape=(
            jax.ShapeDtypeStruct((T * KR, C), F32),
            jax.ShapeDtypeStruct(east.shape, F32),
        ),
        in_specs=[vmem, vmem],
        out_specs=(hbm, hbm),
        scratch_shapes=[dma((2,))],
        compiler_params=pltpu.CompilerParams(vmem_limit_bytes=1024 * 1024),
        name="store_outputs",
    )(advanced, heating)
    return advanced.reshape(T, K, R, C), heating


def solution(mesh):
    n, ntx, nty = (mesh.shape[axis] for axis in ("sect", "tx", "ty"))
    columns = P("sect", None, ("tx", "ty"))
    in_specs = (
        P(None, None, "sect", ("tx", "ty")),
        P("sect", ("tx", "ty")),
        columns,
        columns,
        columns,
        columns,
        columns,
        P(),
    )
    out_specs = (P(None, None, "sect", ("tx", "ty")), columns)

    def step(solutes, *rest):
        T, K, X, Y = solutes.shape
        R, C = X // n, Y // (ntx * nty)
        assert R == HALO and K % n == 0 and 4 * K * R == C
        sizes = (T, K, R, C, n, ntx, nty)
        return jax.shard_map(
            functools.partial(body, sizes),
            mesh=mesh,
            in_specs=in_specs,
            out_specs=out_specs,
            check_vma=False,
        )(solutes, *rest)

    return step
```

```python
import functools

import jax
import jax.numpy as jnp
from jax import lax
from jax.experimental import pallas as pl
from jax.experimental.pallas import tpu as pltpu
from jax.sharding import PartitionSpec as P

MESH = pl.DeviceIdType.MESH
SUB = 8
HALO = 2
F32 = jnp.float32
VMEM_LIMIT = 60 * 1024 * 1024


def round_up(value, unit):
    return -(-value // unit) * unit


def limited(first, second):
    return jnp.maximum(jnp.minimum(first, second), 0.0) + jnp.minimum(
        jnp.maximum(first, second), 0.0
    )


def face_flux(c, weight, near_low, near_high, low, mid, high):
    up = c >= 0
    base = jnp.where(up, near_low, near_high)
    return c * base + weight * limited(mid, jnp.where(up, low, high))


def limiter_weight(c):
    size = jnp.abs(c)
    return 0.5 * size * (1.0 - size)


def kernel(
    sizes,
    sol_hbm,
    tally_hbm,
    east_hbm,
    north_hbm,
    kappa_hbm,
    temp_hbm,
    salt_hbm,
    chem_hbm,
    outp,
    heat_ref,
    tally_ref,
    east_ref,
    north_ref,
    kappa_ref,
    temp_ref,
    salt_ref,
    chem_ref,
    own,
    lo,
    hi,
    xs,
    mv,
    fsend,
    frecv,
    ysend,
    yleft,
    yright,
    csend,
    cleft,
    fld,
    elow,
    coef,
    clow,
    flp,
    hsend,
    hrecv,
    chem,
    early,
    f_ssem,
    f_rsem,
    z_ssem,
    z_rsem,
    y_ssem,
    y_rsem,
    c_ssem,
    c_rsem,
    h_ssem,
    h_rsem,
    own_sem,
    in_sem,
):
    T, K, R, C, n, ntx, nty = sizes
    L = K // n
    LR = L * R
    KR = K * R
    TP = round_up(T, SUB)
    groups = TP // SUB
    me = lax.axis_index("sect")
    tx = lax.axis_index("tx")
    ty = lax.axis_index("ty")
    flat = tx * nty + ty
    has_lo = me > 0
    has_hi = me < n - 1
    has_left = flat > 0
    has_right = flat < ntx * nty - 1
    left = {"tx": (flat + ntx * nty - 1) % (ntx * nty) // nty, "ty": (flat + ntx * nty - 1) % nty}
    right = {"tx": (flat + 1) % (ntx * nty) // nty, "ty": (flat + 1) % nty}

    pairs = (
        (tally_hbm, tally_ref),
        (east_hbm, east_ref),
        (north_hbm, north_ref),
        (kappa_hbm, kappa_ref),
        (temp_hbm, temp_ref),
        (salt_hbm, salt_ref),
        (chem_hbm, chem_ref),
    )
    fetches = [pltpu.make_async_copy(a, b, in_sem.at[i]) for i, (a, b) in enumerate(pairs)]
    for fetch in fetches:
        fetch.start()
    own_copy = pltpu.make_async_copy(sol_hbm, own.at[pl.ds(0, T * KR)], own_sem)
    own_copy.start()

    barrier = pltpu.get_barrier_semaphore()
    for off in range(1, n):
        pl.semaphore_signal(
            barrier, inc=1, device_id={"sect": (me + off) % n}, device_id_type=MESH
        )

    @pl.when(has_left)
    def _():
        pl.semaphore_signal(barrier, inc=1, device_id=left, device_id_type=MESH)

    @pl.when(has_right)
    def _():
        pl.semaphore_signal(barrier, inc=1, device_id=right, device_id_type=MESH)

    pl.semaphore_wait(
        barrier, n - 1 + has_left.astype(jnp.int32) + has_right.astype(jnp.int32)
    )

    def tile_copy(up, g):
        rows = pl.ds(g * SUB * KR, (min((g + 1) * SUB, T) - g * SUB) * KR)
        return pltpu.make_async_remote_copy(
            src_ref=sol_hbm.at[rows],
            dst_ref=(lo if up else hi).at[rows],
            send_sem=z_ssem.at[int(up), g],
            recv_sem=z_rsem.at[int(up), g],
            device_id={"sect": (me + 1) % n if up else (me + n - 1) % n},
            device_id_type=MESH,
        )

    def send_tiles(g):
        @pl.when(has_hi)
        def _():
            tile_copy(True, g).start()

        @pl.when(has_lo)
        def _():
            tile_copy(False, g).start()

    for fetch in fetches:
        fetch.wait()

    growth = jnp.exp(0.0633 * (temp_ref[...] - 15.0)) * (1.0 + 0.25 * (salt_ref[...] - 35.0))
    tally = tally_ref[...].astype(F32)
    used = 4 * LR + L + R
    block_rows = fsend.shape[1]
    fsend[...] = jnp.zeros(fsend.shape, F32)
    for d in range(n):
        for l in range(L):
            at = l * R
            rows = slice(d * R, (d + 1) * R)
            fsend[d, at : at + R] = east_ref[l, rows]
            fsend[d, LR + at : LR + at + R] = north_ref[l, rows]
            fsend[d, 2 * LR + at : 2 * LR + at + R] = kappa_ref[l, rows]
            fsend[d, 3 * LR + at : 3 * LR + at + R] = growth[l, d * R : (d + 1) * R]
            if d > 0:
                fsend[d, 4 * LR + l : 4 * LR + l + 1] = east_ref[l, d * R - 1 : d * R]
        fsend[d, used - R : used] = tally

    def field_copy(off):
        to = (me + off) % n
        return pltpu.make_async_remote_copy(
            src_ref=fsend.at[to],
            dst_ref=frecv.at[me],
            send_sem=f_ssem.at[off],
            recv_sem=f_rsem.at[off],
            device_id={"sect": to},
            device_id_type=MESH,
        )

    for off in range(1, n):
        field_copy(off).start()

    for g in range(groups):
        send_tiles(g)

    frecv[pl.ds(me, 1)] = fsend[pl.ds(me, 1)]

    for buf in (own, lo, hi):
        if TP > T:
            buf[T * KR :] = jnp.zeros(((TP - T) * KR, C), F32)

    lane_t = lax.broadcasted_iota(jnp.int32, (TP, C), 1)
    tal_row = [tally[r : r + 1] for r in range(R)]
    own_copy.wait()

    def pack(k, packed):
        for r in range(R):
            kr = k * R + r
            wet = lax.convert_element_type(k, F32) < tal_row[r]
            cells = jnp.where(wet, own[pl.ds(kr, TP, stride=KR), :], 0.0)
            xs[kr] = cells
            moved_edge = pltpu.roll(cells, HALO + 4 * kr, 1)
            packed = jnp.where(jnp.right_shift(lane_t, 2) == kr, moved_edge, packed)
        return packed

    packed_own = lax.fori_loop(0, K, pack, jnp.zeros((TP, C), F32), unroll=True)
    ysend[0:TP] = packed_own
    ysend[TP:] = jnp.zeros((SUB, C), F32)
    ysend[TP : TP + R] = tally

    def edge_copy(to_right):
        return pltpu.make_async_remote_copy(
            src_ref=ysend,
            dst_ref=yleft if to_right else yright,
            send_sem=y_ssem.at[int(to_right)],
            recv_sem=y_rsem.at[int(to_right)],
            device_id=right if to_right else left,
            device_id_type=MESH,
        )

    def north_copy():
        return pltpu.make_async_remote_copy(
            src_ref=csend,
            dst_ref=cleft,
            send_sem=c_ssem,
            recv_sem=c_rsem,
            device_id=right,
            device_id_type=MESH,
        )

    @pl.when(has_right)
    def _():
        edge_copy(True).start()

    @pl.when(has_left)
    def _():
        edge_copy(False).start()

    for off in range(1, n):
        field_copy(off).wait_recv()
    for s in range(n):
        for f in range(4):
            fld[f, s * LR : (s + 1) * LR] = frecv[s, f * LR : (f + 1) * LR]
        elow[s * L : (s + 1) * L] = frecv[s, 4 * LR : 4 * LR + L]

    row = lax.broadcasted_iota(jnp.int32, (KR, C), 0)
    lane = lax.broadcasted_iota(jnp.int32, (KR, C), 1)
    level = jnp.right_shift(row, 1).astype(F32)
    odd = jnp.bitwise_and(row, 1) == 1
    north = fld[1]
    edge_c = jnp.where(jnp.right_shift(lane, 2) == row, north[:, C - 1 : C], 0.0)
    csend[...] = jnp.broadcast_to(jnp.sum(edge_c, axis=0, keepdims=True), (SUB, C))

    @pl.when(has_right)
    def _():
        north_copy().start()

    below = frecv[lax.rem(me + n - 1, n), used - R : used]
    above = frecv[lax.rem(me + 1, n), used - R : used]
    below = jnp.where(has_lo, below, 0.0)
    above = jnp.where(has_hi, above, 0.0)
    tal = jnp.where(odd, tal_row[1], tal_row[0])
    tal_next = jnp.where(odd, above[0:1], tal_row[1])
    CX, WX, CY, WY, INV, UINV, RATIO, COUP, WET, WG, ABS, OPT, ROW0 = range(13)
    c_x = jnp.where(level < jnp.minimum(tal, tal_next), fld[0], 0.0)
    coef[CX] = c_x
    coef[WX] = limiter_weight(c_x)
    level_k = lax.broadcasted_iota(jnp.int32, (K, C), 0).astype(F32)
    c_low = jnp.where(level_k < jnp.minimum(below[R - 1 : R], tal_row[0]), elow[0:K], 0.0)
    clow[0] = c_low
    clow[1] = limiter_weight(c_low)
    wet_all = (level < tal).astype(F32)
    coef[WET] = wet_all
    coef[WG] = wet_all * (0.2 * fld[3])
    coef[COUP] = jnp.where(level + 1.0 < tal, fld[2], 0.0)

    def eliminate(k, carry):
        out = []
        for r in range(R):
            ratio, above_link = carry[r]
            at = pl.ds(k * R + r, 1)
            link = coef[COUP, at]
            inverse = 1.0 / (1.0 + above_link + link + above_link * ratio)
            ratio = -link * inverse
            coef[INV, at] = inverse
            coef[UINV, at] = above_link * inverse
            coef[RATIO, at] = ratio
            out.append((ratio, link))
        return tuple(out)

    none = jnp.zeros((1, C), F32)
    lax.fori_loop(0, K, eliminate, tuple((none, none) for _ in range(R)), unroll=True)

    @pl.when(has_left)
    def _():
        edge_copy(True).wait_recv()

    @pl.when(has_right)
    def _():
        edge_copy(False).wait_recv()

    left_cols = jnp.where(has_left, yleft[0:TP], 0.0)
    right_cols = jnp.where(has_right, yright[0:TP], 0.0)
    tal_left = jnp.where(has_left, yleft[TP : TP + R], 0.0)
    tal_right = jnp.where(has_right, yright[TP : TP + R], 0.0)
    tal_far = jnp.where(odd, tal_right[1:2], tal_right[0:1])
    tal_east = pltpu.roll(jnp.where(lane == 0, tal_far, tal), C - 1, 1)
    c_y = jnp.where(level < jnp.minimum(tal, tal_east), north, 0.0)
    coef[CY] = c_y
    coef[WY] = limiter_weight(c_y)

    part = jnp.bitwise_and(lane_t, 3)
    packed_own = ysend[0:TP]
    edges = jnp.where(part < HALO, left_cols, right_cols)
    around = jnp.where(part < HALO, left_cols, packed_own)

    @pl.when(has_left)
    def _():
        north_copy().wait_recv()

    wide = (SUB, C)
    lane_8 = lax.broadcasted_iota(jnp.int32, wide, 1)
    shut = []
    for r in range(R):
        before = pltpu.roll(jnp.broadcast_to(tal_left[r : r + 1], wide), 1, 1)
        both = jnp.minimum(before, jnp.broadcast_to(tal_row[r], wide))
        shut.append(jnp.broadcast_to(both[:, 0:1], wide))
    tal_edge = jnp.where(jnp.bitwise_and(jnp.right_shift(lane_8, 2), 1) == 1, shut[1], shut[0])
    level_8 = jnp.right_shift(lane_8, 3).astype(F32)
    c_edge = jnp.where(level_8 < tal_edge, cleft[...], 0.0)[0:1]
    nxt = pltpu.roll(around, C - 1, 1)
    nxt2 = pltpu.roll(around, C - 2, 1)
    prv = pltpu.roll(around, 1, 1)
    flp[...] = face_flux(
        c_edge, limiter_weight(c_edge), around, nxt, around - prv, nxt - around, nxt2 - nxt
    )

    def along_y(k, carry):
        for r in range(R):
            kr = k * R + r
            at = pl.ds(kr, 1)
            cells = xs[kr]
            side = pltpu.roll(edges, C - HALO - 4 * kr, 1)
            prv = pltpu.roll(jnp.where(lane_t == C - 1, side, cells), 1, 1)
            nxt = pltpu.roll(jnp.where(lane_t == 0, side, cells), C - 1, 1)
            nxt2 = pltpu.roll(jnp.where(lane_t < HALO, side, cells), C - HALO, 1)
            flux = face_flux(
                coef[CY, at], coef[WY, at], cells, nxt, cells - prv, nxt - cells, nxt2 - nxt
            )
            first = pltpu.roll(flp[...], C - 1 - 4 * kr, 1)
            lower = jnp.where(lane_t == 0, first, pltpu.roll(flux, 1, 1))
            mv[kr] = cells + (lower - flux)
        return carry

    lax.fori_loop(0, K, along_y, 0, unroll=4)

    chem[...] = jnp.zeros(chem.shape, F32)
    chem[0:T, 0:T] = chem_ref[...]
    square = (TP, TP)
    across = lax.broadcasted_iota(jnp.int32, square, 1)
    down = lax.broadcasted_iota(jnp.int32, square, 0)
    first_row = jnp.where(across == down, jnp.broadcast_to(chem[0:1, 0:TP], square), 0.0)
    first_rates = jnp.broadcast_to(jnp.sum(first_row, axis=1, keepdims=True), (TP, C))

    rest = TP - SUB
    rates = chem[...]
    rates_high = rates.astype(jnp.bfloat16).astype(F32)
    rates_low = rates - rates_high
    halves = jnp.where(
        lane_t < rest,
        pltpu.roll(rates_high, C - SUB, 1),
        jnp.where(
            lane_t < 2 * rest,
            pltpu.roll(rates_high, (rest + C - SUB) % C, 1),
            pltpu.roll(rates_low, (2 * rest + C - SUB) % C, 1),
        ),
    )[:, 0 : 3 * rest].astype(jnp.bfloat16)

    def late_products(k):
        mixed = jnp.concatenate([mv[k * R + r, SUB:TP] for r in range(R)], axis=1)
        high = mixed.astype(jnp.bfloat16)
        low = (mixed - high.astype(F32)).astype(jnp.bfloat16)
        return jnp.dot(
            halves,
            jnp.concatenate([high, low, high], axis=0),
            preferred_element_type=F32,
        )

    def products(k, first, last):
        return jnp.dot(
            chem[:, first:last],
            jnp.concatenate([mv[k * R + r, first:last] for r in range(R)], axis=1),
            precision=lax.Precision.HIGHEST,
            preferred_element_type=F32,
        )

    for g in range(groups):

        @pl.when(has_lo)
        def _():
            tile_copy(True, g).wait_recv()

        @pl.when(has_hi)
        def _():
            tile_copy(False, g).wait_recv()

        tracers = pl.ds(g * SUB, SUB)

        def along_x(k, carry):
            base = g * SUB * KR + k * R
            depth = lax.convert_element_type(k, F32)
            cells = []
            for r in range(R):
                value = lo[pl.ds(base + r, SUB, stride=KR), :]
                cells.append(jnp.where(depth < below[r : r + 1], value, 0.0))
            for r in range(R):
                cells.append(xs[k * R + r, tracers])
            for r in range(R):
                value = hi[pl.ds(base + r, SUB, stride=KR), :]
                cells.append(jnp.where(depth < above[r : r + 1], value, 0.0))
            diff = [b - a for a, b in zip(cells, cells[1:])]
            flux = []
            for face in range(R + 1):
                if face == 0:
                    c, weight = clow[0, pl.ds(k, 1)], clow[1, pl.ds(k, 1)]
                else:
                    at = pl.ds(k * R + face - 1, 1)
                    c, weight = coef[CX, at], coef[WX, at]
                flux.append(face_flux(c, weight, cells[face + 1], cells[face + 2], *diff[face : face + 3]))
            out = []
            for r in range(R):
                kr = k * R + r
                at = pl.ds(kr, 1)
                moved = mv[kr, tracers] + (flux[r] - flux[r + 1])
                rhs = moved * coef[INV, at] + coef[UINV, at] * carry[r]
                mv[kr, tracers] = rhs
                out.append(rhs)
            return tuple(out)

        zero = jnp.zeros((SUB, C), F32)
        lax.fori_loop(0, K, along_x, (zero,) * R, unroll=True)

        def upward(i, carry):
            k = K - 1 - i
            out = []
            for r in range(R):
                kr = k * R + r
                at = pl.ds(kr, 1)
                solved = mv[kr, tracers] - coef[RATIO, at] * carry[r]
                mv[kr, tracers] = solved
                part = jnp.sum(solved * first_rates[g * SUB : (g + 1) * SUB], axis=0, keepdims=True)
                if g > 0:
                    part = coef[ROW0, at] + part
                if g < groups - 1:
                    coef[ROW0, at] = part
                else:
                    wet = coef[WET, at]
                    value = wet * mv[kr, 0:1] + coef[WG, at] * part
                    coef[ABS, at] = wet * (0.02 + 0.04 * jnp.maximum(value, 0.0))
                out.append(solved)
            return tuple(out)

        lax.fori_loop(0, K, upward, (zero,) * R, unroll=True)

        if g == 0:

            def begin(k, carry):
                early[k] = products(k, 0, SUB)
                return carry

            lax.fori_loop(0, K, begin, 0, unroll=4)

    def shade(k, carry):
        out = []
        for r in range(R):
            at = pl.ds(k * R + r, 1)
            coef[OPT, at] = carry[r]
            out.append(carry[r] + coef[ABS, at])
        return tuple(out)

    lax.fori_loop(0, K, shade, (none,) * R, unroll=True)
    heat = 16.0 * jnp.exp(-coef[OPT]) * (1.0 - jnp.exp(-coef[ABS]))
    if hsend.shape[1] > LR:
        hsend[...] = jnp.zeros(hsend.shape, F32)
    for d in range(n):
        hsend[d, 0:LR] = heat[d * LR : (d + 1) * LR]

    def heat_copy(off):
        to = (me + off) % n
        return pltpu.make_async_remote_copy(
            src_ref=hsend.at[to],
            dst_ref=hrecv.at[me],
            send_sem=h_ssem.at[off],
            recv_sem=h_rsem.at[off],
            device_id={"sect": to},
            device_id_type=MESH,
        )

    for off in range(1, n):
        heat_copy(off).start()
    hrecv[pl.ds(me, 1)] = hsend[pl.ds(me, 1)]

    def react(k, carry):
        reacted = early[k] + late_products(k)
        for r in range(R):
            kr = k * R + r
            at = pl.ds(kr, 1)
            outp[pl.ds(kr, TP, stride=KR), :] = (
                coef[WET, at] * mv[kr] + coef[WG, at] * reacted[:, r * C : (r + 1) * C]
            )
        return carry

    lax.fori_loop(0, K, react, 0, unroll=True)

    for off in range(1, n):
        field_copy(off).wait_send()
    for g in range(groups):

        @pl.when(has_hi)
        def _():
            tile_copy(True, g).wait_send()

        @pl.when(has_lo)
        def _():
            tile_copy(False, g).wait_send()

    @pl.when(has_right)
    def _():
        edge_copy(True).wait_send()
        north_copy().wait_send()

    @pl.when(has_left)
    def _():
        edge_copy(False).wait_send()

    for off in range(1, n):
        heat_copy(off).wait_recv()
    for s in range(n):
        for l in range(L):
            heat_ref[l, s * R : (s + 1) * R] = hrecv[s, l * R : (l + 1) * R]
    for off in range(1, n):
        heat_copy(off).wait_send()


def store(adv, heat, adv_hbm, heat_hbm, sem):
    copies = (
        pltpu.make_async_copy(adv.at[pl.ds(0, adv_hbm.shape[0])], adv_hbm, sem.at[0]),
        pltpu.make_async_copy(heat, heat_hbm, sem.at[1]),
    )
    for copy in copies:
        copy.start()
    for copy in copies:
        copy.wait()


def body(sizes, solutes, tally, east, north, kappa, temp, salt, chemistry):
    T, K, R, C, n, ntx, nty = sizes
    KR, LR = K * R, K // n * R
    TP = round_up(T, SUB)
    groups = TP // SUB
    block = round_up(4 * LR + K // n + R, SUB)
    dma = pltpu.SemaphoreType.DMA
    vmem = pl.BlockSpec(memory_space=pltpu.VMEM)
    hbm = pl.BlockSpec(memory_space=pltpu.HBM)
    tile = pltpu.VMEM((TP * KR, C), F32)
    stack = pltpu.VMEM((KR, TP, C), F32)
    advanced, heating = pl.pallas_call(
        functools.partial(kernel, sizes),
        out_shape=(
            pltpu.VMEM((TP * KR, C), F32),
            pltpu.VMEM(east.shape, F32),
        ),
        in_specs=[hbm] * 8,
        out_specs=(vmem, vmem),
        scratch_shapes=[
            pltpu.VMEM(tally.shape, tally.dtype),
            *[pltpu.VMEM(east.shape, F32)] * 5,
            pltpu.VMEM(chemistry.shape, F32),
            tile,
            tile,
            tile,
            stack,
            stack,
            pltpu.VMEM((n, block, C), F32),
            pltpu.VMEM((n, block, C), F32),
            pltpu.VMEM((TP + SUB, C), F32),
            pltpu.VMEM((TP + SUB, C), F32),
            pltpu.VMEM((TP + SUB, C), F32),
            pltpu.VMEM((SUB, C), F32),
            pltpu.VMEM((SUB, C), F32),
            pltpu.VMEM((4, KR, C), F32),
            pltpu.VMEM((round_up(K, SUB), C), F32),
            pltpu.VMEM((13, KR, C), F32),
            pltpu.VMEM((2, round_up(K, SUB), C), F32),
            pltpu.VMEM((TP, C), F32),
            pltpu.VMEM((n, round_up(LR, SUB), C), F32),
            pltpu.VMEM((n, round_up(LR, SUB), C), F32),
            pltpu.VMEM((TP, C), F32),
            pltpu.VMEM((K, TP, R * C), F32),
            dma((n,)),
            dma((n,)),
            dma((2, groups)),
            dma((2, groups)),
            dma((2,)),
            dma((2,)),
            dma,
            dma,
            dma((n,)),
            dma((n,)),
            dma,
            dma((7,)),
        ],
        compiler_params=pltpu.CompilerParams(
            collective_id=0, has_side_effects=True, vmem_limit_bytes=VMEM_LIMIT
        ),
        name="ocean_step",
    )(solutes.reshape(T * KR, C), tally, east, north, kappa, temp, salt, chemistry)
    advanced, heating = pl.pallas_call(
        store,
        out_shape=(
            jax.ShapeDtypeStruct((T * KR, C), F32),
            jax.ShapeDtypeStruct(east.shape, F32),
        ),
        in_specs=[vmem, vmem],
        out_specs=(hbm, hbm),
        scratch_shapes=[dma((2,))],
        compiler_params=pltpu.CompilerParams(vmem_limit_bytes=1024 * 1024),
        name="store_outputs",
    )(advanced, heating)
    return advanced.reshape(T, K, R, C), heating


def solution(mesh):
    n, ntx, nty = (mesh.shape[axis] for axis in ("sect", "tx", "ty"))
    columns = P("sect", None, ("tx", "ty"))
    in_specs = (
        P(None, None, "sect", ("tx", "ty")),
        P("sect", ("tx", "ty")),
        columns,
        columns,
        columns,
        columns,
        columns,
        P(),
    )
    out_specs = (P(None, None, "sect", ("tx", "ty")), columns)

    def step(solutes, *rest):
        T, K, X, Y = solutes.shape
        R, C = X // n, Y // (ntx * nty)
        assert R == HALO and K % n == 0 and 4 * K * R == C
        sizes = (T, K, R, C, n, ntx, nty)
        return jax.shard_map(
            functools.partial(body, sizes),
            mesh=mesh,
            in_specs=in_specs,
            out_specs=out_specs,
            check_vma=False,
        )(solutes, *rest)

    return step
```

```python
import functools

import jax
import jax.numpy as jnp
from jax import lax
from jax.experimental import pallas as pl
from jax.experimental.pallas import tpu as pltpu
from jax.sharding import PartitionSpec as P

MESH = pl.DeviceIdType.MESH
SUB = 8
HALO = 2
F32 = jnp.float32
VMEM_LIMIT = 60 * 1024 * 1024


def round_up(value, unit):
    return -(-value // unit) * unit


def limited(first, second):
    return jnp.maximum(jnp.minimum(first, second), 0.0) + jnp.minimum(
        jnp.maximum(first, second), 0.0
    )


def face_flux(c, weight, near_low, near_high, low, mid, high):
    up = c >= 0
    base = jnp.where(up, near_low, near_high)
    return c * base + weight * limited(mid, jnp.where(up, low, high))


def limiter_weight(c):
    size = jnp.abs(c)
    return 0.5 * size * (1.0 - size)


def kernel(
    sizes,
    sol_hbm,
    tally_hbm,
    east_hbm,
    north_hbm,
    kappa_hbm,
    temp_hbm,
    salt_hbm,
    chem_hbm,
    outp,
    heat_ref,
    tally_ref,
    east_ref,
    north_ref,
    kappa_ref,
    temp_ref,
    salt_ref,
    chem_ref,
    own,
    lo,
    hi,
    xs,
    mv,
    fsend,
    frecv,
    ysend,
    yleft,
    yright,
    nsend,
    nleft,
    fld,
    elow,
    coef,
    clow,
    around,
    hsend,
    hrecv,
    chem,
    early,
    f_ssem,
    f_rsem,
    z_ssem,
    z_rsem,
    y_ssem,
    y_rsem,
    n_ssem,
    n_rsem,
    h_ssem,
    h_rsem,
    own_sem,
    in_sem,
):
    T, K, R, C, n, ntx, nty = sizes
    L = K // n
    LR = L * R
    KR = K * R
    TP = round_up(T, SUB)
    groups = TP // SUB
    me = lax.axis_index("sect")
    tx = lax.axis_index("tx")
    ty = lax.axis_index("ty")
    flat = tx * nty + ty
    has_lo = me > 0
    has_hi = me < n - 1
    has_left = flat > 0
    has_right = flat < ntx * nty - 1
    left = {"tx": (flat + ntx * nty - 1) % (ntx * nty) // nty, "ty": (flat + ntx * nty - 1) % nty}
    right = {"tx": (flat + 1) % (ntx * nty) // nty, "ty": (flat + 1) % nty}

    pairs = (
        (tally_hbm, tally_ref),
        (east_hbm, east_ref),
        (north_hbm, north_ref),
        (kappa_hbm, kappa_ref),
        (temp_hbm, temp_ref),
        (salt_hbm, salt_ref),
        (chem_hbm, chem_ref),
    )
    fetches = [pltpu.make_async_copy(a, b, in_sem.at[i]) for i, (a, b) in enumerate(pairs)]
    for fetch in fetches:
        fetch.start()
    own_copy = pltpu.make_async_copy(sol_hbm, own.at[pl.ds(0, T * KR)], own_sem)
    own_copy.start()

    def beside(off, side):
        return {"sect": (me + off) % n, **side}

    def greet(device):
        pl.semaphore_signal(barrier, inc=1, device_id=device, device_id_type=MESH)

    barrier = pltpu.get_barrier_semaphore()
    for off in range(1, n):
        greet({"sect": (me + off) % n})

    @pl.when(has_left)
    def _():
        for off in range(n):
            greet(beside(off, left))

    @pl.when(has_right)
    def _():
        for off in range(n):
            greet(beside(off, right))

    sides = has_left.astype(jnp.int32) + has_right.astype(jnp.int32)
    pl.semaphore_wait(barrier, n - 1 + n * sides)

    def tile_copy(up, g):
        rows = pl.ds(g * SUB * KR, (min((g + 1) * SUB, T) - g * SUB) * KR)
        return pltpu.make_async_remote_copy(
            src_ref=sol_hbm.at[rows],
            dst_ref=(lo if up else hi).at[rows],
            send_sem=z_ssem.at[int(up), g],
            recv_sem=z_rsem.at[int(up), g],
            device_id={"sect": (me + 1) % n if up else (me + n - 1) % n},
            device_id_type=MESH,
        )

    def send_tiles(g):
        @pl.when(has_hi)
        def _():
            tile_copy(True, g).start()

        @pl.when(has_lo)
        def _():
            tile_copy(False, g).start()

    for fetch in fetches:
        fetch.wait()

    growth = jnp.exp(0.0633 * (temp_ref[...] - 15.0)) * (1.0 + 0.25 * (salt_ref[...] - 35.0))
    tally = tally_ref[...].astype(F32)
    used = 4 * LR + L + R
    block_rows = fsend.shape[1]
    fsend[...] = jnp.zeros(fsend.shape, F32)
    for d in range(n):
        for l in range(L):
            at = l * R
            rows = slice(d * R, (d + 1) * R)
            fsend[d, at : at + R] = east_ref[l, rows]
            fsend[d, LR + at : LR + at + R] = north_ref[l, rows]
            fsend[d, 2 * LR + at : 2 * LR + at + R] = kappa_ref[l, rows]
            fsend[d, 3 * LR + at : 3 * LR + at + R] = growth[l, d * R : (d + 1) * R]
            if d > 0:
                fsend[d, 4 * LR + l : 4 * LR + l + 1] = east_ref[l, d * R - 1 : d * R]
        fsend[d, used - R : used] = tally
    if nsend.shape[1] > LR:
        nsend[...] = jnp.zeros(nsend.shape, F32)
    for d in range(n):
        nsend[d, 0:LR] = fsend[d, LR : 2 * LR]

    def field_copy(off):
        to = (me + off) % n
        return pltpu.make_async_remote_copy(
            src_ref=fsend.at[to],
            dst_ref=frecv.at[me],
            send_sem=f_ssem.at[off],
            recv_sem=f_rsem.at[off],
            device_id={"sect": to},
            device_id_type=MESH,
        )

    def north_copy(off):
        return pltpu.make_async_remote_copy(
            src_ref=nsend.at[(me + off) % n],
            dst_ref=nleft.at[me],
            send_sem=n_ssem.at[off],
            recv_sem=n_rsem.at[off],
            device_id=beside(off, right),
            device_id_type=MESH,
        )

    for off in range(1, n):
        field_copy(off).start()

    @pl.when(has_right)
    def _():
        for off in range(n):
            north_copy(off).start()

    for g in range(groups):
        send_tiles(g)

    frecv[pl.ds(me, 1)] = fsend[pl.ds(me, 1)]

    for buf in (own, lo, hi):
        if TP > T:
            buf[T * KR :] = jnp.zeros(((TP - T) * KR, C), F32)

    lane_t = lax.broadcasted_iota(jnp.int32, (TP, C), 1)
    tal_row = [tally[r : r + 1] for r in range(R)]
    own_copy.wait()

    def pack(k, packed):
        for r in range(R):
            kr = k * R + r
            wet = lax.convert_element_type(k, F32) < tal_row[r]
            cells = jnp.where(wet, own[pl.ds(kr, TP, stride=KR), :], 0.0)
            xs[kr] = cells
            moved_edge = pltpu.roll(cells, HALO + 4 * kr, 1)
            packed = jnp.where(jnp.right_shift(lane_t, 2) == kr, moved_edge, packed)
        return packed

    packed_own = lax.fori_loop(0, K, pack, jnp.zeros((TP, C), F32), unroll=True)
    ysend[0:TP] = packed_own
    ysend[TP:] = jnp.zeros((SUB, C), F32)
    ysend[TP : TP + R] = tally

    def edge_copy(to_right):
        return pltpu.make_async_remote_copy(
            src_ref=ysend,
            dst_ref=yleft if to_right else yright,
            send_sem=y_ssem.at[int(to_right)],
            recv_sem=y_rsem.at[int(to_right)],
            device_id=right if to_right else left,
            device_id_type=MESH,
        )

    @pl.when(has_right)
    def _():
        edge_copy(True).start()

    @pl.when(has_left)
    def _():
        edge_copy(False).start()

    @pl.when(has_left)
    def _():
        edge_copy(True).wait_recv()

    @pl.when(has_right)
    def _():
        edge_copy(False).wait_recv()

    left_cols = jnp.where(has_left, yleft[0:TP], 0.0)
    right_cols = jnp.where(has_right, yright[0:TP], 0.0)
    tal_left = jnp.where(has_left, yleft[TP : TP + R], 0.0)
    tal_right = jnp.where(has_right, yright[TP : TP + R], 0.0)
    edges = jnp.where(jnp.bitwise_and(lane_t, 3) < HALO, left_cols, right_cols)

    def slopes(k, carry):
        for r in range(R):
            kr = k * R + r
            cells = xs[kr]
            side = pltpu.roll(edges, C - HALO - 4 * kr, 1)
            prv = pltpu.roll(jnp.where(lane_t == C - 1, side, cells), 1, 1)
            prv2 = pltpu.roll(jnp.where(lane_t >= C - HALO, side, cells), HALO, 1)
            nxt = pltpu.roll(jnp.where(lane_t == 0, side, cells), C - 1, 1)
            nxt2 = pltpu.roll(jnp.where(lane_t < HALO, side, cells), C - HALO, 1)
            back, ahead = cells - prv, nxt - cells
            around[0, kr] = prv
            around[1, kr] = nxt
            around[2, kr] = limited(prv - prv2, back)
            around[3, kr] = limited(back, ahead)
            around[4, kr] = limited(ahead, nxt2 - nxt)
        return carry

    lax.fori_loop(0, K, slopes, 0, unroll=4)

    for off in range(1, n):
        field_copy(off).wait_recv()
    for s in range(n):
        for f in range(4):
            fld[f, s * LR : (s + 1) * LR] = frecv[s, f * LR : (f + 1) * LR]
        elow[s * L : (s + 1) * L] = frecv[s, 4 * LR : 4 * LR + L]

    @pl.when(has_left)
    def _():
        for off in range(n):
            north_copy(off).wait_recv()

    for s in range(n):
        fld[4, s * LR : (s + 1) * LR] = nleft[s, 0:LR]

    row = lax.broadcasted_iota(jnp.int32, (KR, C), 0)
    lane = lax.broadcasted_iota(jnp.int32, (KR, C), 1)
    level = jnp.right_shift(row, 1).astype(F32)
    odd = jnp.bitwise_and(row, 1) == 1
    north = fld[1]
    below = frecv[lax.rem(me + n - 1, n), used - R : used]
    above = frecv[lax.rem(me + 1, n), used - R : used]
    below = jnp.where(has_lo, below, 0.0)
    above = jnp.where(has_hi, above, 0.0)
    tal = jnp.where(odd, tal_row[1], tal_row[0])
    tal_next = jnp.where(odd, above[0:1], tal_row[1])
    CX, WX, INV, UINV, RATIO, COUP, WET, WG, ABS, OPT, ROW0, CY = range(12)
    c_x = jnp.where(level < jnp.minimum(tal, tal_next), fld[0], 0.0)
    coef[CX] = c_x
    coef[WX] = limiter_weight(c_x)
    level_k = lax.broadcasted_iota(jnp.int32, (K, C), 0).astype(F32)
    c_low = jnp.where(level_k < jnp.minimum(below[R - 1 : R], tal_row[0]), elow[0:K], 0.0)
    clow[0] = c_low
    clow[1] = limiter_weight(c_low)
    wet_all = (level < tal).astype(F32)
    coef[WET] = wet_all
    coef[WG] = wet_all * (0.2 * fld[3])
    coef[COUP] = jnp.where(level + 1.0 < tal, fld[2], 0.0)

    tal_far = jnp.where(odd, tal_right[1:2], tal_right[0:1])
    tal_near = jnp.where(odd, tal_left[1:2], tal_left[0:1])
    tal_east = pltpu.roll(jnp.where(lane == 0, tal_far, tal), C - 1, 1)
    tal_west = pltpu.roll(jnp.where(lane == C - 1, tal_near, tal), 1, 1)
    north_west = pltpu.roll(jnp.where(lane == C - 1, fld[4], north), 1, 1)
    c_up = jnp.where(level < jnp.minimum(tal, tal_east), north, 0.0)
    c_dn = jnp.where(level < jnp.minimum(tal, tal_west), north_west, 0.0)
    w_up, w_dn = limiter_weight(c_up), limiter_weight(c_dn)
    coef[CY] = jnp.maximum(c_dn, 0.0)
    coef[CY + 1] = 1.0 + jnp.minimum(c_dn, 0.0) - jnp.maximum(c_up, 0.0)
    coef[CY + 2] = -jnp.minimum(c_up, 0.0)
    coef[CY + 3] = jnp.where(c_dn >= 0, w_dn, 0.0)
    coef[CY + 4] = jnp.where(c_dn >= 0, 0.0, w_dn) - jnp.where(c_up >= 0, w_up, 0.0)
    coef[CY + 5] = jnp.where(c_up >= 0, 0.0, -w_up)

    def along_y(k, carry):
        out = []
        for r in range(R):
            ratio, above_link = carry[r]
            kr = k * R + r
            at = pl.ds(kr, 1)
            link = coef[COUP, at]
            inverse = 1.0 / (1.0 + above_link + link + above_link * ratio)
            ratio = -link * inverse
            coef[INV, at] = inverse
            coef[UINV, at] = above_link * inverse
            coef[RATIO, at] = ratio
            out.append((ratio, link))
            mv[kr] = (
                coef[CY, at] * around[0, kr]
                + coef[CY + 1, at] * xs[kr]
                + coef[CY + 2, at] * around[1, kr]
            ) + (
                coef[CY + 3, at] * around[2, kr]
                + coef[CY + 4, at] * around[3, kr]
                + coef[CY + 5, at] * around[4, kr]
            )
        return tuple(out)

    none = jnp.zeros((1, C), F32)
    lax.fori_loop(0, K, along_y, tuple((none, none) for _ in range(R)), unroll=True)

    chem[...] = jnp.zeros(chem.shape, F32)
    chem[0:T, 0:T] = chem_ref[...]
    square = (TP, TP)
    across = lax.broadcasted_iota(jnp.int32, square, 1)
    down = lax.broadcasted_iota(jnp.int32, square, 0)
    first_row = jnp.where(across == down, jnp.broadcast_to(chem[0:1, 0:TP], square), 0.0)
    first_rates = jnp.broadcast_to(jnp.sum(first_row, axis=1, keepdims=True), (TP, C))

    rest = TP - SUB
    rates = chem[...]
    rates_high = rates.astype(jnp.bfloat16).astype(F32)
    rates_low = rates - rates_high
    halves = jnp.where(
        lane_t < rest,
        pltpu.roll(rates_high, C - SUB, 1),
        jnp.where(
            lane_t < 2 * rest,
            pltpu.roll(rates_high, (rest + C - SUB) % C, 1),
            pltpu.roll(rates_low, (2 * rest + C - SUB) % C, 1),
        ),
    )[:, 0 : 3 * rest].astype(jnp.bfloat16)

    def late_products(k):
        mixed = jnp.concatenate([mv[k * R + r, SUB:TP] for r in range(R)], axis=1)
        high = mixed.astype(jnp.bfloat16)
        low = (mixed - high.astype(F32)).astype(jnp.bfloat16)
        return jnp.dot(
            halves,
            jnp.concatenate([high, low, high], axis=0),
            preferred_element_type=F32,
        )

    def products(k, first, last):
        return jnp.dot(
            chem[:, first:last],
            jnp.concatenate([mv[k * R + r, first:last] for r in range(R)], axis=1),
            precision=lax.Precision.HIGHEST,
            preferred_element_type=F32,
        )

    for g in range(groups):

        @pl.when(has_lo)
        def _():
            tile_copy(True, g).wait_recv()

        @pl.when(has_hi)
        def _():
            tile_copy(False, g).wait_recv()

        tracers = pl.ds(g * SUB, SUB)

        def along_x(k, carry):
            base = g * SUB * KR + k * R
            depth = lax.convert_element_type(k, F32)
            cells = []
            for r in range(R):
                value = lo[pl.ds(base + r, SUB, stride=KR), :]
                cells.append(jnp.where(depth < below[r : r + 1], value, 0.0))
            for r in range(R):
                cells.append(xs[k * R + r, tracers])
            for r in range(R):
                value = hi[pl.ds(base + r, SUB, stride=KR), :]
                cells.append(jnp.where(depth < above[r : r + 1], value, 0.0))
            diff = [b - a for a, b in zip(cells, cells[1:])]
            flux = []
            for face in range(R + 1):
                if face == 0:
                    c, weight = clow[0, pl.ds(k, 1)], clow[1, pl.ds(k, 1)]
                else:
                    at = pl.ds(k * R + face - 1, 1)
                    c, weight = coef[CX, at], coef[WX, at]
                flux.append(face_flux(c, weight, cells[face + 1], cells[face + 2], *diff[face : face + 3]))
            out = []
            for r in range(R):
                kr = k * R + r
                at = pl.ds(kr, 1)
                moved = mv[kr, tracers] + (flux[r] - flux[r + 1])
                rhs = moved * coef[INV, at] + coef[UINV, at] * carry[r]
                mv[kr, tracers] = rhs
                out.append(rhs)
            return tuple(out)

        zero = jnp.zeros((SUB, C), F32)
        lax.fori_loop(0, K, along_x, (zero,) * R, unroll=True)

        def upward(i, carry):
            k = K - 1 - i
            out = []
            for r in range(R):
                kr = k * R + r
                at = pl.ds(kr, 1)
                solved = mv[kr, tracers] - coef[RATIO, at] * carry[r]
                mv[kr, tracers] = solved
                part = jnp.sum(solved * first_rates[g * SUB : (g + 1) * SUB], axis=0, keepdims=True)
                if g > 0:
                    part = coef[ROW0, at] + part
                if g < groups - 1:
                    coef[ROW0, at] = part
                else:
                    wet = coef[WET, at]
                    value = wet * mv[kr, 0:1] + coef[WG, at] * part
                    coef[ABS, at] = wet * (0.02 + 0.04 * jnp.maximum(value, 0.0))
                out.append(solved)
            return tuple(out)

        lax.fori_loop(0, K, upward, (zero,) * R, unroll=True)

        if g == 0:

            def begin(k, carry):
                early[k] = products(k, 0, SUB)
                return carry

            lax.fori_loop(0, K, begin, 0, unroll=4)

    def shade(k, carry):
        out = []
        for r in range(R):
            at = pl.ds(k * R + r, 1)
            coef[OPT, at] = carry[r]
            out.append(carry[r] + coef[ABS, at])
        return tuple(out)

    lax.fori_loop(0, K, shade, (none,) * R, unroll=True)
    heat = 16.0 * jnp.exp(-coef[OPT]) * (1.0 - jnp.exp(-coef[ABS]))
    if hsend.shape[1] > LR:
        hsend[...] = jnp.zeros(hsend.shape, F32)
    for d in range(n):
        hsend[d, 0:LR] = heat[d * LR : (d + 1) * LR]

    def heat_copy(off):
        to = (me + off) % n
        return pltpu.make_async_remote_copy(
            src_ref=hsend.at[to],
            dst_ref=hrecv.at[me],
            send_sem=h_ssem.at[off],
            recv_sem=h_rsem.at[off],
            device_id={"sect": to},
            device_id_type=MESH,
        )

    for off in range(1, n):
        heat_copy(off).start()
    hrecv[pl.ds(me, 1)] = hsend[pl.ds(me, 1)]

    def react(k, carry):
        reacted = early[k] + late_products(k)
        for r in range(R):
            kr = k * R + r
            at = pl.ds(kr, 1)
            outp[pl.ds(kr, TP, stride=KR), :] = (
                coef[WET, at] * mv[kr] + coef[WG, at] * reacted[:, r * C : (r + 1) * C]
            )
        return carry

    lax.fori_loop(0, K, react, 0, unroll=True)

    for off in range(1, n):
        field_copy(off).wait_send()
    for g in range(groups):

        @pl.when(has_hi)
        def _():
            tile_copy(True, g).wait_send()

        @pl.when(has_lo)
        def _():
            tile_copy(False, g).wait_send()

    @pl.when(has_right)
    def _():
        edge_copy(True).wait_send()
        for off in range(n):
            north_copy(off).wait_send()

    @pl.when(has_left)
    def _():
        edge_copy(False).wait_send()

    for off in range(1, n):
        heat_copy(off).wait_recv()
    for s in range(n):
        for l in range(L):
            heat_ref[l, s * R : (s + 1) * R] = hrecv[s, l * R : (l + 1) * R]
    for off in range(1, n):
        heat_copy(off).wait_send()


def store(adv, heat, adv_hbm, heat_hbm, sem):
    copies = (
        pltpu.make_async_copy(adv.at[pl.ds(0, adv_hbm.shape[0])], adv_hbm, sem.at[0]),
        pltpu.make_async_copy(heat, heat_hbm, sem.at[1]),
    )
    for copy in copies:
        copy.start()
    for copy in copies:
        copy.wait()


def body(sizes, solutes, tally, east, north, kappa, temp, salt, chemistry):
    T, K, R, C, n, ntx, nty = sizes
    KR, LR = K * R, K // n * R
    TP = round_up(T, SUB)
    groups = TP // SUB
    block = round_up(4 * LR + K // n + R, SUB)
    dma = pltpu.SemaphoreType.DMA
    vmem = pl.BlockSpec(memory_space=pltpu.VMEM)
    hbm = pl.BlockSpec(memory_space=pltpu.HBM)
    tile = pltpu.VMEM((TP * KR, C), F32)
    stack = pltpu.VMEM((KR, TP, C), F32)
    advanced, heating = pl.pallas_call(
        functools.partial(kernel, sizes),
        out_shape=(
            pltpu.VMEM((TP * KR, C), F32),
            pltpu.VMEM(east.shape, F32),
        ),
        in_specs=[hbm] * 8,
        out_specs=(vmem, vmem),
        scratch_shapes=[
            pltpu.VMEM(tally.shape, tally.dtype),
            *[pltpu.VMEM(east.shape, F32)] * 5,
            pltpu.VMEM(chemistry.shape, F32),
            tile,
            tile,
            tile,
            stack,
            stack,
            pltpu.VMEM((n, block, C), F32),
            pltpu.VMEM((n, block, C), F32),
            pltpu.VMEM((TP + SUB, C), F32),
            pltpu.VMEM((TP + SUB, C), F32),
            pltpu.VMEM((TP + SUB, C), F32),
            pltpu.VMEM((n, round_up(LR, SUB), C), F32),
            pltpu.VMEM((n, round_up(LR, SUB), C), F32),
            pltpu.VMEM((5, KR, C), F32),
            pltpu.VMEM((round_up(K, SUB), C), F32),
            pltpu.VMEM((17, KR, C), F32),
            pltpu.VMEM((2, round_up(K, SUB), C), F32),
            pltpu.VMEM((5, KR, TP, C), F32),
            pltpu.VMEM((n, round_up(LR, SUB), C), F32),
            pltpu.VMEM((n, round_up(LR, SUB), C), F32),
            pltpu.VMEM((TP, C), F32),
            pltpu.VMEM((K, TP, R * C), F32),
            dma((n,)),
            dma((n,)),
            dma((2, groups)),
            dma((2, groups)),
            dma((2,)),
            dma((2,)),
            dma((n,)),
            dma((n,)),
            dma((n,)),
            dma((n,)),
            dma,
            dma((7,)),
        ],
        compiler_params=pltpu.CompilerParams(
            collective_id=0, has_side_effects=True, vmem_limit_bytes=VMEM_LIMIT
        ),
        name="ocean_step",
    )(solutes.reshape(T * KR, C), tally, east, north, kappa, temp, salt, chemistry)
    advanced, heating = pl.pallas_call(
        store,
        out_shape=(
            jax.ShapeDtypeStruct((T * KR, C), F32),
            jax.ShapeDtypeStruct(east.shape, F32),
        ),
        in_specs=[vmem, vmem],
        out_specs=(hbm, hbm),
        scratch_shapes=[dma((2,))],
        compiler_params=pltpu.CompilerParams(vmem_limit_bytes=1024 * 1024),
        name="store_outputs",
    )(advanced, heating)
    return advanced.reshape(T, K, R, C), heating


def solution(mesh):
    n, ntx, nty = (mesh.shape[axis] for axis in ("sect", "tx", "ty"))
    columns = P("sect", None, ("tx", "ty"))
    in_specs = (
        P(None, None, "sect", ("tx", "ty")),
        P("sect", ("tx", "ty")),
        columns,
        columns,
        columns,
        columns,
        columns,
        P(),
    )
    out_specs = (P(None, None, "sect", ("tx", "ty")), columns)

    def step(solutes, *rest):
        T, K, X, Y = solutes.shape
        R, C = X // n, Y // (ntx * nty)
        assert R == HALO and K % n == 0 and 4 * K * R == C
        sizes = (T, K, R, C, n, ntx, nty)
        return jax.shard_map(
            functools.partial(body, sizes),
            mesh=mesh,
            in_specs=in_specs,
            out_specs=out_specs,
            check_vma=False,
        )(solutes, *rest)

    return step
```

```python
import functools

import jax
import jax.numpy as jnp
from jax import lax
from jax.experimental import pallas as pl
from jax.experimental.pallas import tpu as pltpu
from jax.sharding import PartitionSpec as P

MESH = pl.DeviceIdType.MESH
SUB = 8
HALO = 2
F32 = jnp.float32
VMEM_LIMIT = 60 * 1024 * 1024


def round_up(value, unit):
    return -(-value // unit) * unit


def limited(first, second):
    return jnp.maximum(jnp.minimum(first, second), 0.0) + jnp.minimum(
        jnp.maximum(first, second), 0.0
    )


def face_flux(c, weight, near_low, near_high, low, mid, high):
    up = c >= 0
    base = jnp.where(up, near_low, near_high)
    return c * base + weight * limited(mid, jnp.where(up, low, high))


def limiter_weight(c):
    size = jnp.abs(c)
    return 0.5 * size * (1.0 - size)


def kernel(
    sizes,
    sol_hbm,
    tally_hbm,
    east_hbm,
    north_hbm,
    kappa_hbm,
    temp_hbm,
    salt_hbm,
    chem_hbm,
    outp,
    heat_ref,
    tally_ref,
    east_ref,
    north_ref,
    kappa_ref,
    temp_ref,
    salt_ref,
    chem_ref,
    own,
    lo,
    hi,
    xs,
    mv,
    fsend,
    frecv,
    ysend,
    yleft,
    yright,
    nsend,
    nleft,
    fld,
    elow,
    coef,
    clow,
    around,
    hsend,
    hrecv,
    chem,
    early,
    f_ssem,
    f_rsem,
    z_ssem,
    z_rsem,
    y_ssem,
    y_rsem,
    n_ssem,
    n_rsem,
    h_ssem,
    h_rsem,
    own_sem,
    in_sem,
):
    T, K, R, C, n, ntx, nty = sizes
    L = K // n
    LR = L * R
    KR = K * R
    TP = round_up(T, SUB)
    groups = TP // SUB
    me = lax.axis_index("sect")
    tx = lax.axis_index("tx")
    ty = lax.axis_index("ty")
    flat = tx * nty + ty
    has_lo = me > 0
    has_hi = me < n - 1
    has_left = flat > 0
    has_right = flat < ntx * nty - 1
    left = {"tx": (flat + ntx * nty - 1) % (ntx * nty) // nty, "ty": (flat + ntx * nty - 1) % nty}
    right = {"tx": (flat + 1) % (ntx * nty) // nty, "ty": (flat + 1) % nty}

    pairs = (
        (tally_hbm, tally_ref),
        (east_hbm, east_ref),
        (north_hbm, north_ref),
        (kappa_hbm, kappa_ref),
        (temp_hbm, temp_ref),
        (salt_hbm, salt_ref),
        (chem_hbm, chem_ref),
    )
    fetches = [pltpu.make_async_copy(a, b, in_sem.at[i]) for i, (a, b) in enumerate(pairs)]
    for fetch in fetches:
        fetch.start()
    own_copy = pltpu.make_async_copy(sol_hbm, own.at[pl.ds(0, T * KR)], own_sem)
    own_copy.start()

    def beside(off, side):
        return {"sect": (me + off) % n, **side}

    def greet(device):
        pl.semaphore_signal(barrier, inc=1, device_id=device, device_id_type=MESH)

    barrier = pltpu.get_barrier_semaphore()
    for off in range(1, n):
        greet({"sect": (me + off) % n})

    @pl.when(has_left)
    def _():
        for off in range(n):
            greet(beside(off, left))

    @pl.when(has_right)
    def _():
        for off in range(n):
            greet(beside(off, right))

    sides = has_left.astype(jnp.int32) + has_right.astype(jnp.int32)
    pl.semaphore_wait(barrier, n - 1 + n * sides)

    def tile_copy(up, g):
        rows = pl.ds(g * SUB * KR, (min((g + 1) * SUB, T) - g * SUB) * KR)
        return pltpu.make_async_remote_copy(
            src_ref=sol_hbm.at[rows],
            dst_ref=(lo if up else hi).at[rows],
            send_sem=z_ssem.at[int(up), g],
            recv_sem=z_rsem.at[int(up), g],
            device_id={"sect": (me + 1) % n if up else (me + n - 1) % n},
            device_id_type=MESH,
        )

    def send_tiles(g):
        @pl.when(has_hi)
        def _():
            tile_copy(True, g).start()

        @pl.when(has_lo)
        def _():
            tile_copy(False, g).start()

    for fetch in fetches:
        fetch.wait()

    growth = jnp.exp(0.0633 * (temp_ref[...] - 15.0)) * (1.0 + 0.25 * (salt_ref[...] - 35.0))
    tally = tally_ref[...].astype(F32)
    used = 4 * LR + L + R
    block_rows = fsend.shape[1]
    fsend[...] = jnp.zeros(fsend.shape, F32)
    for d in range(n):
        for l in range(L):
            at = l * R
            rows = slice(d * R, (d + 1) * R)
            fsend[d, at : at + R] = east_ref[l, rows]
            fsend[d, LR + at : LR + at + R] = north_ref[l, rows]
            fsend[d, 2 * LR + at : 2 * LR + at + R] = kappa_ref[l, rows]
            fsend[d, 3 * LR + at : 3 * LR + at + R] = growth[l, d * R : (d + 1) * R]
            if d > 0:
                fsend[d, 4 * LR + l : 4 * LR + l + 1] = east_ref[l, d * R - 1 : d * R]
        fsend[d, used - R : used] = tally
    if nsend.shape[1] > LR:
        nsend[...] = jnp.zeros(nsend.shape, F32)
    for d in range(n):
        nsend[d, 0:LR] = fsend[d, LR : 2 * LR]

    def field_copy(off):
        to = (me + off) % n
        return pltpu.make_async_remote_copy(
            src_ref=fsend.at[to],
            dst_ref=frecv.at[me],
            send_sem=f_ssem.at[off],
            recv_sem=f_rsem.at[off],
            device_id={"sect": to},
            device_id_type=MESH,
        )

    def north_copy(off):
        return pltpu.make_async_remote_copy(
            src_ref=nsend.at[(me + off) % n],
            dst_ref=nleft.at[me],
            send_sem=n_ssem.at[off],
            recv_sem=n_rsem.at[off],
            device_id=beside(off, right),
            device_id_type=MESH,
        )

    for off in range(1, n):
        field_copy(off).start()

    @pl.when(has_right)
    def _():
        for off in range(n):
            north_copy(off).start()

    frecv[pl.ds(me, 1)] = fsend[pl.ds(me, 1)]

    for buf in (own,):
        if TP > T:
            buf[T * KR :] = jnp.zeros(((TP - T) * KR, C), F32)

    lane_t = lax.broadcasted_iota(jnp.int32, (TP, C), 1)
    tal_row = [tally[r : r + 1] for r in range(R)]
    own_copy.wait()

    def pack(k, packed):
        for r in range(R):
            kr = k * R + r
            wet = lax.convert_element_type(k, F32) < tal_row[r]
            cells = jnp.where(wet, own[pl.ds(kr, TP, stride=KR), :], 0.0)
            xs[kr] = cells
            moved_edge = pltpu.roll(cells, HALO + 4 * kr, 1)
            packed = jnp.where(jnp.right_shift(lane_t, 2) == kr, moved_edge, packed)
        return packed

    packed_own = lax.fori_loop(0, K, pack, jnp.zeros((TP, C), F32), unroll=True)
    ysend[0:TP] = packed_own
    ysend[TP:] = jnp.zeros((SUB, C), F32)
    ysend[TP : TP + R] = tally

    def edge_copy(to_right):
        return pltpu.make_async_remote_copy(
            src_ref=ysend,
            dst_ref=yleft if to_right else yright,
            send_sem=y_ssem.at[int(to_right)],
            recv_sem=y_rsem.at[int(to_right)],
            device_id=right if to_right else left,
            device_id_type=MESH,
        )

    @pl.when(has_right)
    def _():
        edge_copy(True).start()

    @pl.when(has_left)
    def _():
        edge_copy(False).start()

    for g in range(groups):
        send_tiles(g)

    for buf in (lo, hi):
        if TP > T:
            buf[T * KR :] = jnp.zeros(((TP - T) * KR, C), F32)

    @pl.when(has_left)
    def _():
        edge_copy(True).wait_recv()

    @pl.when(has_right)
    def _():
        edge_copy(False).wait_recv()

    left_cols = jnp.where(has_left, yleft[0:TP], 0.0)
    right_cols = jnp.where(has_right, yright[0:TP], 0.0)
    tal_left = jnp.where(has_left, yleft[TP : TP + R], 0.0)
    tal_right = jnp.where(has_right, yright[TP : TP + R], 0.0)
    edges = jnp.where(jnp.bitwise_and(lane_t, 3) < HALO, left_cols, right_cols)

    def slopes(k, carry):
        for r in range(R):
            kr = k * R + r
            cells = xs[kr]
            side = pltpu.roll(edges, C - HALO - 4 * kr, 1)
            prv = pltpu.roll(jnp.where(lane_t == C - 1, side, cells), 1, 1)
            prv2 = pltpu.roll(jnp.where(lane_t >= C - HALO, side, cells), HALO, 1)
            nxt = pltpu.roll(jnp.where(lane_t == 0, side, cells), C - 1, 1)
            nxt2 = pltpu.roll(jnp.where(lane_t < HALO, side, cells), C - HALO, 1)
            back, ahead = cells - prv, nxt - cells
            around[0, kr] = prv
            around[1, kr] = nxt
            around[2, kr] = limited(prv - prv2, back)
            around[3, kr] = limited(back, ahead)
            around[4, kr] = limited(ahead, nxt2 - nxt)
        return carry

    lax.fori_loop(0, K, slopes, 0, unroll=4)

    for off in range(1, n):
        field_copy(off).wait_recv()
    for s in range(n):
        for f in range(4):
            fld[f, s * LR : (s + 1) * LR] = frecv[s, f * LR : (f + 1) * LR]
        elow[s * L : (s + 1) * L] = frecv[s, 4 * LR : 4 * LR + L]

    @pl.when(has_left)
    def _():
        for off in range(n):
            north_copy(off).wait_recv()

    for s in range(n):
        fld[4, s * LR : (s + 1) * LR] = nleft[s, 0:LR]

    row = lax.broadcasted_iota(jnp.int32, (KR, C), 0)
    lane = lax.broadcasted_iota(jnp.int32, (KR, C), 1)
    level = jnp.right_shift(row, 1).astype(F32)
    odd = jnp.bitwise_and(row, 1) == 1
    north = fld[1]
    below = frecv[lax.rem(me + n - 1, n), used - R : used]
    above = frecv[lax.rem(me + 1, n), used - R : used]
    below = jnp.where(has_lo, below, 0.0)
    above = jnp.where(has_hi, above, 0.0)
    tal = jnp.where(odd, tal_row[1], tal_row[0])
    tal_next = jnp.where(odd, above[0:1], tal_row[1])
    CX, WX, INV, UINV, RATIO, COUP, WET, WG, ABS, OPT, ROW0, CY = range(12)
    c_x = jnp.where(level < jnp.minimum(tal, tal_next), fld[0], 0.0)
    coef[CX] = c_x
    coef[WX] = limiter_weight(c_x)
    level_k = lax.broadcasted_iota(jnp.int32, (K, C), 0).astype(F32)
    c_low = jnp.where(level_k < jnp.minimum(below[R - 1 : R], tal_row[0]), elow[0:K], 0.0)
    clow[0] = c_low
    clow[1] = limiter_weight(c_low)
    wet_all = (level < tal).astype(F32)
    coef[WET] = wet_all
    coef[WG] = wet_all * (0.2 * fld[3])
    coef[COUP] = jnp.where(level + 1.0 < tal, fld[2], 0.0)

    tal_far = jnp.where(odd, tal_right[1:2], tal_right[0:1])
    tal_near = jnp.where(odd, tal_left[1:2], tal_left[0:1])
    tal_east = pltpu.roll(jnp.where(lane == 0, tal_far, tal), C - 1, 1)
    tal_west = pltpu.roll(jnp.where(lane == C - 1, tal_near, tal), 1, 1)
    north_west = pltpu.roll(jnp.where(lane == C - 1, fld[4], north), 1, 1)
    c_up = jnp.where(level < jnp.minimum(tal, tal_east), north, 0.0)
    c_dn = jnp.where(level < jnp.minimum(tal, tal_west), north_west, 0.0)
    w_up, w_dn = limiter_weight(c_up), limiter_weight(c_dn)
    coef[CY] = jnp.maximum(c_dn, 0.0)
    coef[CY + 1] = 1.0 + jnp.minimum(c_dn, 0.0) - jnp.maximum(c_up, 0.0)
    coef[CY + 2] = -jnp.minimum(c_up, 0.0)
    coef[CY + 3] = jnp.where(c_dn >= 0, w_dn, 0.0)
    coef[CY + 4] = jnp.where(c_dn >= 0, 0.0, w_dn) - jnp.where(c_up >= 0, w_up, 0.0)
    coef[CY + 5] = jnp.where(c_up >= 0, 0.0, -w_up)

    def along_y(k, carry):
        out = []
        for r in range(R):
            ratio, above_link = carry[r]
            kr = k * R + r
            at = pl.ds(kr, 1)
            link = coef[COUP, at]
            inverse = 1.0 / (1.0 + above_link + link + above_link * ratio)
            ratio = -link * inverse
            coef[INV, at] = inverse
            coef[UINV, at] = above_link * inverse
            coef[RATIO, at] = ratio
            out.append((ratio, link))
            mv[kr] = (
                coef[CY, at] * around[0, kr]
                + coef[CY + 1, at] * xs[kr]
                + coef[CY + 2, at] * around[1, kr]
            ) + (
                coef[CY + 3, at] * around[2, kr]
                + coef[CY + 4, at] * around[3, kr]
                + coef[CY + 5, at] * around[4, kr]
            )
        return tuple(out)

    none = jnp.zeros((1, C), F32)
    lax.fori_loop(0, K, along_y, tuple((none, none) for _ in range(R)), unroll=True)

    chem[...] = jnp.zeros(chem.shape, F32)
    chem[0:T, 0:T] = chem_ref[...]
    square = (TP, TP)
    across = lax.broadcasted_iota(jnp.int32, square, 1)
    down = lax.broadcasted_iota(jnp.int32, square, 0)
    first_row = jnp.where(across == down, jnp.broadcast_to(chem[0:1, 0:TP], square), 0.0)
    first_rates = jnp.broadcast_to(jnp.sum(first_row, axis=1, keepdims=True), (TP, C))

    rest = TP - SUB
    rates = chem[...]
    rates_high = rates.astype(jnp.bfloat16).astype(F32)
    rates_low = rates - rates_high
    halves = jnp.where(
        lane_t < rest,
        pltpu.roll(rates_high, C - SUB, 1),
        jnp.where(
            lane_t < 2 * rest,
            pltpu.roll(rates_high, (rest + C - SUB) % C, 1),
            pltpu.roll(rates_low, (2 * rest + C - SUB) % C, 1),
        ),
    )[:, 0 : 3 * rest].astype(jnp.bfloat16)

    def late_products(k):
        mixed = jnp.concatenate([mv[k * R + r, SUB:TP] for r in range(R)], axis=1)
        high = mixed.astype(jnp.bfloat16)
        low = (mixed - high.astype(F32)).astype(jnp.bfloat16)
        return jnp.dot(
            halves,
            jnp.concatenate([high, low, high], axis=0),
            preferred_element_type=F32,
        )

    def products(k, first, last):
        return jnp.dot(
            chem[:, first:last],
            jnp.concatenate([mv[k * R + r, first:last] for r in range(R)], axis=1),
            precision=lax.Precision.HIGHEST,
            preferred_element_type=F32,
        )

    for g in range(groups):

        @pl.when(has_lo)
        def _():
            tile_copy(True, g).wait_recv()

        @pl.when(has_hi)
        def _():
            tile_copy(False, g).wait_recv()

        tracers = pl.ds(g * SUB, SUB)

        def along_x(k, carry):
            base = g * SUB * KR + k * R
            depth = lax.convert_element_type(k, F32)
            cells = []
            for r in range(R):
                value = lo[pl.ds(base + r, SUB, stride=KR), :]
                cells.append(jnp.where(depth < below[r : r + 1], value, 0.0))
            for r in range(R):
                cells.append(xs[k * R + r, tracers])
            for r in range(R):
                value = hi[pl.ds(base + r, SUB, stride=KR), :]
                cells.append(jnp.where(depth < above[r : r + 1], value, 0.0))
            diff = [b - a for a, b in zip(cells, cells[1:])]
            flux = []
            for face in range(R + 1):
                if face == 0:
                    c, weight = clow[0, pl.ds(k, 1)], clow[1, pl.ds(k, 1)]
                else:
                    at = pl.ds(k * R + face - 1, 1)
                    c, weight = coef[CX, at], coef[WX, at]
                flux.append(face_flux(c, weight, cells[face + 1], cells[face + 2], *diff[face : face + 3]))
            out = []
            for r in range(R):
                kr = k * R + r
                at = pl.ds(kr, 1)
                moved = mv[kr, tracers] + (flux[r] - flux[r + 1])
                rhs = moved * coef[INV, at] + coef[UINV, at] * carry[r]
                mv[kr, tracers] = rhs
                out.append(rhs)
            return tuple(out)

        zero = jnp.zeros((SUB, C), F32)
        lax.fori_loop(0, K, along_x, (zero,) * R, unroll=True)

        def upward(i, carry):
            k = K - 1 - i
            out = []
            for r in range(R):
                kr = k * R + r
                at = pl.ds(kr, 1)
                solved = mv[kr, tracers] - coef[RATIO, at] * carry[r]
                mv[kr, tracers] = solved
                part = jnp.sum(solved * first_rates[g * SUB : (g + 1) * SUB], axis=0, keepdims=True)
                if g > 0:
                    part = coef[ROW0, at] + part
                if g < groups - 1:
                    coef[ROW0, at] = part
                else:
                    wet = coef[WET, at]
                    value = wet * mv[kr, 0:1] + coef[WG, at] * part
                    coef[ABS, at] = wet * (0.02 + 0.04 * jnp.maximum(value, 0.0))
                out.append(solved)
            return tuple(out)

        lax.fori_loop(0, K, upward, (zero,) * R, unroll=True)

        if g == 0:

            def begin(k, carry):
                early[k] = products(k, 0, SUB)
                return carry

            lax.fori_loop(0, K, begin, 0, unroll=4)

    def shade(k, carry):
        out = []
        for r in range(R):
            at = pl.ds(k * R + r, 1)
            coef[OPT, at] = carry[r]
            out.append(carry[r] + coef[ABS, at])
        return tuple(out)

    lax.fori_loop(0, K, shade, (none,) * R, unroll=True)
    heat = 16.0 * jnp.exp(-coef[OPT]) * (1.0 - jnp.exp(-coef[ABS]))
    if hsend.shape[1] > LR:
        hsend[...] = jnp.zeros(hsend.shape, F32)
    for d in range(n):
        hsend[d, 0:LR] = heat[d * LR : (d + 1) * LR]

    def heat_copy(off):
        to = (me + off) % n
        return pltpu.make_async_remote_copy(
            src_ref=hsend.at[to],
            dst_ref=hrecv.at[me],
            send_sem=h_ssem.at[off],
            recv_sem=h_rsem.at[off],
            device_id={"sect": to},
            device_id_type=MESH,
        )

    for off in range(1, n):
        heat_copy(off).start()
    hrecv[pl.ds(me, 1)] = hsend[pl.ds(me, 1)]

    def react(k, carry):
        reacted = early[k] + late_products(k)
        for r in range(R):
            kr = k * R + r
            at = pl.ds(kr, 1)
            outp[pl.ds(kr, TP, stride=KR), :] = (
                coef[WET, at] * mv[kr] + coef[WG, at] * reacted[:, r * C : (r + 1) * C]
            )
        return carry

    lax.fori_loop(0, K, react, 0, unroll=True)

    for off in range(1, n):
        field_copy(off).wait_send()
    for g in range(groups):

        @pl.when(has_hi)
        def _():
            tile_copy(True, g).wait_send()

        @pl.when(has_lo)
        def _():
            tile_copy(False, g).wait_send()

    @pl.when(has_right)
    def _():
        edge_copy(True).wait_send()
        for off in range(n):
            north_copy(off).wait_send()

    @pl.when(has_left)
    def _():
        edge_copy(False).wait_send()

    for off in range(1, n):
        heat_copy(off).wait_recv()
    for s in range(n):
        for l in range(L):
            heat_ref[l, s * R : (s + 1) * R] = hrecv[s, l * R : (l + 1) * R]
    for off in range(1, n):
        heat_copy(off).wait_send()


def store(adv, heat, adv_hbm, heat_hbm, sem):
    copies = (
        pltpu.make_async_copy(adv.at[pl.ds(0, adv_hbm.shape[0])], adv_hbm, sem.at[0]),
        pltpu.make_async_copy(heat, heat_hbm, sem.at[1]),
    )
    for copy in copies:
        copy.start()
    for copy in copies:
        copy.wait()


def body(sizes, solutes, tally, east, north, kappa, temp, salt, chemistry):
    T, K, R, C, n, ntx, nty = sizes
    KR, LR = K * R, K // n * R
    TP = round_up(T, SUB)
    groups = TP // SUB
    block = round_up(4 * LR + K // n + R, SUB)
    dma = pltpu.SemaphoreType.DMA
    vmem = pl.BlockSpec(memory_space=pltpu.VMEM)
    hbm = pl.BlockSpec(memory_space=pltpu.HBM)
    tile = pltpu.VMEM((TP * KR, C), F32)
    stack = pltpu.VMEM((KR, TP, C), F32)
    advanced, heating = pl.pallas_call(
        functools.partial(kernel, sizes),
        out_shape=(
            pltpu.VMEM((TP * KR, C), F32),
            pltpu.VMEM(east.shape, F32),
        ),
        in_specs=[hbm] * 8,
        out_specs=(vmem, vmem),
        scratch_shapes=[
            pltpu.VMEM(tally.shape, tally.dtype),
            *[pltpu.VMEM(east.shape, F32)] * 5,
            pltpu.VMEM(chemistry.shape, F32),
            tile,
            tile,
            tile,
            stack,
            stack,
            pltpu.VMEM((n, block, C), F32),
            pltpu.VMEM((n, block, C), F32),
            pltpu.VMEM((TP + SUB, C), F32),
            pltpu.VMEM((TP + SUB, C), F32),
            pltpu.VMEM((TP + SUB, C), F32),
            pltpu.VMEM((n, round_up(LR, SUB), C), F32),
            pltpu.VMEM((n, round_up(LR, SUB), C), F32),
            pltpu.VMEM((5, KR, C), F32),
            pltpu.VMEM((round_up(K, SUB), C), F32),
            pltpu.VMEM((17, KR, C), F32),
            pltpu.VMEM((2, round_up(K, SUB), C), F32),
            pltpu.VMEM((5, KR, TP, C), F32),
            pltpu.VMEM((n, round_up(LR, SUB), C), F32),
            pltpu.VMEM((n, round_up(LR, SUB), C), F32),
            pltpu.VMEM((TP, C), F32),
            pltpu.VMEM((K, TP, R * C), F32),
            dma((n,)),
            dma((n,)),
            dma((2, groups)),
            dma((2, groups)),
            dma((2,)),
            dma((2,)),
            dma((n,)),
            dma((n,)),
            dma((n,)),
            dma((n,)),
            dma,
            dma((7,)),
        ],
        compiler_params=pltpu.CompilerParams(
            collective_id=0, has_side_effects=True, vmem_limit_bytes=VMEM_LIMIT
        ),
        name="ocean_step",
    )(solutes.reshape(T * KR, C), tally, east, north, kappa, temp, salt, chemistry)
    advanced, heating = pl.pallas_call(
        store,
        out_shape=(
            jax.ShapeDtypeStruct((T * KR, C), F32),
            jax.ShapeDtypeStruct(east.shape, F32),
        ),
        in_specs=[vmem, vmem],
        out_specs=(hbm, hbm),
        scratch_shapes=[dma((2,))],
        compiler_params=pltpu.CompilerParams(vmem_limit_bytes=1024 * 1024),
        name="store_outputs",
    )(advanced, heating)
    return advanced.reshape(T, K, R, C), heating


def solution(mesh):
    n, ntx, nty = (mesh.shape[axis] for axis in ("sect", "tx", "ty"))
    columns = P("sect", None, ("tx", "ty"))
    in_specs = (
        P(None, None, "sect", ("tx", "ty")),
        P("sect", ("tx", "ty")),
        columns,
        columns,
        columns,
        columns,
        columns,
        P(),
    )
    out_specs = (P(None, None, "sect", ("tx", "ty")), columns)

    def step(solutes, *rest):
        T, K, X, Y = solutes.shape
        R, C = X // n, Y // (ntx * nty)
        assert R == HALO and K % n == 0 and 4 * K * R == C
        sizes = (T, K, R, C, n, ntx, nty)
        return jax.shard_map(
            functools.partial(body, sizes),
            mesh=mesh,
            in_specs=in_specs,
            out_specs=out_specs,
            check_vma=False,
        )(solutes, *rest)

    return step
```

```python
import functools

import jax
import jax.numpy as jnp
from jax import lax
from jax.experimental import pallas as pl
from jax.experimental.pallas import tpu as pltpu
from jax.sharding import PartitionSpec as P

MESH = pl.DeviceIdType.MESH
SUB = 8
HALO = 2
F32 = jnp.float32
VMEM_LIMIT = 60 * 1024 * 1024


def round_up(value, unit):
    return -(-value // unit) * unit


def limited(first, second):
    return jnp.maximum(jnp.minimum(first, second), 0.0) + jnp.minimum(
        jnp.maximum(first, second), 0.0
    )


def face_flux(c, weight, near_low, near_high, low, mid, high):
    up = c >= 0
    base = jnp.where(up, near_low, near_high)
    return c * base + weight * limited(mid, jnp.where(up, low, high))


def limiter_weight(c):
    size = jnp.abs(c)
    return 0.5 * size * (1.0 - size)


def kernel(
    sizes,
    sol_hbm,
    tally_hbm,
    east_hbm,
    north_hbm,
    kappa_hbm,
    temp_hbm,
    salt_hbm,
    chem_hbm,
    outp,
    heat_ref,
    tally_ref,
    east_ref,
    north_ref,
    kappa_ref,
    temp_ref,
    salt_ref,
    chem_ref,
    own,
    lo,
    hi,
    xs,
    mv,
    fsend,
    frecv,
    ysend,
    yleft,
    yright,
    csend,
    cleft,
    fld,
    elow,
    coef,
    clow,
    flp,
    hsend,
    hrecv,
    chem,
    early,
    f_ssem,
    f_rsem,
    z_ssem,
    z_rsem,
    y_ssem,
    y_rsem,
    c_ssem,
    c_rsem,
    h_ssem,
    h_rsem,
    own_sem,
    in_sem,
):
    T, K, R, C, n, ntx, nty = sizes
    L = K // n
    LR = L * R
    KR = K * R
    TP = round_up(T, SUB)
    groups = TP // SUB
    me = lax.axis_index("sect")
    tx = lax.axis_index("tx")
    ty = lax.axis_index("ty")
    flat = tx * nty + ty
    has_lo = me > 0
    has_hi = me < n - 1
    has_left = flat > 0
    has_right = flat < ntx * nty - 1
    left = {"tx": (flat + ntx * nty - 1) % (ntx * nty) // nty, "ty": (flat + ntx * nty - 1) % nty}
    right = {"tx": (flat + 1) % (ntx * nty) // nty, "ty": (flat + 1) % nty}

    pairs = (
        (tally_hbm, tally_ref),
        (east_hbm, east_ref),
        (north_hbm, north_ref),
        (kappa_hbm, kappa_ref),
        (temp_hbm, temp_ref),
        (salt_hbm, salt_ref),
        (chem_hbm, chem_ref),
    )
    fetches = [pltpu.make_async_copy(a, b, in_sem.at[i]) for i, (a, b) in enumerate(pairs)]
    for fetch in fetches:
        fetch.start()
    own_copy = pltpu.make_async_copy(sol_hbm, own.at[pl.ds(0, T * KR)], own_sem)
    own_copy.start()

    barrier = pltpu.get_barrier_semaphore()
    for off in range(1, n):
        pl.semaphore_signal(
            barrier, inc=1, device_id={"sect": (me + off) % n}, device_id_type=MESH
        )

    @pl.when(has_left)
    def _():
        pl.semaphore_signal(barrier, inc=1, device_id=left, device_id_type=MESH)

    @pl.when(has_right)
    def _():
        pl.semaphore_signal(barrier, inc=1, device_id=right, device_id_type=MESH)

    pl.semaphore_wait(
        barrier, n - 1 + has_left.astype(jnp.int32) + has_right.astype(jnp.int32)
    )

    def tile_copy(up, g):
        rows = pl.ds(g * SUB * KR, (min((g + 1) * SUB, T) - g * SUB) * KR)
        return pltpu.make_async_remote_copy(
            src_ref=sol_hbm.at[rows],
            dst_ref=(lo if up else hi).at[rows],
            send_sem=z_ssem.at[int(up), g],
            recv_sem=z_rsem.at[int(up), g],
            device_id={"sect": (me + 1) % n if up else (me + n - 1) % n},
            device_id_type=MESH,
        )

    def send_tiles(g):
        @pl.when(has_hi)
        def _():
            tile_copy(True, g).start()

        @pl.when(has_lo)
        def _():
            tile_copy(False, g).start()

    for fetch in fetches:
        fetch.wait()

    growth = jnp.exp(0.0633 * (temp_ref[...] - 15.0)) * (1.0 + 0.25 * (salt_ref[...] - 35.0))
    tally = tally_ref[...].astype(F32)
    used = 4 * LR + L + R
    block_rows = fsend.shape[1]
    fsend[...] = jnp.zeros(fsend.shape, F32)
    for d in range(n):
        for l in range(L):
            at = l * R
            rows = slice(d * R, (d + 1) * R)
            fsend[d, at : at + R] = east_ref[l, rows]
            fsend[d, LR + at : LR + at + R] = north_ref[l, rows]
            fsend[d, 2 * LR + at : 2 * LR + at + R] = kappa_ref[l, rows]
            fsend[d, 3 * LR + at : 3 * LR + at + R] = growth[l, d * R : (d + 1) * R]
            if d > 0:
                fsend[d, 4 * LR + l : 4 * LR + l + 1] = east_ref[l, d * R - 1 : d * R]
        fsend[d, used - R : used] = tally

    def field_copy(off):
        to = (me + off) % n
        return pltpu.make_async_remote_copy(
            src_ref=fsend.at[to],
            dst_ref=frecv.at[me],
            send_sem=f_ssem.at[off],
            recv_sem=f_rsem.at[off],
            device_id={"sect": to},
            device_id_type=MESH,
        )

    for off in range(1, n):
        field_copy(off).start()

    send_tiles(0)

    frecv[pl.ds(me, 1)] = fsend[pl.ds(me, 1)]

    for buf in (own, lo, hi):
        if TP > T:
            buf[T * KR :] = jnp.zeros(((TP - T) * KR, C), F32)

    lane_t = lax.broadcasted_iota(jnp.int32, (TP, C), 1)
    tal_row = [tally[r : r + 1] for r in range(R)]
    own_copy.wait()

    def pack(k, packed):
        for r in range(R):
            kr = k * R + r
            wet = lax.convert_element_type(k, F32) < tal_row[r]
            cells = jnp.where(wet, own[pl.ds(kr, TP, stride=KR), :], 0.0)
            xs[kr] = cells
            moved_edge = pltpu.roll(cells, HALO + 4 * kr, 1)
            packed = jnp.where(jnp.right_shift(lane_t, 2) == kr, moved_edge, packed)
        return packed

    packed_own = lax.fori_loop(0, K, pack, jnp.zeros((TP, C), F32), unroll=True)
    ysend[0:TP] = packed_own
    ysend[TP:] = jnp.zeros((SUB, C), F32)
    ysend[TP : TP + R] = tally

    def edge_copy(to_right):
        return pltpu.make_async_remote_copy(
            src_ref=ysend,
            dst_ref=yleft if to_right else yright,
            send_sem=y_ssem.at[int(to_right)],
            recv_sem=y_rsem.at[int(to_right)],
            device_id=right if to_right else left,
            device_id_type=MESH,
        )

    def north_copy():
        return pltpu.make_async_remote_copy(
            src_ref=csend,
            dst_ref=cleft,
            send_sem=c_ssem,
            recv_sem=c_rsem,
            device_id=right,
            device_id_type=MESH,
        )

    @pl.when(has_right)
    def _():
        edge_copy(True).start()

    @pl.when(has_left)
    def _():
        edge_copy(False).start()

    for off in range(1, n):
        field_copy(off).wait_recv()
    for s in range(n):
        for f in range(4):
            fld[f, s * LR : (s + 1) * LR] = frecv[s, f * LR : (f + 1) * LR]
        elow[s * L : (s + 1) * L] = frecv[s, 4 * LR : 4 * LR + L]

    row = lax.broadcasted_iota(jnp.int32, (KR, C), 0)
    lane = lax.broadcasted_iota(jnp.int32, (KR, C), 1)
    level = jnp.right_shift(row, 1).astype(F32)
    odd = jnp.bitwise_and(row, 1) == 1
    north = fld[1]
    edge_c = jnp.where(jnp.right_shift(lane, 2) == row, north[:, C - 1 : C], 0.0)
    csend[...] = jnp.broadcast_to(jnp.sum(edge_c, axis=0, keepdims=True), (SUB, C))

    @pl.when(has_right)
    def _():
        north_copy().start()

    if groups > 1:
        send_tiles(1)

    below = frecv[lax.rem(me + n - 1, n), used - R : used]
    above = frecv[lax.rem(me + 1, n), used - R : used]
    below = jnp.where(has_lo, below, 0.0)
    above = jnp.where(has_hi, above, 0.0)
    tal = jnp.where(odd, tal_row[1], tal_row[0])
    tal_next = jnp.where(odd, above[0:1], tal_row[1])
    CX, WX, CY, WY, INV, UINV, RATIO, COUP, WET, WG, ABS, OPT, ROW0 = range(13)
    c_x = jnp.where(level < jnp.minimum(tal, tal_next), fld[0], 0.0)
    coef[CX] = c_x
    coef[WX] = limiter_weight(c_x)
    level_k = lax.broadcasted_iota(jnp.int32, (K, C), 0).astype(F32)
    c_low = jnp.where(level_k < jnp.minimum(below[R - 1 : R], tal_row[0]), elow[0:K], 0.0)
    clow[0] = c_low
    clow[1] = limiter_weight(c_low)
    wet_all = (level < tal).astype(F32)
    coef[WET] = wet_all
    coef[WG] = wet_all * (0.2 * fld[3])
    coef[COUP] = jnp.where(level + 1.0 < tal, fld[2], 0.0)

    def eliminate(k, carry):
        out = []
        for r in range(R):
            ratio, above_link = carry[r]
            at = pl.ds(k * R + r, 1)
            link = coef[COUP, at]
            inverse = 1.0 / (1.0 + above_link + link + above_link * ratio)
            ratio = -link * inverse
            coef[INV, at] = inverse
            coef[UINV, at] = above_link * inverse
            coef[RATIO, at] = ratio
            out.append((ratio, link))
        return tuple(out)

    none = jnp.zeros((1, C), F32)
    lax.fori_loop(0, K, eliminate, tuple((none, none) for _ in range(R)), unroll=True)

    @pl.when(has_left)
    def _():
        edge_copy(True).wait_recv()

    @pl.when(has_right)
    def _():
        edge_copy(False).wait_recv()

    for g in range(2, groups):
        send_tiles(g)

    left_cols = jnp.where(has_left, yleft[0:TP], 0.0)
    right_cols = jnp.where(has_right, yright[0:TP], 0.0)
    tal_left = jnp.where(has_left, yleft[TP : TP + R], 0.0)
    tal_right = jnp.where(has_right, yright[TP : TP + R], 0.0)
    tal_far = jnp.where(odd, tal_right[1:2], tal_right[0:1])
    tal_east = pltpu.roll(jnp.where(lane == 0, tal_far, tal), C - 1, 1)
    c_y = jnp.where(level < jnp.minimum(tal, tal_east), north, 0.0)
    coef[CY] = c_y
    coef[WY] = limiter_weight(c_y)

    part = jnp.bitwise_and(lane_t, 3)
    packed_own = ysend[0:TP]
    edges = jnp.where(part < HALO, left_cols, right_cols)
    around = jnp.where(part < HALO, left_cols, packed_own)

    @pl.when(has_left)
    def _():
        north_copy().wait_recv()

    wide = (SUB, C)
    lane_8 = lax.broadcasted_iota(jnp.int32, wide, 1)
    shut = []
    for r in range(R):
        before = pltpu.roll(jnp.broadcast_to(tal_left[r : r + 1], wide), 1, 1)
        both = jnp.minimum(before, jnp.broadcast_to(tal_row[r], wide))
        shut.append(jnp.broadcast_to(both[:, 0:1], wide))
    tal_edge = jnp.where(jnp.bitwise_and(jnp.right_shift(lane_8, 2), 1) == 1, shut[1], shut[0])
    level_8 = jnp.right_shift(lane_8, 3).astype(F32)
    c_edge = jnp.where(level_8 < tal_edge, cleft[...], 0.0)[0:1]
    nxt = pltpu.roll(around, C - 1, 1)
    nxt2 = pltpu.roll(around, C - 2, 1)
    prv = pltpu.roll(around, 1, 1)
    flp[...] = face_flux(
        c_edge, limiter_weight(c_edge), around, nxt, around - prv, nxt - around, nxt2 - nxt
    )

    def along_y(k, carry):
        for r in range(R):
            kr = k * R + r
            at = pl.ds(kr, 1)
            cells = xs[kr]
            side = pltpu.roll(edges, C - HALO - 4 * kr, 1)
            prv = pltpu.roll(jnp.where(lane_t == C - 1, side, cells), 1, 1)
            nxt = pltpu.roll(jnp.where(lane_t == 0, side, cells), C - 1, 1)
            nxt2 = pltpu.roll(jnp.where(lane_t < HALO, side, cells), C - HALO, 1)
            flux = face_flux(
                coef[CY, at], coef[WY, at], cells, nxt, cells - prv, nxt - cells, nxt2 - nxt
            )
            first = pltpu.roll(flp[...], C - 1 - 4 * kr, 1)
            lower = jnp.where(lane_t == 0, first, pltpu.roll(flux, 1, 1))
            mv[kr] = cells + (lower - flux)
        return carry

    lax.fori_loop(0, K, along_y, 0, unroll=4)

    chem[...] = jnp.zeros(chem.shape, F32)
    chem[0:T, 0:T] = chem_ref[...]
    square = (TP, TP)
    across = lax.broadcasted_iota(jnp.int32, square, 1)
    down = lax.broadcasted_iota(jnp.int32, square, 0)
    first_row = jnp.where(across == down, jnp.broadcast_to(chem[0:1, 0:TP], square), 0.0)
    first_rates = jnp.broadcast_to(jnp.sum(first_row, axis=1, keepdims=True), (TP, C))

    rest = TP - SUB
    rates = chem[...]
    rates_high = rates.astype(jnp.bfloat16).astype(F32)
    rates_low = rates - rates_high
    halves = jnp.where(
        lane_t < rest,
        pltpu.roll(rates_high, C - SUB, 1),
        jnp.where(
            lane_t < 2 * rest,
            pltpu.roll(rates_high, (rest + C - SUB) % C, 1),
            pltpu.roll(rates_low, (2 * rest + C - SUB) % C, 1),
        ),
    )[:, 0 : 3 * rest].astype(jnp.bfloat16)

    def late_products(k):
        mixed = jnp.concatenate([mv[k * R + r, SUB:TP] for r in range(R)], axis=1)
        high = mixed.astype(jnp.bfloat16)
        low = (mixed - high.astype(F32)).astype(jnp.bfloat16)
        return jnp.dot(
            halves,
            jnp.concatenate([high, low, high], axis=0),
            preferred_element_type=F32,
        )

    def products(k, first, last):
        return jnp.dot(
            chem[:, first:last],
            jnp.concatenate([mv[k * R + r, first:last] for r in range(R)], axis=1),
            precision=lax.Precision.HIGHEST,
            preferred_element_type=F32,
        )

    for g in range(groups):

        @pl.when(has_lo)
        def _():
            tile_copy(True, g).wait_recv()

        @pl.when(has_hi)
        def _():
            tile_copy(False, g).wait_recv()

        tracers = pl.ds(g * SUB, SUB)

        def along_x(k, carry):
            base = g * SUB * KR + k * R
            depth = lax.convert_element_type(k, F32)
            cells = []
            for r in range(R):
                value = lo[pl.ds(base + r, SUB, stride=KR), :]
                cells.append(jnp.where(depth < below[r : r + 1], value, 0.0))
            for r in range(R):
                cells.append(xs[k * R + r, tracers])
            for r in range(R):
                value = hi[pl.ds(base + r, SUB, stride=KR), :]
                cells.append(jnp.where(depth < above[r : r + 1], value, 0.0))
            diff = [b - a for a, b in zip(cells, cells[1:])]
            flux = []
            for face in range(R + 1):
                if face == 0:
                    c, weight = clow[0, pl.ds(k, 1)], clow[1, pl.ds(k, 1)]
                else:
                    at = pl.ds(k * R + face - 1, 1)
                    c, weight = coef[CX, at], coef[WX, at]
                flux.append(face_flux(c, weight, cells[face + 1], cells[face + 2], *diff[face : face + 3]))
            out = []
            for r in range(R):
                kr = k * R + r
                at = pl.ds(kr, 1)
                moved = mv[kr, tracers] + (flux[r] - flux[r + 1])
                rhs = moved * coef[INV, at] + coef[UINV, at] * carry[r]
                mv[kr, tracers] = rhs
                out.append(rhs)
            return tuple(out)

        zero = jnp.zeros((SUB, C), F32)
        lax.fori_loop(0, K, along_x, (zero,) * R, unroll=True)

        def upward(i, carry):
            k = K - 1 - i
            out = []
            for r in range(R):
                kr = k * R + r
                at = pl.ds(kr, 1)
                solved = mv[kr, tracers] - coef[RATIO, at] * carry[r]
                mv[kr, tracers] = solved
                part = jnp.sum(solved * first_rates[g * SUB : (g + 1) * SUB], axis=0, keepdims=True)
                if g > 0:
                    part = coef[ROW0, at] + part
                if g < groups - 1:
                    coef[ROW0, at] = part
                else:
                    wet = coef[WET, at]
                    value = wet * mv[kr, 0:1] + coef[WG, at] * part
                    coef[ABS, at] = wet * (0.02 + 0.04 * jnp.maximum(value, 0.0))
                out.append(solved)
            return tuple(out)

        lax.fori_loop(0, K, upward, (zero,) * R, unroll=True)

        if g == 0:

            def begin(k, carry):
                early[k] = products(k, 0, SUB)
                return carry

            lax.fori_loop(0, K, begin, 0, unroll=4)

    def shade(k, carry):
        out = []
        for r in range(R):
            at = pl.ds(k * R + r, 1)
            coef[OPT, at] = carry[r]
            out.append(carry[r] + coef[ABS, at])
        return tuple(out)

    lax.fori_loop(0, K, shade, (none,) * R, unroll=True)
    heat = 16.0 * jnp.exp(-coef[OPT]) * (1.0 - jnp.exp(-coef[ABS]))
    if hsend.shape[1] > LR:
        hsend[...] = jnp.zeros(hsend.shape, F32)
    for d in range(n):
        hsend[d, 0:LR] = heat[d * LR : (d + 1) * LR]

    def heat_copy(off):
        to = (me + off) % n
        return pltpu.make_async_remote_copy(
            src_ref=hsend.at[to],
            dst_ref=hrecv.at[me],
            send_sem=h_ssem.at[off],
            recv_sem=h_rsem.at[off],
            device_id={"sect": to},
            device_id_type=MESH,
        )

    for off in range(1, n):
        heat_copy(off).start()
    hrecv[pl.ds(me, 1)] = hsend[pl.ds(me, 1)]

    def react(k, carry):
        reacted = early[k] + late_products(k)
        for r in range(R):
            kr = k * R + r
            at = pl.ds(kr, 1)
            outp[pl.ds(kr, TP, stride=KR), :] = (
                coef[WET, at] * mv[kr] + coef[WG, at] * reacted[:, r * C : (r + 1) * C]
            )
        return carry

    lax.fori_loop(0, K, react, 0, unroll=True)

    for off in range(1, n):
        field_copy(off).wait_send()
    for g in range(groups):

        @pl.when(has_hi)
        def _():
            tile_copy(True, g).wait_send()

        @pl.when(has_lo)
        def _():
            tile_copy(False, g).wait_send()

    @pl.when(has_right)
    def _():
        edge_copy(True).wait_send()
        north_copy().wait_send()

    @pl.when(has_left)
    def _():
        edge_copy(False).wait_send()

    for off in range(1, n):
        heat_copy(off).wait_recv()
    for s in range(n):
        for l in range(L):
            heat_ref[l, s * R : (s + 1) * R] = hrecv[s, l * R : (l + 1) * R]
    for off in range(1, n):
        heat_copy(off).wait_send()


def store(adv, heat, adv_hbm, heat_hbm, sem):
    copies = (
        pltpu.make_async_copy(adv.at[pl.ds(0, adv_hbm.shape[0])], adv_hbm, sem.at[0]),
        pltpu.make_async_copy(heat, heat_hbm, sem.at[1]),
    )
    for copy in copies:
        copy.start()
    for copy in copies:
        copy.wait()


def body(sizes, solutes, tally, east, north, kappa, temp, salt, chemistry):
    T, K, R, C, n, ntx, nty = sizes
    KR, LR = K * R, K // n * R
    TP = round_up(T, SUB)
    groups = TP // SUB
    block = round_up(4 * LR + K // n + R, SUB)
    dma = pltpu.SemaphoreType.DMA
    vmem = pl.BlockSpec(memory_space=pltpu.VMEM)
    hbm = pl.BlockSpec(memory_space=pltpu.HBM)
    tile = pltpu.VMEM((TP * KR, C), F32)
    stack = pltpu.VMEM((KR, TP, C), F32)
    advanced, heating = pl.pallas_call(
        functools.partial(kernel, sizes),
        out_shape=(
            pltpu.VMEM((TP * KR, C), F32),
            pltpu.VMEM(east.shape, F32),
        ),
        in_specs=[hbm] * 8,
        out_specs=(vmem, vmem),
        scratch_shapes=[
            pltpu.VMEM(tally.shape, tally.dtype),
            *[pltpu.VMEM(east.shape, F32)] * 5,
            pltpu.VMEM(chemistry.shape, F32),
            tile,
            tile,
            tile,
            stack,
            stack,
            pltpu.VMEM((n, block, C), F32),
            pltpu.VMEM((n, block, C), F32),
            pltpu.VMEM((TP + SUB, C), F32),
            pltpu.VMEM((TP + SUB, C), F32),
            pltpu.VMEM((TP + SUB, C), F32),
            pltpu.VMEM((SUB, C), F32),
            pltpu.VMEM((SUB, C), F32),
            pltpu.VMEM((4, KR, C), F32),
            pltpu.VMEM((round_up(K, SUB), C), F32),
            pltpu.VMEM((13, KR, C), F32),
            pltpu.VMEM((2, round_up(K, SUB), C), F32),
            pltpu.VMEM((TP, C), F32),
            pltpu.VMEM((n, round_up(LR, SUB), C), F32),
            pltpu.VMEM((n, round_up(LR, SUB), C), F32),
            pltpu.VMEM((TP, C), F32),
            pltpu.VMEM((K, TP, R * C), F32),
            dma((n,)),
            dma((n,)),
            dma((2, groups)),
            dma((2, groups)),
            dma((2,)),
            dma((2,)),
            dma,
            dma,
            dma((n,)),
            dma((n,)),
            dma,
            dma((7,)),
        ],
        compiler_params=pltpu.CompilerParams(
            collective_id=0, has_side_effects=True, vmem_limit_bytes=VMEM_LIMIT
        ),
        name="ocean_step",
    )(solutes.reshape(T * KR, C), tally, east, north, kappa, temp, salt, chemistry)
    advanced, heating = pl.pallas_call(
        store,
        out_shape=(
            jax.ShapeDtypeStruct((T * KR, C), F32),
            jax.ShapeDtypeStruct(east.shape, F32),
        ),
        in_specs=[vmem, vmem],
        out_specs=(hbm, hbm),
        scratch_shapes=[dma((2,))],
        compiler_params=pltpu.CompilerParams(vmem_limit_bytes=1024 * 1024),
        name="store_outputs",
    )(advanced, heating)
    return advanced.reshape(T, K, R, C), heating


def solution(mesh):
    n, ntx, nty = (mesh.shape[axis] for axis in ("sect", "tx", "ty"))
    columns = P("sect", None, ("tx", "ty"))
    in_specs = (
        P(None, None, "sect", ("tx", "ty")),
        P("sect", ("tx", "ty")),
        columns,
        columns,
        columns,
        columns,
        columns,
        P(),
    )
    out_specs = (P(None, None, "sect", ("tx", "ty")), columns)

    def step(solutes, *rest):
        T, K, X, Y = solutes.shape
        R, C = X // n, Y // (ntx * nty)
        assert R == HALO and K % n == 0 and 4 * K * R == C
        sizes = (T, K, R, C, n, ntx, nty)
        return jax.shard_map(
            functools.partial(body, sizes),
            mesh=mesh,
            in_specs=in_specs,
            out_specs=out_specs,
            check_vma=False,
        )(solutes, *rest)

    return step
```

```python
import functools

import jax
import jax.numpy as jnp
from jax import lax
from jax.experimental import pallas as pl
from jax.experimental.pallas import tpu as pltpu
from jax.sharding import PartitionSpec as P

MESH = pl.DeviceIdType.MESH
SUB = 8
HALO = 2
F32 = jnp.float32
VMEM_LIMIT = 60 * 1024 * 1024


def round_up(value, unit):
    return -(-value // unit) * unit


def limited(first, second):
    return jnp.maximum(jnp.minimum(first, second), 0.0) + jnp.minimum(
        jnp.maximum(first, second), 0.0
    )


def face_flux(c, weight, near_low, near_high, low, mid, high):
    up = c >= 0
    base = jnp.where(up, near_low, near_high)
    return c * base + weight * limited(mid, jnp.where(up, low, high))


def limiter_weight(c):
    size = jnp.abs(c)
    return 0.5 * size * (1.0 - size)


def kernel(
    sizes,
    sol_hbm,
    tally_hbm,
    east_hbm,
    north_hbm,
    kappa_hbm,
    temp_hbm,
    salt_hbm,
    chem_hbm,
    outp,
    heat_ref,
    tally_ref,
    east_ref,
    north_ref,
    kappa_ref,
    temp_ref,
    salt_ref,
    chem_ref,
    own,
    lo,
    hi,
    xs,
    mv,
    fsend,
    frecv,
    ysend,
    yleft,
    yright,
    csend,
    cleft,
    fld,
    elow,
    coef,
    clow,
    flp,
    hsend,
    hrecv,
    chem,
    f_ssem,
    f_rsem,
    z_ssem,
    z_rsem,
    y_ssem,
    y_rsem,
    c_ssem,
    c_rsem,
    h_ssem,
    h_rsem,
    own_sem,
    in_sem,
):
    T, K, R, C, n, ntx, nty = sizes
    L = K // n
    LR = L * R
    KR = K * R
    TP = round_up(T, SUB)
    groups = TP // SUB
    me = lax.axis_index("sect")
    tx = lax.axis_index("tx")
    ty = lax.axis_index("ty")
    flat = tx * nty + ty
    has_lo = me > 0
    has_hi = me < n - 1
    has_left = flat > 0
    has_right = flat < ntx * nty - 1
    left = {"tx": (flat + ntx * nty - 1) % (ntx * nty) // nty, "ty": (flat + ntx * nty - 1) % nty}
    right = {"tx": (flat + 1) % (ntx * nty) // nty, "ty": (flat + 1) % nty}

    pairs = (
        (tally_hbm, tally_ref),
        (east_hbm, east_ref),
        (north_hbm, north_ref),
        (kappa_hbm, kappa_ref),
        (temp_hbm, temp_ref),
        (salt_hbm, salt_ref),
        (chem_hbm, chem_ref),
    )
    fetches = [pltpu.make_async_copy(a, b, in_sem.at[i]) for i, (a, b) in enumerate(pairs)]
    for fetch in fetches:
        fetch.start()
    own_copy = pltpu.make_async_copy(sol_hbm, own.at[pl.ds(0, T * KR)], own_sem)
    own_copy.start()

    barrier = pltpu.get_barrier_semaphore()
    for off in range(1, n):
        pl.semaphore_signal(
            barrier, inc=1, device_id={"sect": (me + off) % n}, device_id_type=MESH
        )

    @pl.when(has_left)
    def _():
        pl.semaphore_signal(barrier, inc=1, device_id=left, device_id_type=MESH)

    @pl.when(has_right)
    def _():
        pl.semaphore_signal(barrier, inc=1, device_id=right, device_id_type=MESH)

    pl.semaphore_wait(
        barrier, n - 1 + has_left.astype(jnp.int32) + has_right.astype(jnp.int32)
    )

    def tile_copy(up, g):
        rows = pl.ds(g * SUB * KR, (min((g + 1) * SUB, T) - g * SUB) * KR)
        return pltpu.make_async_remote_copy(
            src_ref=sol_hbm.at[rows],
            dst_ref=(lo if up else hi).at[rows],
            send_sem=z_ssem.at[int(up), g],
            recv_sem=z_rsem.at[int(up), g],
            device_id={"sect": (me + 1) % n if up else (me + n - 1) % n},
            device_id_type=MESH,
        )

    def send_tiles(g):
        @pl.when(has_hi)
        def _():
            tile_copy(True, g).start()

        @pl.when(has_lo)
        def _():
            tile_copy(False, g).start()

    for fetch in fetches:
        fetch.wait()

    growth = jnp.exp(0.0633 * (temp_ref[...] - 15.0)) * (1.0 + 0.25 * (salt_ref[...] - 35.0))
    tally = tally_ref[...].astype(F32)
    used = 4 * LR + L + R
    block_rows = fsend.shape[1]
    fsend[...] = jnp.zeros(fsend.shape, F32)
    for d in range(n):
        for l in range(L):
            at = l * R
            rows = slice(d * R, (d + 1) * R)
            fsend[d, at : at + R] = east_ref[l, rows]
            fsend[d, LR + at : LR + at + R] = north_ref[l, rows]
            fsend[d, 2 * LR + at : 2 * LR + at + R] = kappa_ref[l, rows]
            fsend[d, 3 * LR + at : 3 * LR + at + R] = growth[l, d * R : (d + 1) * R]
            if d > 0:
                fsend[d, 4 * LR + l : 4 * LR + l + 1] = east_ref[l, d * R - 1 : d * R]
        fsend[d, used - R : used] = tally

    def field_copy(off):
        to = (me + off) % n
        return pltpu.make_async_remote_copy(
            src_ref=fsend.at[to],
            dst_ref=frecv.at[me],
            send_sem=f_ssem.at[off],
            recv_sem=f_rsem.at[off],
            device_id={"sect": to},
            device_id_type=MESH,
        )

    for off in range(1, n):
        field_copy(off).start()

    for g in range(groups):
        send_tiles(g)

    frecv[pl.ds(me, 1)] = fsend[pl.ds(me, 1)]

    for buf in (own, lo, hi):
        if TP > T:
            buf[T * KR :] = jnp.zeros(((TP - T) * KR, C), F32)

    lane_t = lax.broadcasted_iota(jnp.int32, (TP, C), 1)
    tal_row = [tally[r : r + 1] for r in range(R)]
    own_copy.wait()

    def pack(k, packed):
        for r in range(R):
            kr = k * R + r
            wet = lax.convert_element_type(k, F32) < tal_row[r]
            cells = jnp.where(wet, own[pl.ds(kr, TP, stride=KR), :], 0.0)
            xs[kr] = cells
            moved_edge = pltpu.roll(cells, HALO + 4 * kr, 1)
            packed = jnp.where(jnp.right_shift(lane_t, 2) == kr, moved_edge, packed)
        return packed

    packed_own = lax.fori_loop(0, K, pack, jnp.zeros((TP, C), F32), unroll=True)
    ysend[0:TP] = packed_own
    ysend[TP:] = jnp.zeros((SUB, C), F32)
    ysend[TP : TP + R] = tally

    def edge_copy(to_right):
        return pltpu.make_async_remote_copy(
            src_ref=ysend,
            dst_ref=yleft if to_right else yright,
            send_sem=y_ssem.at[int(to_right)],
            recv_sem=y_rsem.at[int(to_right)],
            device_id=right if to_right else left,
            device_id_type=MESH,
        )

    def north_copy():
        return pltpu.make_async_remote_copy(
            src_ref=csend,
            dst_ref=cleft,
            send_sem=c_ssem,
            recv_sem=c_rsem,
            device_id=right,
            device_id_type=MESH,
        )

    @pl.when(has_right)
    def _():
        edge_copy(True).start()

    @pl.when(has_left)
    def _():
        edge_copy(False).start()

    for off in range(1, n):
        field_copy(off).wait_recv()
    for s in range(n):
        for f in range(4):
            fld[f, s * LR : (s + 1) * LR] = frecv[s, f * LR : (f + 1) * LR]
        elow[s * L : (s + 1) * L] = frecv[s, 4 * LR : 4 * LR + L]

    row = lax.broadcasted_iota(jnp.int32, (KR, C), 0)
    lane = lax.broadcasted_iota(jnp.int32, (KR, C), 1)
    level = jnp.right_shift(row, 1).astype(F32)
    odd = jnp.bitwise_and(row, 1) == 1
    north = fld[1]
    edge_c = jnp.where(jnp.right_shift(lane, 2) == row, north[:, C - 1 : C], 0.0)
    csend[...] = jnp.broadcast_to(jnp.sum(edge_c, axis=0, keepdims=True), (SUB, C))

    @pl.when(has_right)
    def _():
        north_copy().start()

    below = frecv[lax.rem(me + n - 1, n), used - R : used]
    above = frecv[lax.rem(me + 1, n), used - R : used]
    below = jnp.where(has_lo, below, 0.0)
    above = jnp.where(has_hi, above, 0.0)
    tal = jnp.where(odd, tal_row[1], tal_row[0])
    tal_next = jnp.where(odd, above[0:1], tal_row[1])
    CX, WX, CY, WY, INV, UINV, RATIO, COUP, WET, WG, ABS, OPT, ROW0 = range(13)
    c_x = jnp.where(level < jnp.minimum(tal, tal_next), fld[0], 0.0)
    coef[CX] = c_x
    coef[WX] = limiter_weight(c_x)
    level_k = lax.broadcasted_iota(jnp.int32, (K, C), 0).astype(F32)
    c_low = jnp.where(level_k < jnp.minimum(below[R - 1 : R], tal_row[0]), elow[0:K], 0.0)
    clow[0] = c_low
    clow[1] = limiter_weight(c_low)
    wet_all = (level < tal).astype(F32)
    coef[WET] = wet_all
    coef[WG] = wet_all * (0.2 * fld[3])
    coef[COUP] = jnp.where(level + 1.0 < tal, fld[2], 0.0)

    @pl.when(has_left)
    def _():
        edge_copy(True).wait_recv()

    @pl.when(has_right)
    def _():
        edge_copy(False).wait_recv()

    left_cols = jnp.where(has_left, yleft[0:TP], 0.0)
    right_cols = jnp.where(has_right, yright[0:TP], 0.0)
    tal_left = jnp.where(has_left, yleft[TP : TP + R], 0.0)
    tal_right = jnp.where(has_right, yright[TP : TP + R], 0.0)
    tal_far = jnp.where(odd, tal_right[1:2], tal_right[0:1])
    tal_east = pltpu.roll(jnp.where(lane == 0, tal_far, tal), C - 1, 1)
    c_y = jnp.where(level < jnp.minimum(tal, tal_east), north, 0.0)
    coef[CY] = c_y
    coef[WY] = limiter_weight(c_y)

    part = jnp.bitwise_and(lane_t, 3)
    packed_own = ysend[0:TP]
    edges = jnp.where(part < HALO, left_cols, right_cols)
    around = jnp.where(part < HALO, left_cols, packed_own)

    @pl.when(has_left)
    def _():
        north_copy().wait_recv()

    wide = (SUB, C)
    lane_8 = lax.broadcasted_iota(jnp.int32, wide, 1)
    shut = []
    for r in range(R):
        before = pltpu.roll(jnp.broadcast_to(tal_left[r : r + 1], wide), 1, 1)
        both = jnp.minimum(before, jnp.broadcast_to(tal_row[r], wide))
        shut.append(jnp.broadcast_to(both[:, 0:1], wide))
    tal_edge = jnp.where(jnp.bitwise_and(jnp.right_shift(lane_8, 2), 1) == 1, shut[1], shut[0])
    level_8 = jnp.right_shift(lane_8, 3).astype(F32)
    c_edge = jnp.where(level_8 < tal_edge, cleft[...], 0.0)[0:1]
    nxt = pltpu.roll(around, C - 1, 1)
    nxt2 = pltpu.roll(around, C - 2, 1)
    prv = pltpu.roll(around, 1, 1)
    flp[...] = face_flux(
        c_edge, limiter_weight(c_edge), around, nxt, around - prv, nxt - around, nxt2 - nxt
    )

    def along_y(k, carry):
        out = []
        for r in range(R):
            ratio, above_link = carry[r]
            kr = k * R + r
            at = pl.ds(kr, 1)
            link = coef[COUP, at]
            inverse = 1.0 / (1.0 + above_link + link + above_link * ratio)
            ratio = -link * inverse
            coef[INV, at] = inverse
            coef[UINV, at] = above_link * inverse
            coef[RATIO, at] = ratio
            out.append((ratio, link))
            cells = xs[kr]
            side = pltpu.roll(edges, C - HALO - 4 * kr, 1)
            prv = pltpu.roll(jnp.where(lane_t == C - 1, side, cells), 1, 1)
            nxt = pltpu.roll(jnp.where(lane_t == 0, side, cells), C - 1, 1)
            nxt2 = pltpu.roll(jnp.where(lane_t < HALO, side, cells), C - HALO, 1)
            flux = face_flux(
                coef[CY, at], coef[WY, at], cells, nxt, cells - prv, nxt - cells, nxt2 - nxt
            )
            first = pltpu.roll(flp[...], C - 1 - 4 * kr, 1)
            lower = jnp.where(lane_t == 0, first, pltpu.roll(flux, 1, 1))
            mv[kr] = cells + (lower - flux)
        return tuple(out)

    none = jnp.zeros((1, C), F32)
    lax.fori_loop(0, K, along_y, tuple((none, none) for _ in range(R)), unroll=True)

    chem[...] = jnp.zeros(chem.shape, F32)
    chem[0:T, 0:T] = chem_ref[...]
    square = (TP, TP)
    across = lax.broadcasted_iota(jnp.int32, square, 1)
    down = lax.broadcasted_iota(jnp.int32, square, 0)
    first_row = jnp.where(across == down, jnp.broadcast_to(chem[0:1, 0:TP], square), 0.0)
    first_rates = jnp.broadcast_to(jnp.sum(first_row, axis=1, keepdims=True), (TP, C))

    rates = chem[...]
    rates_high = rates.astype(jnp.bfloat16).astype(F32)
    depth = round_up(3 * TP, 2 * SUB)
    halves = (
        rates_high
        + pltpu.roll(rates_high, TP, 1)
        + pltpu.roll(rates - rates_high, 2 * TP, 1)
    )[:, 0:depth].astype(jnp.bfloat16)

    def products(k):
        mixed = jnp.concatenate([mv[k * R + r] for r in range(R)], axis=1)
        high = mixed.astype(jnp.bfloat16).astype(F32)
        stacked = [high, mixed - high, high]
        if depth > 3 * TP:
            stacked.append(jnp.zeros((depth - 3 * TP, R * C), F32))
        return jnp.dot(
            halves,
            jnp.concatenate(stacked, axis=0).astype(jnp.bfloat16),
            preferred_element_type=F32,
        )

    for g in range(groups):

        @pl.when(has_lo)
        def _():
            tile_copy(True, g).wait_recv()

        @pl.when(has_hi)
        def _():
            tile_copy(False, g).wait_recv()

        tracers = pl.ds(g * SUB, SUB)

        def along_x(k, carry):
            base = g * SUB * KR + k * R
            depth = lax.convert_element_type(k, F32)
            cells = []
            for r in range(R):
                value = lo[pl.ds(base + r, SUB, stride=KR), :]
                cells.append(jnp.where(depth < below[r : r + 1], value, 0.0))
            for r in range(R):
                cells.append(xs[k * R + r, tracers])
            for r in range(R):
                value = hi[pl.ds(base + r, SUB, stride=KR), :]
                cells.append(jnp.where(depth < above[r : r + 1], value, 0.0))
            diff = [b - a for a, b in zip(cells, cells[1:])]
            flux = []
            for face in range(R + 1):
                if face == 0:
                    c, weight = clow[0, pl.ds(k, 1)], clow[1, pl.ds(k, 1)]
                else:
                    at = pl.ds(k * R + face - 1, 1)
                    c, weight = coef[CX, at], coef[WX, at]
                flux.append(face_flux(c, weight, cells[face + 1], cells[face + 2], *diff[face : face + 3]))
            out = []
            for r in range(R):
                kr = k * R + r
                at = pl.ds(kr, 1)
                moved = mv[kr, tracers] + (flux[r] - flux[r + 1])
                rhs = moved * coef[INV, at] + coef[UINV, at] * carry[r]
                mv[kr, tracers] = rhs
                out.append(rhs)
            return tuple(out)

        zero = jnp.zeros((SUB, C), F32)
        lax.fori_loop(0, K, along_x, (zero,) * R, unroll=True)

        def upward(i, carry):
            k = K - 1 - i
            out = []
            for r in range(R):
                kr = k * R + r
                at = pl.ds(kr, 1)
                solved = mv[kr, tracers] - coef[RATIO, at] * carry[r]
                mv[kr, tracers] = solved
                part = jnp.sum(solved * first_rates[g * SUB : (g + 1) * SUB], axis=0, keepdims=True)
                if g > 0:
                    part = coef[ROW0, at] + part
                if g < groups - 1:
                    coef[ROW0, at] = part
                else:
                    wet = coef[WET, at]
                    value = wet * mv[kr, 0:1] + coef[WG, at] * part
                    coef[ABS, at] = wet * (0.02 + 0.04 * jnp.maximum(value, 0.0))
                out.append(solved)
            return tuple(out)

        lax.fori_loop(0, K, upward, (zero,) * R, unroll=True)

    def shade(k, carry):
        out = []
        for r in range(R):
            at = pl.ds(k * R + r, 1)
            coef[OPT, at] = carry[r]
            out.append(carry[r] + coef[ABS, at])
        return tuple(out)

    lax.fori_loop(0, K, shade, (none,) * R, unroll=True)
    heat = 16.0 * jnp.exp(-coef[OPT]) * (1.0 - jnp.exp(-coef[ABS]))
    if hsend.shape[1] > LR:
        hsend[...] = jnp.zeros(hsend.shape, F32)
    for d in range(n):
        hsend[d, 0:LR] = heat[d * LR : (d + 1) * LR]

    def heat_copy(off):
        to = (me + off) % n
        return pltpu.make_async_remote_copy(
            src_ref=hsend.at[to],
            dst_ref=hrecv.at[me],
            send_sem=h_ssem.at[off],
            recv_sem=h_rsem.at[off],
            device_id={"sect": to},
            device_id_type=MESH,
        )

    for off in range(1, n):
        heat_copy(off).start()
    hrecv[pl.ds(me, 1)] = hsend[pl.ds(me, 1)]

    def react(k, carry):
        reacted = products(k)
        for r in range(R):
            kr = k * R + r
            at = pl.ds(kr, 1)
            outp[pl.ds(kr, TP, stride=KR), :] = (
                coef[WET, at] * mv[kr] + coef[WG, at] * reacted[:, r * C : (r + 1) * C]
            )
        return carry

    lax.fori_loop(0, K, react, 0, unroll=True)

    for off in range(1, n):
        field_copy(off).wait_send()
    for g in range(groups):

        @pl.when(has_hi)
        def _():
            tile_copy(True, g).wait_send()

        @pl.when(has_lo)
        def _():
            tile_copy(False, g).wait_send()

    @pl.when(has_right)
    def _():
        edge_copy(True).wait_send()
        north_copy().wait_send()

    @pl.when(has_left)
    def _():
        edge_copy(False).wait_send()

    for off in range(1, n):
        heat_copy(off).wait_recv()
    for s in range(n):
        for l in range(L):
            heat_ref[l, s * R : (s + 1) * R] = hrecv[s, l * R : (l + 1) * R]
    for off in range(1, n):
        heat_copy(off).wait_send()


def store(adv, heat, adv_hbm, heat_hbm, sem):
    copies = (
        pltpu.make_async_copy(adv.at[pl.ds(0, adv_hbm.shape[0])], adv_hbm, sem.at[0]),
        pltpu.make_async_copy(heat, heat_hbm, sem.at[1]),
    )
    for copy in copies:
        copy.start()
    for copy in copies:
        copy.wait()


def body(sizes, solutes, tally, east, north, kappa, temp, salt, chemistry):
    T, K, R, C, n, ntx, nty = sizes
    KR, LR = K * R, K // n * R
    TP = round_up(T, SUB)
    groups = TP // SUB
    block = round_up(4 * LR + K // n + R, SUB)
    dma = pltpu.SemaphoreType.DMA
    vmem = pl.BlockSpec(memory_space=pltpu.VMEM)
    hbm = pl.BlockSpec(memory_space=pltpu.HBM)
    tile = pltpu.VMEM((TP * KR, C), F32)
    stack = pltpu.VMEM((KR, TP, C), F32)
    advanced, heating = pl.pallas_call(
        functools.partial(kernel, sizes),
        out_shape=(
            pltpu.VMEM((TP * KR, C), F32),
            pltpu.VMEM(east.shape, F32),
        ),
        in_specs=[hbm] * 8,
        out_specs=(vmem, vmem),
        scratch_shapes=[
            pltpu.VMEM(tally.shape, tally.dtype),
            *[pltpu.VMEM(east.shape, F32)] * 5,
            pltpu.VMEM(chemistry.shape, F32),
            tile,
            tile,
            tile,
            stack,
            stack,
            pltpu.VMEM((n, block, C), F32),
            pltpu.VMEM((n, block, C), F32),
            pltpu.VMEM((TP + SUB, C), F32),
            pltpu.VMEM((TP + SUB, C), F32),
            pltpu.VMEM((TP + SUB, C), F32),
            pltpu.VMEM((SUB, C), F32),
            pltpu.VMEM((SUB, C), F32),
            pltpu.VMEM((4, KR, C), F32),
            pltpu.VMEM((round_up(K, SUB), C), F32),
            pltpu.VMEM((13, KR, C), F32),
            pltpu.VMEM((2, round_up(K, SUB), C), F32),
            pltpu.VMEM((TP, C), F32),
            pltpu.VMEM((n, round_up(LR, SUB), C), F32),
            pltpu.VMEM((n, round_up(LR, SUB), C), F32),
            pltpu.VMEM((TP, C), F32),
            dma((n,)),
            dma((n,)),
            dma((2, groups)),
            dma((2, groups)),
            dma((2,)),
            dma((2,)),
            dma,
            dma,
            dma((n,)),
            dma((n,)),
            dma,
            dma((7,)),
        ],
        compiler_params=pltpu.CompilerParams(
            collective_id=0, has_side_effects=True, vmem_limit_bytes=VMEM_LIMIT
        ),
        name="ocean_step",
    )(solutes.reshape(T * KR, C), tally, east, north, kappa, temp, salt, chemistry)
    advanced, heating = pl.pallas_call(
        store,
        out_shape=(
            jax.ShapeDtypeStruct((T * KR, C), F32),
            jax.ShapeDtypeStruct(east.shape, F32),
        ),
        in_specs=[vmem, vmem],
        out_specs=(hbm, hbm),
        scratch_shapes=[dma((2,))],
        compiler_params=pltpu.CompilerParams(vmem_limit_bytes=1024 * 1024),
        name="store_outputs",
    )(advanced, heating)
    return advanced.reshape(T, K, R, C), heating


def solution(mesh):
    n, ntx, nty = (mesh.shape[axis] for axis in ("sect", "tx", "ty"))
    columns = P("sect", None, ("tx", "ty"))
    in_specs = (
        P(None, None, "sect", ("tx", "ty")),
        P("sect", ("tx", "ty")),
        columns,
        columns,
        columns,
        columns,
        columns,
        P(),
    )
    out_specs = (P(None, None, "sect", ("tx", "ty")), columns)

    def step(solutes, *rest):
        T, K, X, Y = solutes.shape
        R, C = X // n, Y // (ntx * nty)
        assert R == HALO and K % n == 0 and 4 * K * R == C
        sizes = (T, K, R, C, n, ntx, nty)
        return jax.shard_map(
            functools.partial(body, sizes),
            mesh=mesh,
            in_specs=in_specs,
            out_specs=out_specs,
            check_vma=False,
        )(solutes, *rest)

    return step
```
